32 devices in a mesh: dp: 16 (over z, y, core), sub: 2 (over x).
Axes of the slice: x: 2, y: 2, z: 4, core: 2. Of those that a mesh axis runs over, the one named last changes fastest.
Arguments:
- block_input: bfloat16 [2, 4096, 2048], P(None, ('dp', 'sub')), may hold values from -6 to 6
- out_grad: bfloat16 [2, 4096, 2048], P(None, ('dp', 'sub')), may hold values from -6 to 6
- seq_lengths: int32 [2, 32, 3], P(None, ('dp', 'sub')), may hold values from 1 to 96, 128 in all within a row
- attn_gain: bfloat16 [2048], P(('dp', 'sub')), may hold values from 0.5 to 1.5
- w_query: bfloat16 [2048, 2048], P(('dp', 'sub')), may hold values from -0.125 to 0.125
- w_key: bfloat16 [256, 2048], P(('dp', 'sub')), may hold values from -0.125 to 0.125
- w_value: bfloat16 [256, 2048], P(('dp', 'sub')), may hold values from -0.125 to 0.125
- w_output: bfloat16 [2048, 2048], P(('dp', 'sub')), may hold values from -0.75 to 0.75
- mlp_gain: bfloat16 [2048], P(('dp', 'sub')), may hold values from 0.5 to 1.5
- w_gate: bfloat16 [5632, 2048], P(('dp', 'sub')), may hold values from -0.125 to 0.125
- w_up: bfloat16 [5632, 2048], P(('dp', 'sub')), may hold values from -0.125 to 0.125
- w_down: bfloat16 [5632, 2048], P(('dp', 'sub')), may hold values from -0.109375 to 0.109375
Outputs:
- block_output: bfloat16 [2, 4096, 2048], P(None, ('dp', 'sub'))
- input_grad: bfloat16 [2, 4096, 2048], P(None, ('dp', 'sub'))
- attn_gain_grad: float32 [2048], P(('dp', 'sub'))
- query_grad: float32 [2048, 2048], P(('dp', 'sub'))
- key_grad: float32 [256, 2048], P(('dp', 'sub'))
- value_grad: float32 [256, 2048], P(('dp', 'sub'))
- output_grad: float32 [2048, 2048], P(('dp', 'sub'))
- mlp_gain_grad: float32 [2048], P(('dp', 'sub'))
- gate_grad: float32 [5632, 2048], P(('dp', 'sub'))
- up_grad: float32 [5632, 2048], P(('dp', 'sub'))
- down_grad: float32 [5632, 2048], P(('dp', 'sub'))
The draws below stay inside these ranges and needn't reach their ends.
Inputs may be any that keep to these rules, and one draw needn't show every extreme that they name: `seq_lengths`: the 3 lengths of each row sum to 128; the largest of each row is exactly 96.
All inputs are finite; a program needn't handle non-finite values.
Results may differ from the reference program's by a relative error of at most 0.014.
Values may be sent and summed in bfloat16 or wider, within the bound.
No kernel may reach another device: no remote copies, remote signals or barrier semaphores. Data moves between devices by JAX's collectives and lax.ppermute only.
A program may use at most 768 MiB of HBM per device.

```python
import math
import jax
import jax.numpy as jnp
import numpy as np
from jax import lax

D = 2048
HEADS = 32
KV_HEADS = 4
HEAD_DIM = 64
FF = 5632
TOK_DEV = 128
MICRO = 2
PACK = 3
LONGEST = 96
NDEV = 32
TOKENS = 4096


def level_of(own_key, dims, shards, least, top_value):
    def one(axis_at, blocks):
        heights = jax.random.uniform(jax.random.fold_in(jax.random.fold_in(own_key, 6), axis_at), (blocks,), jnp.float32, least / len(shards), top_value / len(shards))
        return jnp.repeat(jnp.exp(heights), dims[axis_at] // blocks).reshape((-1,) + (1,) * (len(dims) - axis_at - 1))

    level = one(*shards[0])
    for cut in shards[1:]:
        level = level * one(*cut)
    return level


def profile(count, total, limit, skew):
    weights = [(1 << 20) // math.isqrt(rank ** skew) + 1 for rank in range(2, count + 1)]
    rest, counts = total - limit - (count - 1), [1] * (count - 1)
    while rest > 0:
        candidates = [i for i in range(count - 1) if counts[i] < limit]
        pool, budget = sum([weights[i] for i in candidates]), rest
        for i in candidates:
            extra = min(limit - counts[i], max(1, budget * weights[i] // pool), rest)
            counts[i] = counts[i] + extra
            rest = rest - extra
    return np.array([limit] + counts)


def ragged_sizes(own_key, amount, total, reach, lean):
    if amount == 2:
        one = jax.random.randint(own_key, (), max(1, total - reach), min(reach, total - 1) + 1)
        return jnp.stack([one, total - one])
    sizes = jnp.asarray(profile(amount, total, reach, lean), jnp.int32)
    pairs = (amount - 1) // 2
    donor, receiver = sizes[1:1 + 2 * pairs:2], sizes[2:2 + 2 * pairs:2]
    slack = jnp.minimum(donor - 1, reach - receiver)
    moved = jax.random.randint(jax.random.fold_in(own_key, 1), (pairs,), 0, 1 << 20) % (slack + 1)
    sizes = sizes.at[1:1 + 2 * pairs:2].set(donor - moved).at[2:2 + 2 * pairs:2].set(receiver + moved)
    return sizes[jax.random.permutation(jax.random.fold_in(own_key, 2), amount)]


def scatter_about(stream_key, dims, scale, bound, split=(), kind=jnp.bfloat16):
    gain = level_of(stream_key, dims, split, -0.22, 0.18) if split else 1.0
    result = jax.random.normal(stream_key, dims, jnp.float32) * scale * gain
    return jnp.minimum(jnp.maximum(result, -bound), bound).astype(kind)


def setup_inputs(seed: int = 0) -> dict:
    streams_of = jax.random.split(jax.random.key(seed), 13)
    return {
        "block_input": scatter_about(streams_of[0], (MICRO, TOKENS, D), 1.0, 6.0, ((1, 32),)),
        "out_grad": scatter_about(streams_of[1], (MICRO, TOKENS, D), 1.0, 6.0, ((1, 32),)),
        "seq_lengths": jax.vmap(lambda own: ragged_sizes(own, PACK, TOK_DEV, LONGEST, 2))(jax.random.split(streams_of[2], MICRO * NDEV)).reshape((MICRO, NDEV, PACK)).astype(jnp.int32),
        "attn_gain": jnp.clip(1.0 + 0.1 * jax.random.normal(streams_of[3], (D,), jnp.float32), 0.5, 1.5).astype(jnp.bfloat16),
        "w_query": scatter_about(streams_of[4], (HEADS * HEAD_DIM, D), D ** -0.5, 0.125, ((0, 32),)),
        "w_key": scatter_about(streams_of[5], (KV_HEADS * HEAD_DIM, D), D ** -0.5, 0.125, ((0, 32),)),
        "w_value": scatter_about(streams_of[6], (KV_HEADS * HEAD_DIM, D), D ** -0.5, 0.125, ((0, 32),)),
        "w_output": scatter_about(streams_of[7], (HEADS * HEAD_DIM, D), (HEADS * HEAD_DIM // 32) ** -0.5, 0.75, ((0, 32),)),
        "mlp_gain": jnp.clip(1.0 + 0.1 * jax.random.normal(streams_of[8], (D,), jnp.float32), 0.5, 1.5).astype(jnp.bfloat16),
        "w_gate": scatter_about(streams_of[9], (FF, D), D ** -0.5, 0.125, ((0, 32),)),
        "w_up": scatter_about(streams_of[10], (FF, D), D ** -0.5, 0.125, ((0, 32),)),
        "w_down": scatter_about(streams_of[11], (FF, D), (FF // 2) ** -0.5, 0.109375, ((0, 32),)),
    }


@jax.custom_vjp
def low(v):
    return lax.optimization_barrier(v.astype(jnp.bfloat16)).astype(jnp.float32)

@jax.custom_vjp
def low_back(v):
    return v

def low_keep(v):
    return (low(v), None)

def low_pass(kept, grad):
    return (grad,)

def back_keep(v):
    return (v, None)

def back_low(kept, grad):
    return (low(grad),)
low.defvjp(low_keep, low_pass)
low_back.defvjp(back_keep, back_low)
EPS = 1e-05
ROPE_BASE = 10000.0
NEG_LARGE = -1e+30
HIGH = lax.Precision.HIGHEST

def positions(lengths_row, row_count):
    seq_ends = jnp.cumsum(lengths_row).astype(jnp.int32)
    starts = seq_ends - lengths_row
    token_index = jnp.arange(row_count, dtype=jnp.int32)
    segment = lax.optimization_barrier(jnp.sum((token_index[:, None] >= seq_ends[None, :]).astype(jnp.int32), 1))
    chosen = segment[:, None] == jnp.arange(lengths_row.shape[0], dtype=jnp.int32)[None, :]
    offsets = token_index - lax.optimization_barrier(jnp.sum(jnp.where(chosen, starts[None, :], 0), 1))
    allowed = (segment[:, None] == segment[None, :]) & (token_index[None, :] <= token_index[:, None])
    return (offsets, allowed)

def rotary_tables(offsets, width):
    half_width = width // 2
    frequency = ROPE_BASE ** (-jnp.arange(half_width, dtype=jnp.float32) * 2.0 / width)
    angles = offsets.astype(jnp.float32)[:, None] * frequency[None, :]
    return (jnp.cos(angles)[:, None, :], jnp.sin(angles)[:, None, :])

def rotate(values, cosine, sine_table):
    half_width = values.shape[-1] // 2
    first_half = values[..., :half_width]
    second_half = values[..., half_width:]
    return jnp.concatenate([first_half * cosine - second_half * sine_table, second_half * cosine + first_half * sine_table], -1)

def matmul(left_rows, right_rows):
    return jnp.dot(left_rows, right_rows, precision=HIGH)

def rms_normed(values):
    return values * lax.rsqrt(lax.optimization_barrier(jnp.mean(values * values, -1, keepdims=True)) + EPS)

def layer_row(x_row, lengths_row, params):
    attn_gain, w_query, w_key, w_value, w_output, mlp_gain, w_gate, w_up, w_down = params
    row_count = x_row.shape[0]
    group_size = HEADS // KV_HEADS
    offsets, allowed = positions(lengths_row, row_count)
    cosine, sine_table = rotary_tables(offsets, HEAD_DIM)
    hidden_one = low(rms_normed(x_row) * attn_gain)
    query_lin = low_back(matmul(hidden_one, w_query.T)).reshape(row_count, HEADS, HEAD_DIM)
    key_lin = low_back(matmul(hidden_one, w_key.T)).reshape(row_count, KV_HEADS, HEAD_DIM)
    value_rows = low(low_back(matmul(hidden_one, w_value.T))).reshape(row_count, KV_HEADS, HEAD_DIM)
    query_rot = low(rotate(query_lin, cosine, sine_table)).reshape(row_count, KV_HEADS, group_size, HEAD_DIM)
    key_rot = low(rotate(key_lin, cosine, sine_table))
    scores = low_back(jnp.einsum('qhgd,khd->hgqk', query_rot, key_rot, precision=HIGH) * HEAD_DIM ** (-0.5))
    scores = jnp.where(allowed, scores, NEG_LARGE)
    top_score = lax.optimization_barrier(jnp.max(scores, -1, keepdims=True))
    exp_scores = jnp.exp(scores - top_score)
    attn_probs = exp_scores / lax.optimization_barrier(jnp.sum(exp_scores, -1, keepdims=True))
    mixed = jnp.einsum('hgqk,khd->qhgd', low(attn_probs), value_rows, precision=HIGH)
    mixed = low(low_back(mixed)).reshape(row_count, HEADS * HEAD_DIM)
    resid_mid = x_row + low_back(matmul(mixed, w_output))
    hidden_two = low(rms_normed(resid_mid) * mlp_gain)
    gate_rows = low_back(matmul(hidden_two, w_gate.T))
    up_rows = low_back(matmul(hidden_two, w_up.T))
    inner = low(jax.nn.silu(gate_rows) * up_rows)
    return resid_mid + low_back(matmul(inner, w_down))

def reference(block_input, out_grad, seq_lengths, attn_gain, w_query, w_key, w_value, w_output, mlp_gain, w_gate, w_up, w_down):
    params = tuple((weight.astype(jnp.float32) for weight in (attn_gain, w_query, w_key, w_value, w_output, mlp_gain, w_gate, w_up, w_down)))
    row_total = MICRO * NDEV
    inputs = block_input.astype(jnp.float32).reshape(row_total, TOK_DEV, D)
    lengths_all = seq_lengths.reshape(row_total, PACK)
    row_step = jax.checkpoint(layer_row)

    def whole_layer(inputs, params):

        def scan_body(scan_carry, row_item):
            return (scan_carry, row_step(row_item[0], row_item[1], params))
        scan_carry, outputs = lax.scan(scan_body, None, (inputs, lengths_all))
        return outputs
    outputs, pullback = jax.vjp(whole_layer, inputs, params)
    grad_inputs, grad_params = pullback(out_grad.astype(jnp.float32).reshape(row_total, TOK_DEV, D))
    shape_out = (MICRO, TOKENS, D)
    return (outputs.astype(jnp.bfloat16).reshape(shape_out), grad_inputs.astype(jnp.bfloat16).reshape(shape_out), grad_params[0], grad_params[1], grad_params[2], grad_params[3], grad_params[4], grad_params[5], grad_params[6], grad_params[7], grad_params[8])
```

```python
import functools
import jax
import jax.numpy as jnp
from jax import lax
from jax.experimental import pallas as pl
from jax.experimental.pallas import tpu as pltpu
from jax.sharding import Mesh
from jax.sharding import PartitionSpec as P

ZH, ZL, MID, CORE, SUB = AXES = ("zh", "zl", "mid", "core", "sub")
DEVICES = ("dp", "sub")

HEAD_DIM = 64
EPS = 1e-05
ROPE_BASE = 10000.0
NEG_LARGE = -1e30
SUM_COLUMNS = 512
F32 = jnp.float32
BF16 = jnp.bfloat16
NT = (((1,), (1,)), ((), ()))
NN = (((1,), (0,)), ((), ()))
TN = (((0,), (0,)), ((), ()))


def dot(a, b, dims=NN):
    return lax.dot_general(a, b, dims, preferred_element_type=F32)


def call(kernel, name, grid, in_specs, out_specs, out_shape, scratch=()):
    return pl.pallas_call(
        kernel,
        grid=grid,
        in_specs=in_specs,
        out_specs=out_specs,
        out_shape=out_shape,
        scratch_shapes=scratch,
        name=name,
        cost_estimate=pl.CostEstimate(flops=1000, bytes_accessed=1000, transcendentals=0),
        compiler_params=pltpu.CompilerParams(
            dimension_semantics=("arbitrary",) * len(grid), vmem_limit_bytes=56 << 20
        ),
    )


def whole(shape):
    zeros = (0,) * len(shape)
    return pl.BlockSpec(shape, lambda *_: zeros, pipeline_mode=pl.Buffered(1))


def turn(values, cosine, sine):
    lane = lax.broadcasted_iota(jnp.int32, (values.shape[0], 128), 1)
    low = lane % HEAD_DIM < HEAD_DIM // 2
    blocks = []
    for at in range(0, values.shape[1], 128):
        block = values[:, at : at + 128]
        other = jnp.where(
            low,
            pltpu.roll(block, 128 - HEAD_DIM // 2, 1),
            pltpu.roll(block, HEAD_DIM // 2, 1),
        )
        blocks.append(block * cosine + other * sine)
    return jnp.concatenate(blocks, 1) if len(blocks) > 1 else blocks[0]


def two_heads(rows):
    low = lax.broadcasted_iota(jnp.int32, rows.shape, 1) < HEAD_DIM
    zero = jnp.zeros_like(rows)
    return jnp.concatenate([jnp.where(low, rows, zero), jnp.where(low, zero, rows)], 0)


def one_head(rows):
    half = rows.shape[0] // 2
    low = lax.broadcasted_iota(jnp.int32, (half, 128), 1) < HEAD_DIM
    return jnp.where(low, rows[:half], rows[half:])


def stack_lanes(values):
    return jnp.concatenate([values[:, at : at + 128] for at in range(0, values.shape[1], 128)], 0)


def unstack_lanes(values, rows):
    return jnp.concatenate([values[at : at + rows] for at in range(0, values.shape[0], rows)], 1)


def mask_of(segment):
    row = segment.shape[1]
    query = lax.broadcasted_iota(jnp.int32, (row, row), 0)
    key = lax.broadcasted_iota(jnp.int32, (row, row), 1)
    across = jnp.broadcast_to(segment, (row, row))
    return (across == across.T) & (key <= query)


def probabilities(stacked_q, keys2, allowed, row):
    scores = dot(stacked_q, keys2, NT)
    blocks = []
    for at in range(0, scores.shape[0], row):
        halves = []
        for side in range(2):
            part = scores[at : at + row, side * row : (side + 1) * row]
            part = jnp.where(allowed, part, NEG_LARGE)
            part = jnp.exp(part - jnp.max(part, -1, keepdims=True))
            halves.append(part * (1.0 / jnp.sum(part, -1, keepdims=True)))
        blocks.append(jnp.concatenate(halves, 1))
    return jnp.concatenate(blocks, 0)


def owner(mid, sub, zh):
    return 4 * mid + 2 * sub + zh


def assemble(parts, into, kind, rows, step=None, stride=None, offset=0):
    step = rows if step is None else step
    stride = rows if stride is None else stride
    for zh in range(2):
        for far in range(2):
            for inner in range(2):
                at = owner(far, inner, zh) if kind == "a" else owner(inner, far, zh)
                at = at * stride + offset
                into[at : at + rows] = parts[2 * zh + far][inner * step : inner * step + rows]


def assemble_down(parts, into, first):
    stride = into.shape[0] // 8
    assemble(parts[:4], into, "a", first, stride=stride)
    assemble(parts[4:], into, "b", stride - first, stride=stride, offset=first)


def tile_at(step):
    return (2 * step + 1) % 5


def pick(tile, refs, into):
    for at, ref in enumerate(refs):

        @pl.when(tile == at)
        def _(ref=ref):
            into[...] = ref[...]


def halves(part, send_ref, keep_ref, here=slice(None)):
    step = pl.program_id(0)

    @pl.when(step < 2)
    def _():
        send_ref[0, :, here] = part.astype(BF16)

    @pl.when(step >= 2)
    def _():
        keep_ref[0, :, here] = part.astype(BF16)


def halves_out(tile, width):
    specs = [
        pl.BlockSpec((1, tile, width), lambda s: (jnp.minimum(s, 1), 0, 0)),
        pl.BlockSpec((1, tile, width), lambda s: (jnp.maximum(s - 2, 0), 0, 0)),
    ]
    return specs, [jax.ShapeDtypeStruct((2, tile, width), BF16)] * 2


def quarters(part, send_refs, keep_ref, here=slice(None)):
    step = pl.program_id(0)
    rows = send_refs[0].shape[0]
    for at in range(2):

        @pl.when(step == at)
        def _(at=at):
            send_refs[2 * at][:, here] = part[:rows].astype(BF16)
            send_refs[2 * at + 1][:, here] = part[rows:].astype(BF16)

    @pl.when(step >= 2)
    def _():
        keep_ref[0, :, here] = part.astype(BF16)


def quarters_out(tile, width):
    specs, shapes = halves_out(tile, width)
    quarter = (tile // 2, width)
    return (
        [pl.BlockSpec(quarter, lambda s: (0, 0))] * 4 + specs[1:],
        [jax.ShapeDtypeStruct(quarter, BF16)] * 4 + shapes[1:],
    )


def pick_two(tile, refs, into):
    rows = refs[0].shape[0]
    for at in range(4):

        @pl.when(tile == at)
        def _(at=at):
            into[:rows] = refs[2 * at][...]
            into[rows:] = refs[2 * at + 1][...]


def attn_forward_kernel(row, head_rows, *refs):
    x_refs, (gain_ref, cos_ref, sin_ref, seg_ref, moved_ref, kv_own_ref, kv_core_ref) = (
        refs[:4],
        refs[4:11],
    )
    a_refs, o_refs = refs[11:15], refs[15:19]
    hid_ref, qkv_ref, mixed_ref, send_ref, keep_ref, wqkv_ref, wo_ref, x_ref = refs[19:]
    step = pl.program_id(0)
    width = 8 * head_rows
    pick(tile_at(step), x_refs, x_ref)

    @pl.when(step == 0)
    def _():
        assemble(a_refs, wqkv_ref, "a", head_rows, step=head_rows + HEAD_DIM // 4)
        assemble(o_refs, wo_ref, "b", head_rows)
        kv_rows = HEAD_DIM // 8
        for side in range(2):
            both = [
                [ref[4 * side + at].astype(F32) for ref in (kv_own_ref, kv_core_ref)]
                for at in range(4)
            ]
            for which in range(2):
                here = slice(which * kv_rows, (which + 1) * kv_rows)
                parts = [
                    both[mid * 2 + sub][core][here]
                    for mid in range(2)
                    for core in range(2)
                    for sub in range(2)
                ]
                placed = dot(moved_ref[...], jnp.concatenate(parts, 0).astype(BF16)).astype(BF16)
                low = width + (2 * which + side) * HEAD_DIM
                wqkv_ref[low : low + HEAD_DIM] = placed

    x = x_ref[...].astype(F32)
    inverse = lax.rsqrt(jnp.mean(x * x, -1, keepdims=True) + EPS)
    hidden = (x * inverse * gain_ref[...]).astype(BF16)
    hid_ref[...] = hidden
    lin = dot(hidden, wqkv_ref[...], NT)
    cosine, sine = cos_ref[...], sin_ref[...]
    qk = turn(lin[:, : width + 128], cosine, sine).astype(BF16)
    v_rows = lin[:, width + 128 :].astype(BF16)
    qkv_ref[:, : width + 128] = qk
    qkv_ref[:, width + 128 :] = v_rows
    scale = HEAD_DIM ** (-0.5)
    for at in range(0, x.shape[0], row):
        allowed = mask_of(seg_ref[0, at // row : at // row + 1])
        keys2 = two_heads(qk[at : at + row, width:] * jnp.asarray(scale, BF16))
        values2 = two_heads(v_rows[at : at + row])
        probs = probabilities(stack_lanes(qk[at : at + row, :width]), keys2, allowed, row)
        mixed = dot(probs.astype(BF16), values2).astype(BF16)
        mixed_ref[at : at + row] = unstack_lanes(mixed, row)
    halves(dot(mixed_ref[...], wo_ref[...]), send_ref, keep_ref)


def attn_forward(x, gain, cosine, sine, segment, moved, kv_own, kv_core, a_parts, o_parts,
                 head_rows, row):
    tile, width = x[0].shape
    rows = lambda n: pl.BlockSpec((tile, n), lambda s: (tile_at(s), 0))
    full = lambda n: pl.BlockSpec((n, width), lambda s: (0, 0))
    q_width = 8 * head_rows
    shape = lambda *dims: jax.ShapeDtypeStruct(dims, BF16)
    half_specs, half_shapes = halves_out(tile, width)
    return call(
        functools.partial(attn_forward_kernel, row, head_rows),
        "attn_forward",
        (4,),
        [whole(one.shape) for one in x]
        + [
            whole((1, width)),
            rows(128),
            rows(128),
            pl.BlockSpec((1,) + segment.shape[1:], lambda s: (tile_at(s), 0, 0)),
        ]
        + [whole(one.shape) for one in (moved, kv_own, kv_core, *a_parts, *o_parts)],
        [rows(width), rows(q_width + 256), rows(q_width)]
        + half_specs
        + [full(q_width + 256), full(q_width)],
        [shape(4 * tile, width), shape(4 * tile, q_width + 256), shape(4 * tile, q_width)]
        + half_shapes
        + [shape(q_width + 256, width), shape(q_width, width)],
        [pltpu.VMEM((tile, width), BF16)],
    )(*x, gain, cosine, sine, segment, moved, kv_own, kv_core, *a_parts, *o_parts)


def attn_backward_kernel(row, *refs):
    g_refs, x_refs = refs[:8], refs[8:12]
    qkv_ref, cos_ref, sin_ref, seg_ref, wqkv_ref, wo_ref = refs[12:18]
    gqkv_ref, gain_ref, *send_refs, keep_ref, g_ref, x_ref = refs[18:]
    step = pl.program_id(0)
    pick_two(tile_at(step), g_refs, g_ref)
    pick(tile_at(step), x_refs, x_ref)
    grad_mixed = dot(g_ref[...], wo_ref[...], NT).astype(BF16)
    width = grad_mixed.shape[1]
    qkv = qkv_ref[...]
    cosine, sine = cos_ref[...], -sin_ref[...]
    scale = HEAD_DIM ** (-0.5)
    for at in range(0, grad_mixed.shape[0], row):
        here = slice(at, at + row)
        allowed = mask_of(seg_ref[0, at // row : at // row + 1])
        keys2 = two_heads(qkv[here, width : width + 128] * jnp.asarray(scale, BF16))
        values2 = two_heads(qkv[here, width + 128 :])
        stacked_q = stack_lanes(qkv[here, :width])
        stacked_g = stack_lanes(grad_mixed[here])
        probs = probabilities(stacked_q, keys2, allowed, row)
        grad_probs = dot(stacked_g, values2, NT)
        moved = grad_probs * probs
        left = probs[:, :row] * (
            grad_probs[:, :row] - jnp.sum(moved[:, :row], -1, keepdims=True)
        )
        right = probs[:, row:] * (
            grad_probs[:, row:] - jnp.sum(moved[:, row:], -1, keepdims=True)
        )
        grad_scores = jnp.concatenate([left, right], 1).astype(BF16)
        grad_value = one_head(dot(probs.astype(BF16), stacked_g, TN))
        grad_key = one_head(dot(grad_scores, stacked_q, TN)) * scale
        grad_query = unstack_lanes(dot(grad_scores, keys2), row)
        gqkv_ref[here, :width] = turn(grad_query, cosine[here], sine[here]).astype(BF16)
        gqkv_ref[here, width : width + 128] = turn(grad_key, cosine[here], sine[here]).astype(BF16)
        gqkv_ref[here, width + 128 :] = grad_value.astype(BF16)
    part = dot(gqkv_ref[...], wqkv_ref[...])
    x = x_ref[...].astype(F32)
    normed = x * lax.rsqrt(jnp.mean(x * x, -1, keepdims=True) + EPS)
    terms = jnp.sum(part * normed, 0, keepdims=True)

    @pl.when(step == 0)
    def _():
        gain_ref[...] = terms

    @pl.when(step > 0)
    def _():
        gain_ref[...] += terms

    quarters(part, send_refs, keep_ref)


def attn_backward(grads, x, qkv, cosine, sine, segment, wqkv, wo, row):
    tile, width = x[0].shape
    rows = lambda n: pl.BlockSpec((tile, n), lambda s: (tile_at(s), 0))
    half_specs, half_shapes = quarters_out(tile, width)
    return call(
        functools.partial(attn_backward_kernel, row),
        "attn_backward",
        (4,),
        [whole(one.shape) for one in (*grads, *x)]
        + [
            rows(qkv.shape[1]),
            rows(128),
            rows(128),
            pl.BlockSpec((1,) + segment.shape[1:], lambda s: (tile_at(s), 0, 0)),
            whole(wqkv.shape),
            whole(wo.shape),
        ],
        [rows(qkv.shape[1]), pl.BlockSpec((1, width), lambda s: (0, 0))] + half_specs,
        [jax.ShapeDtypeStruct(qkv.shape, BF16), jax.ShapeDtypeStruct((1, width), F32)]
        + half_shapes,
        [pltpu.VMEM((tile, width), BF16)] * 2,
    )(*grads, *x, qkv, cosine, sine, segment, wqkv, wo)


def units_kernel(*refs):
    inner_ref, dgate_ref, dup_ref, gate_ref, up_ref, h_ref = refs[12:]
    step = pl.program_id(0)
    pick(step, refs[:4], h_ref)

    @pl.when(step == 0)
    def _():
        assemble(refs[4:8], gate_ref, "a", gate_ref.shape[0] // 8)
        assemble(refs[8:12], up_ref, "b", up_ref.shape[0] // 8)

    gate = dot(h_ref[...], gate_ref[...], NT)
    up = dot(h_ref[...], up_ref[...], NT)
    sigmoid = 1.0 / (1.0 + jnp.exp(-gate))
    silu = gate * sigmoid
    inner_ref[...] = (silu * up).astype(BF16)
    dup_ref[...] = silu.astype(BF16)
    dgate_ref[...] = (up * (sigmoid * (1.0 + gate * (1.0 - sigmoid)))).astype(BF16)


def units(hidden, gate_parts, up_parts):
    tile, width = hidden[0].shape
    count = 4 * gate_parts[0].shape[0]
    rows = pl.BlockSpec((tile, count), lambda s: (s, 0))
    return call(
        units_kernel,
        "units",
        (4,),
        [whole(one.shape) for one in (*hidden, *gate_parts, *up_parts)],
        [rows] * 3,
        [jax.ShapeDtypeStruct((4 * tile, count), BF16)] * 3,
        [pltpu.VMEM((count, width), BF16)] * 2 + [pltpu.VMEM((tile, width), BF16)],
    )(*hidden, *gate_parts, *up_parts)


def unit_grads_kernel(first, *refs):
    dgate_ref, dup_ref = refs[4:6]
    gg_ref, gu_ref, down_ref, g_ref = refs[14:]
    step = pl.program_id(0)
    pick(step, refs[:4], g_ref)

    @pl.when(step == 0)
    def _():
        assemble_down(refs[6:14], down_ref, first)

    inner = dot(g_ref[...], down_ref[...], NT)
    gg_ref[...] = (inner * dgate_ref[...].astype(F32)).astype(BF16)
    gu_ref[...] = (inner * dup_ref[...].astype(F32)).astype(BF16)


def unit_grads(grads, down_parts, dgate, dup, first):
    tile, width = grads[0].shape
    count = dgate.shape[1]
    rows = pl.BlockSpec((tile, count), lambda s: (s, 0))
    return call(
        functools.partial(unit_grads_kernel, first),
        "unit_grads",
        (4,),
        [whole(one.shape) for one in grads]
        + [rows, rows]
        + [whole(one.shape) for one in down_parts],
        [rows] * 2,
        [jax.ShapeDtypeStruct((4 * tile, count), BF16)] * 2,
        [pltpu.VMEM((count, width), BF16), pltpu.VMEM((tile, width), BF16)],
    )(*grads, dgate, dup, *down_parts)


def sum_kernel(count, first, *refs):
    lefts, parts = refs[:count], refs[count : count + 8]
    *send_refs, keep_ref = refs[count + 8 : len(refs) - count]
    weights = refs[len(refs) - count :]
    step = pl.program_id(0)
    rows = weights[0].shape[0] // 8

    @pl.when(step == 0)
    def _():
        if count == 1:
            assemble_down(parts, weights[0], first)
        else:
            assemble(parts[:4], weights[0], "a", rows)
            assemble(parts[4:], weights[1], "b", rows)

    def pieces():
        size = keep_ref.shape[2]
        for low in range(0, size, SUM_COLUMNS):
            here = slice(low, min(low + SUM_COLUMNS, size))
            total = dot(lefts[0][...], weights[0][:, here])
            for left, weight in zip(lefts[1:], weights[1:]):
                total = total + dot(left[...], weight[:, here])
            yield here, total

    for here, total in pieces():
        if len(send_refs) == 4:
            quarters(total, send_refs, keep_ref, here)
        else:
            halves(total, send_refs[0], keep_ref, here)


def sum_rows(lefts, parts, name, first=0):
    tokens, count = lefts[0].shape
    width = parts[0].shape[-1]
    tile = tokens // 4
    out = halves_out if len(lefts) == 1 else quarters_out
    half_specs, half_shapes = out(tile, width)
    return call(
        functools.partial(sum_kernel, len(lefts), first),
        name,
        (4,),
        [pl.BlockSpec((tile, count), lambda s: (tile_at(s), 0)) for one in lefts]
        + [whole(one.shape) for one in parts],
        half_specs,
        half_shapes,
        [pltpu.VMEM((count, width), BF16)] * len(lefts),
    )(*lefts, *parts)


def put_owners(place, a_keep, a_send, b_keep, b_send):
    step = pl.program_id(0)

    @pl.when(step < 2)
    def _():
        place(a_keep, (0, 1, 2, 3))
        place(a_send, (4, 5, 6, 7))

    @pl.when(step >= 2)
    def _():
        place(b_keep, (0, 1, 4, 5))
        place(b_send, (2, 3, 6, 7))


def owners_out(rows, width):
    half = lambda place: pl.BlockSpec((4, rows, width // 4), lambda s: (0, 0, place(s)))
    early, late = half(lambda s: jnp.minimum(s, 1)), half(lambda s: jnp.maximum(s - 2, 0))
    return [early, early, late, late], [jax.ShapeDtypeStruct((4, rows, width // 2), BF16)] * 4


def weight_grad_kernel(rows, l_ref, *refs):
    right = jnp.concatenate([ref[...] for ref in refs[:4]], 0)
    grads = dot(l_ref[...], right, TN).astype(BF16)

    def place(ref, owners):
        for at, one in enumerate(owners):
            ref[at] = grads[one * rows : (one + 1) * rows]

    put_owners(place, *refs[4:])


def weight_grad(left, right, name):
    tokens, count = left.shape
    tile, width = right[0].shape
    specs, shapes = owners_out(count // 8, width)
    return call(
        functools.partial(weight_grad_kernel, count // 8),
        name,
        (4,),
        [whole(left.shape)] + [pl.BlockSpec((tile, width // 4), lambda s: (0, s))] * 4,
        specs,
        shapes,
    )(left, *right)


def attn_grads_kernel(head_rows, kv_rows, gqkv_ref, hid_ref, mixed_ref, moved_ref, *refs):
    first = dot(gqkv_ref[...], hid_ref[...], TN).astype(BF16)
    right = jnp.concatenate([ref[...] for ref in refs[:8]], 0)
    second = dot(mixed_ref[...], right, TN).astype(BF16)
    width = 8 * head_rows
    placed = {}
    for which in range(2):
        for side in range(2):
            low = width + (2 * which + side) * HEAD_DIM
            placed[which, side] = dot(moved_ref[...], first[low : low + HEAD_DIM])

    def place(ref, owners):
        for at, one in enumerate(owners):
            mid, sub, side = one // 4, one // 2 % 2, one % 2
            lows = [(mid * 4 + core * 2 + sub) * kv_rows for core in range(2)]
            kv = [placed[which, side][low : low + kv_rows] for low in lows for which in range(2)]
            here = slice(one * head_rows, (one + 1) * head_rows)
            ref[at, :head_rows] = first[here]
            ref[at, head_rows : head_rows + 4 * kv_rows] = jnp.concatenate(kv, 0).astype(BF16)
            ref[at, head_rows + 4 * kv_rows :] = second[here]

    put_owners(place, *refs[8:])


def attn_grads(gqkv, hidden, mixed, right, moved, head_rows, kv_rows):
    tokens, width = hidden.shape
    columns = width // 4
    specs, shapes = owners_out(2 * head_rows + 4 * kv_rows, width)
    return call(
        functools.partial(attn_grads_kernel, head_rows, kv_rows),
        "attn_grads",
        (4,),
        [
            whole(gqkv.shape),
            pl.BlockSpec((tokens, columns), lambda s: (0, s)),
            whole(mixed.shape),
            whole(moved.shape),
        ]
        + [pl.BlockSpec((tokens // 8, columns), lambda s: (0, s))] * 8,
        specs,
        shapes,
    )(gqkv, hidden, mixed, moved, *right)


def norm_forward(values, gain):
    inverse = lax.rsqrt(jnp.mean(values * values, -1, keepdims=True) + EPS)
    normed = values * inverse
    return (normed, inverse, (normed * gain).astype(BF16))


def norm_backward(grad_hidden, normed, inverse, gain):
    grad_normed = grad_hidden * gain
    return inverse * (grad_normed - normed * jnp.mean(grad_normed * normed, -1, keepdims=True))


def swap(value, axis):
    return lax.ppermute(value, axis, [(0, 1), (1, 0)])


def up32(value):
    return value.astype(F32)


def join(*values):
    return jnp.concatenate(values, 0)


class Live:
    def cut(self):
        names = sorted(vars(self))
        values = lax.optimization_barrier(tuple(getattr(self, name) for name in names))
        for name, value in zip(names, values):
            setattr(self, name, value)

    @property
    def pop(self):
        return Pop(self)


class Pop:
    def __init__(self, live):
        self.live = live

    def __getattr__(self, name):
        value = getattr(self.live, name)
        delattr(self.live, name)
        return value


def tables(lengths_all, row_count):
    seq_ends = jnp.cumsum(lengths_all, 1)
    token = jnp.arange(row_count, dtype=jnp.int32)
    passed = (token[None, :, None] >= seq_ends[:, None, :]).astype(jnp.int32)
    segment = jnp.sum(passed, 2)
    offsets = token[None, :] - jnp.sum(passed * lengths_all[:, None, :], 2)
    half = HEAD_DIM // 2
    lane = jnp.arange(128, dtype=jnp.int32)
    frequency = ROPE_BASE ** (-(lane % half).astype(F32) * 2.0 / HEAD_DIM)
    angles = offsets.reshape(-1, 1).astype(F32) * frequency[None, :]
    sign = jnp.where(lane % HEAD_DIM < half, -1.0, 1.0)
    return (segment.astype(F32), jnp.cos(angles), jnp.sin(angles) * sign[None, :])


def on_device_small(
    block_input,
    out_grad,
    seq_lengths,
    attn_gain,
    w_query,
    w_key,
    w_value,
    w_output,
    mlp_gain,
    w_gate,
    w_up,
    w_down,
):
    width = block_input.shape[2]
    row_count = block_input.shape[1]
    micro = block_input.shape[0]
    tokens = micro * row_count
    head_rows = w_query.shape[0]
    kv_rows = w_key.shape[0]
    gain_width = attn_gain.shape[0]
    packed = seq_lengths.shape[2]
    units_own = w_gate.shape[0]
    first = -(-units_own // 2 // 32) * 32
    second = units_own - first
    qkv_rows = head_rows + 2 * kv_rows
    place = {name: lax.axis_index(name) for name in AXES}
    place8 = place[MID] * 4 + place[CORE] * 2 + place[SUB]
    place32 = place[ZH] * 16 + place[ZL] * 8 + place8
    index = jnp.arange(8 * kv_rows, dtype=jnp.int32)
    block, inside = index // kv_rows, index % kv_rows
    moved = (block[:, None] == (block[None, :] ^ place8)) & (inside[:, None] == inside[None, :])
    moved = moved.astype(BF16)
    index = jnp.arange(32, dtype=jnp.int32)
    ordered = (index[:, None] == (index[None, :] ^ place32)).astype(BF16)

    def pair_sum(keep, got, at):
        return up32(keep[at]) + up32(got[at])

    v = Live()
    own_x = block_input.reshape(tokens, width)
    v.own_g = out_grad.reshape(tokens, width)

    pack = join(attn_gain, mlp_gain, seq_lengths.reshape(micro * packed).astype(BF16))
    v.pack = jnp.pad(pack.reshape(1, -1), ((0, 0), (0, 256 - pack.shape[0])))
    v.pack_far = swap(v.pack, ZL)
    v.a0 = join(w_query, w_key, w_value)
    a_rows = v.a0.shape[0]
    v.w_gate, v.w_up, v.w_down, v.w_output = w_gate, w_up, w_down, w_output
    v.got_x = swap(join(v.a0, w_gate), SUB)
    v.got_y = swap(join(w_output, w_up), MID)
    v.ao = swap(join(v.a0, w_output), ZH)
    v.own_x = own_x
    v.x_far = swap(v.own_x, ZL)
    v.cut()

    v.g0x, v.u0y = v.got_x[a_rows:], v.got_y[head_rows:]
    v.a1, v.o1 = v.ao[:a_rows], v.ao[a_rows:]
    v.o0s = join(v.pop.w_output, v.got_y[:head_rows], v.a1)
    v.a0s = join(v.pop.a0, v.got_x[:a_rows], v.o1)
    v.o0t, v.a0t = swap(v.o0s, SUB), swap(v.a0s, MID)
    packs = jnp.concatenate([v.pop.pack, v.pop.pack_far], 1)
    packs = jnp.concatenate([packs, swap(packs, CORE)], 1)
    v.packs = jnp.pad(packs, ((0, 15), (0, width - packs.shape[1])))
    v.gate_low = swap(join(v.w_gate[:second], v.packs), ZH)
    v.x_core, v.x_far_core = swap(v.own_x, CORE), swap(v.x_far, CORE)
    del v.ao, v.got_x, v.got_y
    v.cut()

    packs = jnp.concatenate([v.packs[:, :1024], v.gate_low[second:, :1024]], 1)
    v.o1s = join(v.pop.o1, v.a0t[2 * a_rows :], packs)
    v.a1s = join(v.pop.a1, v.o0t[2 * head_rows :], packs)
    v.o1t, v.a1t = swap(v.o1s, SUB), swap(v.a1s, MID)
    v.gate_high = swap(v.w_gate[second:], ZH)
    v.packs_near = packs[:1]
    v.packs_across = lax.ppermute(packs[:1], (MID, SUB), [(at, 3 - at) for at in range(4)])
    lengths = v.pop.packs[0, :1024].reshape(2, 2, 256)
    lengths = lengths[:, :, 2 * gain_width : 2 * gain_width + micro * packed]
    lengths_all = lengths.transpose(1, 0, 2).reshape(4 * micro, packed).astype(jnp.int32)
    segment, v.cosine, v.sine = tables(lengths_all, row_count)
    v.segment = segment.reshape(4, micro, row_count)
    v.x = (v.own_x, v.pop.x_core, v.pop.x_far, v.pop.x_far_core)
    v.cut()

    v.u0s, v.g0s = join(v.w_up, v.pop.u0y), join(v.w_gate, v.pop.g0x)
    v.u0t, v.g0t = swap(v.u0s, SUB), swap(v.g0s, MID)
    v.u1 = swap(v.w_up, ZH)
    a_parts = (v.pop.a0s, v.pop.a0t, v.pop.a1s, v.pop.a1t)
    o_parts = (v.pop.o0s, v.pop.o0t, v.pop.o1s, v.pop.o1t)
    kv_own = join(
        *(one[: 2 * a_rows].reshape(2, a_rows, width)[:, head_rows:] for one in a_parts)
    )
    kv_core = swap(kv_own, CORE)
    packs = join(
        v.pop.packs_near, o_parts[3][-16:-15], a_parts[3][-16:-15], v.pop.packs_across
    )
    gains_rel = packs.reshape(2, 2, 2, 2, 2, 256)[..., : 2 * gain_width]
    gains_rel = gains_rel.transpose(2, 4, 0, 3, 1, 5)
    gains_all = dot(ordered, gains_rel.reshape(32, 2 * gain_width))
    v.gain_one = gains_all[:, :gain_width].reshape(1, width)
    v.gain_two = gains_all[:, gain_width:].reshape(1, width)
    attn = attn_forward(
        v.x,
        v.gain_one,
        v.cosine,
        v.sine,
        v.segment,
        moved,
        kv_own,
        kv_core,
        a_parts,
        o_parts,
        head_rows,
        row_count,
    )
    v.hidden_one, v.qkv, v.mixed, v.part_send, v.part_keep, v.wqkv, v.full_o = attn
    v.cut()

    v.g1 = join(v.gate_low[:second], v.pop.gate_high)
    del v.gate_low
    v.got_x = swap(join(v.g1, v.w_down[:first]), SUB)
    v.got_y = swap(join(v.u1, v.w_down[first:]), MID)
    v.da1 = swap(v.w_down[:first], ZH)
    v.part_got = swap(v.pop.part_send, CORE)
    mid_far = pair_sum(v.part_keep, v.part_got, 1).astype(BF16)
    v.mid_far = swap(mid_far, ZL)
    v.cut()

    v.dax, v.dby = v.got_x[units_own:], v.got_y[units_own:]
    v.g1s, v.u1s = join(v.pop.g1, v.got_x[:units_own]), join(v.pop.u1, v.got_y[:units_own])
    v.g1t, v.u1t = swap(v.g1s, MID), swap(v.u1s, SUB)
    v.resid_mid = up32(v.own_x) + (
        pair_sum(v.pop.part_keep, v.pop.part_got, 0) + up32(v.pop.mid_far)
    )
    v.db1 = swap(v.w_down[first:], ZH)
    h_own = norm_forward(v.resid_mid, v.gain_two)[2]
    v.h_far, v.h_core = swap(h_own, ZL), swap(h_own, CORE)
    v.h_own = h_own
    del v.got_x, v.got_y
    v.cut()

    v.db0s = join(v.w_down[first:], v.pop.dby, v.da1)
    v.da0s = join(v.w_down[:first], v.pop.dax, v.db1)
    v.db0t, v.da0t = swap(v.db0s, SUB), swap(v.da0s, MID)
    v.g_far, v.g_core = swap(v.own_g, ZL), swap(v.own_g, CORE)
    v.h = (v.pop.h_own, v.pop.h_core, v.h_far, swap(v.h_far, CORE))
    del v.w_gate, v.w_up, v.w_down, v.h_far
    v.gate_parts = (v.pop.g0s, v.pop.g0t, v.pop.g1s, v.pop.g1t)
    v.up_parts = (v.pop.u0s, v.pop.u0t, v.pop.u1s, v.pop.u1t)
    v.inner, v.dgate, v.dup = units(v.h, v.gate_parts, v.up_parts)
    v.cut()

    v.da1s = join(v.pop.da1, v.db0t[2 * second :])
    v.db1s = join(v.pop.db1, v.da0t[2 * first :])
    v.da1t, v.db1t = swap(v.da1s, MID), swap(v.db1s, SUB)
    v.g = (v.own_g, v.pop.g_core, v.g_far, swap(v.g_far, CORE))
    del v.g_far
    v.dg = weight_grad(v.inner, v.g, "down_grad")
    v.cut()

    def step_one(grads):
        keep_a, send_a, keep_b, send_b = grads
        return (keep_a, swap(send_a, MID), keep_b, swap(send_b, SUB))

    def sums_one(pairs):
        keep_a, got_a, keep_b, got_b = pairs
        far = slice(2, 4)
        return pairs + (
            pair_sum(keep_a, got_a, far).astype(BF16),
            pair_sum(keep_b, got_b, far).astype(BF16),
        )

    def step_two(pairs):
        return pairs[:4] + (swap(pairs[4], SUB), swap(pairs[5], MID))

    def half_sum(pairs, side, at):
        keep, got, two = pairs[2 * side], pairs[2 * side + 1], pairs[4 + side]
        return pair_sum(keep, got, at) + up32(two[at])

    def step_three(pairs, side):
        return pairs + (swap(half_sum(pairs, side, 1).astype(BF16), ZH),)

    def total(pairs):
        sides = [half_sum(pairs, side, 0) + up32(pairs[6 + side]) for side in range(2)]
        return jnp.concatenate(sides, 1)

    def gain_step(name):
        at = 1 + AXES.index(name)
        low, high = jnp.split(v.gain_grads, 2, at)
        mine = jnp.where(place[name] == 0, low, high)
        sent = jnp.where(place[name] == 0, high, low)
        v.gain_grads = mine + swap(sent, name)

    def near_of(keep, got, micro_at):
        here = slice(micro_at * row_count, (micro_at + 1) * row_count)
        return up32(keep[0, here]) + up32(got)

    def far_of(keep, got, micro_at):
        here = slice(micro_at * row_count, (micro_at + 1) * row_count)
        return (up32(keep[1, here]) + up32(got)).astype(BF16)

    def mid_grads(micro_at, far):
        here = slice(micro_at * row_count, (micro_at + 1) * row_count)
        gh2 = near_of(v.gh2_keep, v.gh2_near[micro_at], micro_at) + up32(far)
        resid = v.resid_mid[here]
        inverse = lax.rsqrt(jnp.mean(resid * resid, -1, keepdims=True) + EPS)
        normed = resid * inverse
        grad_mid = up32(v.own_g[here]) + norm_backward(gh2, normed, inverse, v.gain_two)
        return grad_mid, grad_mid.astype(BF16), jnp.sum(gh2 * normed, 0, keepdims=True)

    v.dg = step_one(v.dg)
    v.down_parts = (
        *(v.pop.da0s, v.pop.da0t, v.pop.da1s, v.pop.da1t),
        *(v.pop.db0s, v.pop.db0t, v.pop.db1s, v.pop.db1t),
    )
    v.gg, v.gu = unit_grads(v.pop.g, v.down_parts, v.pop.dgate, v.pop.dup, first)
    *send, v.gh2_keep = sum_rows(
        (v.gg, v.gu), (*v.pop.gate_parts, *v.pop.up_parts), "hidden_grads"
    )
    v.gh2_near = tuple(send[:2])
    v.gh2_far = (swap(send[2], CORE), swap(send[3], CORE))
    v.cut()
    v.dg = sums_one(v.dg)
    v.cut()

    v.dg = step_two(v.dg)
    v.gh2_zero = swap(far_of(v.gh2_keep, v.gh2_far[0], 0), ZL)
    v.gh2_near = tuple(swap(one, CORE) for one in v.gh2_near)
    v.gw = weight_grad(v.pop.gg, v.h, "gate_grad")
    v.cut()

    v.gw = step_one(v.gw)
    v.gh2_one = swap(far_of(v.gh2_keep, v.gh2_far[1], 1), ZL)
    v.grad_mid0, v.gb0, v.mlp_terms = mid_grads(0, v.pop.gh2_zero)
    v.gb0_far = swap(v.gb0, ZL)
    v.dg = step_three(v.dg, 0)
    v.uw = weight_grad(v.pop.gu, v.pop.h, "up_grad")
    v.out_send, v.out_keep = sum_rows((v.pop.inner,), v.pop.down_parts, "block_out", first)
    v.cut()

    v.grad_mid1, v.gb1, terms = mid_grads(1, v.pop.gh2_one)
    v.mlp_terms = v.mlp_terms + terms
    v.gb1_far = swap(v.gb1, ZL)
    del v.gh2_keep, v.gh2_near, v.gh2_far
    v.gw = step_two(sums_one(v.gw))
    v.dg = step_three(v.dg, 1)
    v.out_got = swap(v.pop.out_send, CORE)
    v.cut()

    v.uw = step_one(v.uw)
    v.gw = step_three(v.gw, 0)
    v.out_far = swap(pair_sum(v.out_keep, v.out_got, 1).astype(BF16), ZL)
    gb = (v.pop.gb0, v.pop.gb1), (v.pop.gb0_far, v.pop.gb1_far)
    v.gb = tuple(
        one for rows in gb for one in (*rows, *(swap(piece, CORE) for piece in rows))
    )
    v.gqkv, attn_terms, *send, v.gh1_keep = attn_backward(
        v.gb,
        v.pop.x,
        v.pop.qkv,
        v.pop.cosine,
        v.pop.sine,
        v.pop.segment,
        v.pop.wqkv,
        v.pop.full_o,
        row_count,
    )
    v.gh1_near = tuple(send[:2])
    v.gh1_far = (swap(send[2], CORE), swap(send[3], CORE))
    gain_grads = join(attn_terms, v.pop.mlp_terms)
    v.gain_grads = gain_grads.reshape(2, 2, 2, 2, 2, 2, gain_width)
    v.cut()
    v.uw = sums_one(v.uw)
    v.cut()

    v.uw = step_two(v.uw)
    v.gh1_zero = swap(far_of(v.gh1_keep, v.gh1_far[0], 0), ZL)
    v.gh1_near = tuple(swap(one, CORE) for one in v.gh1_near)
    v.gw = step_three(v.gw, 1)
    v.aw = attn_grads(
        v.pop.gqkv, v.pop.hidden_one, v.pop.mixed, v.pop.gb, moved, head_rows, kv_rows
    )
    gain_step(CORE)
    v.cut()

    v.aw = step_one(v.aw)
    v.gh1_one = swap(far_of(v.gh1_keep, v.gh1_far[1], 1), ZL)
    v.uw = step_three(v.uw, 0)
    gain_step(ZH)
    v.block_out = (
        v.pop.resid_mid + (pair_sum(v.pop.out_keep, v.pop.out_got, 0) + up32(v.pop.out_far))
    ).astype(BF16)
    v.down_grad = total(v.pop.dg)
    v.gate_grad = total(v.pop.gw)
    v.cut()
    v.aw = sums_one(v.aw)
    v.cut()

    v.aw = step_two(v.aw)
    v.uw = step_three(v.uw, 1)
    gain_step(ZL)
    gain_step(MID)
    gh1 = join(
        near_of(v.gh1_keep, v.gh1_near[0], 0) + up32(v.pop.gh1_zero),
        near_of(v.gh1_keep, v.gh1_near[1], 1) + up32(v.pop.gh1_one),
    )
    del v.gh1_keep, v.gh1_near, v.gh1_far
    x_f32 = up32(v.own_x)
    inverse_one = lax.rsqrt(jnp.mean(x_f32 * x_f32, -1, keepdims=True) + EPS)
    v.input_grad = (
        join(v.pop.grad_mid0, v.pop.grad_mid1)
        + norm_backward(gh1, x_f32 * inverse_one, inverse_one, v.gain_one)
    ).astype(BF16)
    v.cut()

    aw = step_three(step_three(v.aw, 0), 1)
    v.up_grad = total(v.pop.uw)
    gain_step(SUB)
    grads = total(aw)
    kv_grads = grads[head_rows:qkv_rows] + swap(grads[qkv_rows : qkv_rows + 2 * kv_rows], CORE)
    return (
        v.block_out.reshape(block_input.shape),
        v.input_grad.reshape(block_input.shape),
        v.gain_grads[0].reshape(gain_width),
        grads[:head_rows],
        kv_grads[:kv_rows],
        kv_grads[kv_rows:],
        grads[qkv_rows + 2 * kv_rows :],
        v.gain_grads[1].reshape(gain_width),
        v.gate_grad,
        v.up_grad,
        v.down_grad,
    )


def positions(lengths_row, row_count):
    seq_ends = jnp.cumsum(lengths_row)
    starts = seq_ends - lengths_row
    token_index = jnp.arange(row_count, dtype=jnp.int32)
    segment = jnp.sum((token_index[:, None] >= seq_ends[None, :]).astype(jnp.int32), 1)
    chosen = segment[:, None] == jnp.arange(lengths_row.shape[0], dtype=jnp.int32)[None, :]
    offsets = token_index - jnp.sum(jnp.where(chosen, starts[None, :], 0), 1)
    allowed = (segment[:, None] == segment[None, :]) & (
        token_index[None, :] <= token_index[:, None]
    )
    return (offsets, allowed)


def rotary_tables(offsets, width):
    half_width = width // 2
    frequency = ROPE_BASE ** (-jnp.arange(half_width, dtype=jnp.float32) * 2.0 / width)
    angles = offsets.astype(jnp.float32)[:, None] * frequency[None, :]
    return (jnp.cos(angles)[:, None, :], jnp.sin(angles)[:, None, :])


def rotate(values, cosine, sine_table):
    half_width = values.shape[-1] // 2
    first_half = values[..., :half_width]
    second_half = values[..., half_width:]
    return jnp.concatenate(
        [
            first_half * cosine - second_half * sine_table,
            second_half * cosine + first_half * sine_table,
        ],
        -1,
    )


def rotate_back(grads, cosine, sine_table):
    half_width = grads.shape[-1] // 2
    upper_half = grads[..., :half_width]
    lower_half = grads[..., half_width:]
    return jnp.concatenate(
        [
            upper_half * cosine + lower_half * sine_table,
            lower_half * cosine - upper_half * sine_table,
        ],
        -1,
    )


def project(activity, weight):
    return lax.dot_general(
        activity, weight, (((1,), (1,)), ((), ())), preferred_element_type=jnp.float32
    )


def apply_rows(activity, weight):
    return jnp.dot(activity, weight, preferred_element_type=jnp.float32)


def general_norm_forward(values, gain_row):
    inverse = lax.rsqrt(jnp.mean(values * values, -1, keepdims=True) + EPS)
    normed = values * inverse
    return (normed, inverse, (normed * gain_row.astype(jnp.float32)).astype(jnp.bfloat16))


def general_norm_backward(grad_hidden, normed, inverse, gain_row):
    grad_normed = grad_hidden * gain_row.astype(jnp.float32)
    return inverse * (grad_normed - normed * jnp.mean(grad_normed * normed, -1, keepdims=True))


def attention_scores(query_rot, key_rot, allowed):
    scores = jnp.einsum(
        "qhgd,khd->hgqk", query_rot, key_rot, preferred_element_type=jnp.float32
    ) * HEAD_DIM ** (-0.5)
    return jnp.where(allowed, scores, NEG_LARGE)


def forward_pass(block_rows, lengths_row, gathered):
    attn_gain, w_query, w_key, w_value, w_output, mlp_gain, w_gate, w_up, w_down = gathered
    row_count = block_rows.shape[0]
    query_heads = w_query.shape[0] // HEAD_DIM
    key_heads = w_key.shape[0] // HEAD_DIM
    group_size = query_heads // key_heads
    offsets, allowed = positions(lengths_row, row_count)
    cosine, sine_table = rotary_tables(offsets, HEAD_DIM)
    resid_in = block_rows.astype(jnp.float32)
    normed_one, inverse_one, hidden_one = general_norm_forward(resid_in, attn_gain)
    query_lin = project(hidden_one, w_query).reshape(row_count, query_heads, HEAD_DIM)
    key_lin = project(hidden_one, w_key).reshape(row_count, key_heads, HEAD_DIM)
    value_rows = (
        project(hidden_one, w_value).astype(jnp.bfloat16).reshape(row_count, key_heads, HEAD_DIM)
    )
    query_rot = (
        rotate(query_lin, cosine, sine_table)
        .astype(jnp.bfloat16)
        .reshape(row_count, key_heads, group_size, HEAD_DIM)
    )
    key_rot = rotate(key_lin, cosine, sine_table).astype(jnp.bfloat16)
    scores = attention_scores(query_rot, key_rot, allowed)
    top_score = jnp.max(scores, -1, keepdims=True)
    exp_scores = jnp.exp(scores - top_score)
    row_total = jnp.sum(exp_scores, -1, keepdims=True)
    prob_low = (exp_scores / row_total).astype(jnp.bfloat16)
    log_total = top_score + jnp.log(row_total)
    mixed = jnp.einsum("hgqk,khd->qhgd", prob_low, value_rows, preferred_element_type=jnp.float32)
    mixed = mixed.astype(jnp.bfloat16).reshape(row_count, query_heads * HEAD_DIM)
    resid_mid = resid_in + apply_rows(mixed, w_output)
    normed_two, inverse_two, hidden_two = general_norm_forward(resid_mid, mlp_gain)
    gate_rows = project(hidden_two, w_gate)
    up_rows = project(hidden_two, w_up)
    inner = (jax.nn.silu(gate_rows) * up_rows).astype(jnp.bfloat16)
    block_out = (resid_mid + apply_rows(inner, w_down)).astype(jnp.bfloat16)
    saved = (
        allowed,
        cosine,
        sine_table,
        normed_one,
        inverse_one,
        hidden_one,
        value_rows,
        query_rot,
        key_rot,
        log_total,
        mixed,
        normed_two,
        inverse_two,
        hidden_two,
        gate_rows,
        up_rows,
        inner,
    )
    return (block_out, saved)


def backward_pass(grad_rows, saved, gathered):
    attn_gain, w_query, w_key, w_value, w_output, mlp_gain, w_gate, w_up, w_down = gathered
    (
        allowed,
        cosine,
        sine_table,
        normed_one,
        inverse_one,
        hidden_one,
        value_rows,
        query_rot,
        key_rot,
        log_total,
        mixed,
        normed_two,
        inverse_two,
        hidden_two,
        gate_rows,
        up_rows,
        inner,
    ) = saved
    row_count = grad_rows.shape[0]
    grad_out = grad_rows.astype(jnp.float32)
    grad_inner = project(grad_rows, w_down)
    sigmoid_gate = jax.nn.sigmoid(gate_rows)
    silu_gate = gate_rows * sigmoid_gate
    grad_gate = (
        grad_inner * up_rows * sigmoid_gate * (1.0 + gate_rows * (1.0 - sigmoid_gate))
    ).astype(jnp.bfloat16)
    grad_up = (grad_inner * silu_gate).astype(jnp.bfloat16)
    grad_hidden_two = apply_rows(grad_gate, w_gate) + apply_rows(grad_up, w_up)
    grad_mid = grad_out + general_norm_backward(grad_hidden_two, normed_two, inverse_two, mlp_gain)
    grad_branch = grad_mid.astype(jnp.bfloat16)
    grad_mixed = project(grad_branch, w_output).astype(jnp.bfloat16).reshape(query_rot.shape)
    scores = attention_scores(query_rot, key_rot, allowed)
    attn_probs = jnp.exp(scores - log_total)
    prob_low = attn_probs.astype(jnp.bfloat16)
    grad_probs = jnp.einsum(
        "qhgd,khd->hgqk", grad_mixed, value_rows, preferred_element_type=jnp.float32
    )
    grad_scores = attn_probs * (grad_probs - jnp.sum(grad_probs * attn_probs, -1, keepdims=True))
    grad_scores = grad_scores.astype(jnp.bfloat16)
    grad_value = jnp.einsum(
        "hgqk,qhgd->khd", prob_low, grad_mixed, preferred_element_type=jnp.float32
    )
    grad_value = grad_value.astype(jnp.bfloat16).reshape(row_count, -1)
    score_scale = HEAD_DIM ** (-0.5)
    grad_qrot = (
        jnp.einsum("hgqk,khd->qhgd", grad_scores, key_rot, preferred_element_type=jnp.float32)
        * score_scale
    )
    grad_krot = (
        jnp.einsum("hgqk,qhgd->khd", grad_scores, query_rot, preferred_element_type=jnp.float32)
        * score_scale
    )
    grad_query = rotate_back(grad_qrot.reshape(row_count, -1, HEAD_DIM), cosine, sine_table)
    grad_query = grad_query.astype(jnp.bfloat16).reshape(row_count, -1)
    grad_key = (
        rotate_back(grad_krot, cosine, sine_table).astype(jnp.bfloat16).reshape(row_count, -1)
    )
    grad_hidden_one = (
        apply_rows(grad_query, w_query)
        + apply_rows(grad_key, w_key)
        + apply_rows(grad_value, w_value)
    )
    grad_input = (
        grad_mid + general_norm_backward(grad_hidden_one, normed_one, inverse_one, attn_gain)
    ).astype(jnp.bfloat16)
    gain_terms = jnp.stack(
        [jnp.sum(grad_hidden_one * normed_one, 0), jnp.sum(grad_hidden_two * normed_two, 0)]
    )
    stored = (
        grad_query,
        hidden_one,
        grad_key,
        grad_value,
        mixed,
        grad_branch,
        grad_gate,
        hidden_two,
        grad_up,
        inner,
        grad_rows,
    )
    return (grad_input, stored, gain_terms)


def slice_term(left_rows, right_rows, owner, width):
    piece = lax.dynamic_slice_in_dim(left_rows, owner * width, width, 1)
    return lax.dot_general(
        piece, right_rows, (((0,), (0,)), ((), ())), preferred_element_type=jnp.float32
    )


def on_device_general(
    block_input,
    out_grad,
    seq_lengths,
    attn_gain,
    w_query,
    w_key,
    w_value,
    w_output,
    mlp_gain,
    w_gate,
    w_up,
    w_down,
):
    block_outs = []
    grad_inputs = []
    collected = [[] for member in range(11)]
    gain_total = jnp.zeros((2, block_input.shape[2]), jnp.float32)
    for batch_index in range(block_input.shape[0]):
        forward_layer = (
            lax.all_gather(attn_gain, DEVICES, axis=0, tiled=True),
            lax.all_gather(w_query, DEVICES, axis=0, tiled=True),
            lax.all_gather(w_key, DEVICES, axis=0, tiled=True),
            lax.all_gather(w_value, DEVICES, axis=0, tiled=True),
            lax.all_gather(w_output, DEVICES, axis=0, tiled=True),
            lax.all_gather(mlp_gain, DEVICES, axis=0, tiled=True),
            lax.all_gather(w_gate, DEVICES, axis=0, tiled=True),
            lax.all_gather(w_up, DEVICES, axis=0, tiled=True),
            lax.all_gather(w_down, DEVICES, axis=0, tiled=True),
        )
        block_out, saved = forward_pass(
            block_input[batch_index], seq_lengths[batch_index, 0], forward_layer
        )
        backward_layer = (
            lax.all_gather(attn_gain, DEVICES, axis=0, tiled=True),
            lax.all_gather(w_query, DEVICES, axis=0, tiled=True),
            lax.all_gather(w_key, DEVICES, axis=0, tiled=True),
            lax.all_gather(w_value, DEVICES, axis=0, tiled=True),
            lax.all_gather(w_output, DEVICES, axis=0, tiled=True),
            lax.all_gather(mlp_gain, DEVICES, axis=0, tiled=True),
            lax.all_gather(w_gate, DEVICES, axis=0, tiled=True),
            lax.all_gather(w_up, DEVICES, axis=0, tiled=True),
            lax.all_gather(w_down, DEVICES, axis=0, tiled=True),
        )
        grad_input, stored, gain_terms = backward_pass(out_grad[batch_index], saved, backward_layer)
        block_outs.append(block_out)
        grad_inputs.append(grad_input)
        gain_total = gain_total + gain_terms
        for member in range(11):
            collected[member].append(stored[member])
    joined = [jnp.concatenate(member_list, 0) for member_list in collected]
    model_width = block_input.shape[2]
    query_width = w_query.shape[0]
    key_width = w_key.shape[0]
    hidden_width = w_gate.shape[0]
    gain_width = attn_gain.shape[0]
    own_rows = 2 * query_width + 2 * key_width + 3 * hidden_width + 1
    filler = jnp.zeros((model_width - 2 * gain_width,), jnp.float32)

    def owner_block(owner):
        gain_row = jnp.concatenate(
            [
                lax.dynamic_slice_in_dim(gain_total[0], owner * gain_width, gain_width, 0),
                lax.dynamic_slice_in_dim(gain_total[1], owner * gain_width, gain_width, 0),
                filler,
            ],
            0,
        )
        return jnp.concatenate(
            [
                slice_term(joined[0], joined[1], owner, query_width),
                slice_term(joined[2], joined[1], owner, key_width),
                slice_term(joined[3], joined[1], owner, key_width),
                slice_term(joined[4], joined[5], owner, query_width),
                slice_term(joined[6], joined[7], owner, hidden_width),
                slice_term(joined[8], joined[7], owner, hidden_width),
                slice_term(joined[9], joined[10], owner, hidden_width),
                gain_row[None, :],
            ],
            0,
        )

    owner_count = own_rows * lax.axis_size(DEVICES) // own_rows
    owners = jnp.arange(owner_count, dtype=jnp.int32)
    blocks = lax.map(owner_block, owners)
    owned = lax.psum_scatter(
        blocks.reshape(owner_count * own_rows, model_width),
        DEVICES,
        scatter_dimension=0,
        tiled=True,
    )
    cuts = [
        query_width,
        key_width,
        key_width,
        query_width,
        hidden_width,
        hidden_width,
        hidden_width,
    ]
    pieces = []
    offset = 0
    for width in cuts:
        pieces.append(owned[offset : offset + width])
        offset = offset + width
    gain_row = owned[offset]
    return (
        jnp.stack(block_outs),
        jnp.stack(grad_inputs),
        gain_row[:gain_width],
        pieces[0],
        pieces[1],
        pieces[2],
        pieces[3],
        gain_row[gain_width : 2 * gain_width],
        pieces[4],
        pieces[5],
        pieces[6],
    )


def solution(mesh):
    groups, sub = mesh.shape["dp"], mesh.shape["sub"]
    rows, weight, gain = P(None, DEVICES, None), P(DEVICES, None), P(DEVICES)
    body = on_device_general
    if groups == 16 and sub == 2:
        mesh = Mesh(mesh.devices.reshape(2, 2, groups // 8, 2, sub), AXES)
        rows, weight, gain = P(None, AXES, None), P(AXES, None), P(AXES)
        body = on_device_small
    return jax.shard_map(
        body,
        mesh=mesh,
        in_specs=(rows, rows, rows, gain) + (weight,) * 4 + (gain,) + (weight,) * 3,
        out_specs=(rows, rows, gain) + (weight,) * 4 + (gain,) + (weight,) * 3,
        check_vma=False,
    )
```

```python
import functools
import jax
import jax.numpy as jnp
from jax import lax
from jax.experimental import pallas as pl
from jax.experimental.pallas import tpu as pltpu
from jax.sharding import Mesh
from jax.sharding import PartitionSpec as P

ZH, ZL, MID, CORE, SUB = AXES = ("zh", "zl", "mid", "core", "sub")
DEVICES = ("dp", "sub")

HEAD_DIM = 64
EPS = 1e-05
ROPE_BASE = 10000.0
NEG_LARGE = -1e30
SUM_COLUMNS = 512
F32 = jnp.float32
BF16 = jnp.bfloat16
NT = (((1,), (1,)), ((), ()))
NN = (((1,), (0,)), ((), ()))
TN = (((0,), (0,)), ((), ()))


def dot(a, b, dims=NN):
    return lax.dot_general(a, b, dims, preferred_element_type=F32)


def call(kernel, name, grid, in_specs, out_specs, out_shape, scratch=()):
    return pl.pallas_call(
        kernel,
        grid=grid,
        in_specs=in_specs,
        out_specs=out_specs,
        out_shape=out_shape,
        scratch_shapes=scratch,
        name=name,
        cost_estimate=pl.CostEstimate(flops=1000, bytes_accessed=1000, transcendentals=0),
        compiler_params=pltpu.CompilerParams(
            dimension_semantics=("arbitrary",) * len(grid), vmem_limit_bytes=56 << 20
        ),
    )


def whole(shape):
    zeros = (0,) * len(shape)
    return pl.BlockSpec(shape, lambda *_: zeros, pipeline_mode=pl.Buffered(1))


def turn(values, cosine, sine):
    lane = lax.broadcasted_iota(jnp.int32, (values.shape[0], 128), 1)
    low = lane % HEAD_DIM < HEAD_DIM // 2
    blocks = []
    for at in range(0, values.shape[1], 128):
        block = values[:, at : at + 128]
        other = jnp.where(
            low,
            pltpu.roll(block, 128 - HEAD_DIM // 2, 1),
            pltpu.roll(block, HEAD_DIM // 2, 1),
        )
        blocks.append(block * cosine + other * sine)
    return jnp.concatenate(blocks, 1) if len(blocks) > 1 else blocks[0]


def two_heads(rows):
    low = lax.broadcasted_iota(jnp.int32, rows.shape, 1) < HEAD_DIM
    zero = jnp.zeros_like(rows)
    return jnp.concatenate([jnp.where(low, rows, zero), jnp.where(low, zero, rows)], 0)


def one_head(rows):
    half = rows.shape[0] // 2
    low = lax.broadcasted_iota(jnp.int32, (half, 128), 1) < HEAD_DIM
    return jnp.where(low, rows[:half], rows[half:])


def stack_lanes(values):
    return jnp.concatenate([values[:, at : at + 128] for at in range(0, values.shape[1], 128)], 0)


def unstack_lanes(values, rows):
    return jnp.concatenate([values[at : at + rows] for at in range(0, values.shape[0], rows)], 1)


def mask_of(segment):
    row = segment.shape[1]
    query = lax.broadcasted_iota(jnp.int32, (row, row), 0)
    key = lax.broadcasted_iota(jnp.int32, (row, row), 1)
    across = jnp.broadcast_to(segment, (row, row))
    return (across == across.T) & (key <= query)


def probabilities(stacked_q, keys2, allowed, row):
    scores = dot(stacked_q, keys2, NT)
    blocks = []
    for at in range(0, scores.shape[0], row):
        halves = []
        for side in range(2):
            part = scores[at : at + row, side * row : (side + 1) * row]
            part = jnp.where(allowed, part, NEG_LARGE)
            part = jnp.exp(part - jnp.max(part, -1, keepdims=True))
            halves.append(part * (1.0 / jnp.sum(part, -1, keepdims=True)))
        blocks.append(jnp.concatenate(halves, 1))
    return jnp.concatenate(blocks, 0)


def owner(mid, sub, zh):
    return 4 * mid + 2 * sub + zh


def assemble(parts, into, kind, rows, step=None, stride=None, offset=0):
    step = rows if step is None else step
    stride = rows if stride is None else stride
    for zh in range(2):
        for far in range(2):
            for inner in range(2):
                at = owner(far, inner, zh) if kind == "a" else owner(inner, far, zh)
                at = at * stride + offset
                into[at : at + rows] = parts[2 * zh + far][inner * step : inner * step + rows]


def assemble_down(parts, into, first):
    stride = into.shape[0] // 8
    assemble(parts[:4], into, "a", first, stride=stride)
    assemble(parts[4:], into, "b", stride - first, stride=stride, offset=first)


def tile_at(step):
    return (2 * step + 1) % 5


def pick(tile, refs, into):
    for at, ref in enumerate(refs):

        @pl.when(tile == at)
        def _(ref=ref):
            into[...] = ref[...]


def halves(part, send_ref, keep_ref, here=slice(None)):
    step = pl.program_id(0)

    @pl.when(step < 2)
    def _():
        send_ref[0, :, here] = part.astype(BF16)

    @pl.when(step >= 2)
    def _():
        keep_ref[0, :, here] = part.astype(BF16)


def halves_out(tile, width):
    specs = [
        pl.BlockSpec((1, tile, width), lambda s: (jnp.minimum(s, 1), 0, 0)),
        pl.BlockSpec((1, tile, width), lambda s: (jnp.maximum(s - 2, 0), 0, 0)),
    ]
    return specs, [jax.ShapeDtypeStruct((2, tile, width), BF16)] * 2


def quarters(part, send_refs, keep_ref, here=slice(None)):
    step = pl.program_id(0)
    near_ref, zero_ref, one_ref = send_refs
    rows = zero_ref.shape[0]

    @pl.when(step == 0)
    def _():
        near_ref[:, here] = part.astype(BF16)

    @pl.when(step == 1)
    def _():
        zero_ref[:, here] = part[:rows].astype(BF16)
        one_ref[:, here] = part[rows:].astype(BF16)

    @pl.when(step >= 2)
    def _():
        keep_ref[0, :, here] = part.astype(BF16)


def quarters_out(tile, width):
    specs, shapes = halves_out(tile, width)
    sizes = [(tile, width)] + [(tile // 2, width)] * 2
    return (
        [pl.BlockSpec(size, lambda s: (0, 0)) for size in sizes] + specs[1:],
        [jax.ShapeDtypeStruct(size, BF16) for size in sizes] + shapes[1:],
    )


def pick_two(tile, refs, into):
    rows = refs[0].shape[0]
    for at in range(4):

        @pl.when(tile == at)
        def _(at=at):
            into[:rows] = refs[2 * at][...]
            into[rows:] = refs[2 * at + 1][...]


def attn_forward_kernel(row, head_rows, *refs):
    x_refs, (gain_ref, cos_ref, sin_ref, seg_ref, moved_ref, kv_own_ref, kv_core_ref) = (
        refs[:4],
        refs[4:11],
    )
    a_refs, o_refs = refs[11:15], refs[15:19]
    hid_ref, qkv_ref, mixed_ref, send_ref, keep_ref, wqkv_ref, wo_ref, x_ref = refs[19:]
    step = pl.program_id(0)
    width = 8 * head_rows
    pick(tile_at(step), x_refs, x_ref)

    @pl.when(step == 0)
    def _():
        assemble(a_refs, wqkv_ref, "a", head_rows, step=head_rows + HEAD_DIM // 4)
        assemble(o_refs, wo_ref, "b", head_rows)
        kv_rows = HEAD_DIM // 8
        for side in range(2):
            both = [
                [ref[4 * side + at].astype(F32) for ref in (kv_own_ref, kv_core_ref)]
                for at in range(4)
            ]
            for which in range(2):
                here = slice(which * kv_rows, (which + 1) * kv_rows)
                parts = [
                    both[mid * 2 + sub][core][here]
                    for mid in range(2)
                    for core in range(2)
                    for sub in range(2)
                ]
                placed = dot(moved_ref[...], jnp.concatenate(parts, 0).astype(BF16)).astype(BF16)
                low = width + (2 * which + side) * HEAD_DIM
                wqkv_ref[low : low + HEAD_DIM] = placed

    x = x_ref[...].astype(F32)
    inverse = lax.rsqrt(jnp.mean(x * x, -1, keepdims=True) + EPS)
    hidden = (x * inverse * gain_ref[...]).astype(BF16)
    hid_ref[...] = hidden
    lin = dot(hidden, wqkv_ref[...], NT)
    cosine, sine = cos_ref[...], sin_ref[...]
    qk = turn(lin[:, : width + 128], cosine, sine).astype(BF16)
    v_rows = lin[:, width + 128 :].astype(BF16)
    qkv_ref[:, : width + 128] = qk
    qkv_ref[:, width + 128 :] = v_rows
    scale = HEAD_DIM ** (-0.5)
    for at in range(0, x.shape[0], row):
        allowed = mask_of(seg_ref[0, at // row : at // row + 1])
        keys2 = two_heads(qk[at : at + row, width:] * jnp.asarray(scale, BF16))
        values2 = two_heads(v_rows[at : at + row])
        probs = probabilities(stack_lanes(qk[at : at + row, :width]), keys2, allowed, row)
        mixed = dot(probs.astype(BF16), values2).astype(BF16)
        mixed_ref[at : at + row] = unstack_lanes(mixed, row)
    halves(dot(mixed_ref[...], wo_ref[...]), send_ref, keep_ref)


def attn_forward(x, gain, cosine, sine, segment, moved, kv_own, kv_core, a_parts, o_parts,
                 head_rows, row):
    tile, width = x[0].shape
    rows = lambda n: pl.BlockSpec((tile, n), lambda s: (tile_at(s), 0))
    full = lambda n: pl.BlockSpec((n, width), lambda s: (0, 0))
    q_width = 8 * head_rows
    shape = lambda *dims: jax.ShapeDtypeStruct(dims, BF16)
    half_specs, half_shapes = halves_out(tile, width)
    return call(
        functools.partial(attn_forward_kernel, row, head_rows),
        "attn_forward",
        (4,),
        [whole(one.shape) for one in x]
        + [
            whole((1, width)),
            rows(128),
            rows(128),
            pl.BlockSpec((1,) + segment.shape[1:], lambda s: (tile_at(s), 0, 0)),
        ]
        + [whole(one.shape) for one in (moved, kv_own, kv_core, *a_parts, *o_parts)],
        [rows(width), rows(q_width + 256), rows(q_width)]
        + half_specs
        + [full(q_width + 256), full(q_width)],
        [shape(4 * tile, width), shape(4 * tile, q_width + 256), shape(4 * tile, q_width)]
        + half_shapes
        + [shape(q_width + 256, width), shape(q_width, width)],
        [pltpu.VMEM((tile, width), BF16)],
    )(*x, gain, cosine, sine, segment, moved, kv_own, kv_core, *a_parts, *o_parts)


def attn_backward_kernel(row, *refs):
    g_refs, x_refs = refs[:8], refs[8:12]
    qkv_ref, cos_ref, sin_ref, seg_ref, wqkv_ref, wo_ref = refs[12:18]
    gqkv_ref, gain_ref, *send_refs, keep_ref, g_ref, x_ref = refs[18:]
    step = pl.program_id(0)
    pick_two(tile_at(step), g_refs, g_ref)
    pick(tile_at(step), x_refs, x_ref)
    grad_mixed = dot(g_ref[...], wo_ref[...], NT).astype(BF16)
    width = grad_mixed.shape[1]
    qkv = qkv_ref[...]
    cosine, sine = cos_ref[...], -sin_ref[...]
    scale = HEAD_DIM ** (-0.5)
    for at in range(0, grad_mixed.shape[0], row):
        here = slice(at, at + row)
        allowed = mask_of(seg_ref[0, at // row : at // row + 1])
        keys2 = two_heads(qkv[here, width : width + 128] * jnp.asarray(scale, BF16))
        values2 = two_heads(qkv[here, width + 128 :])
        stacked_q = stack_lanes(qkv[here, :width])
        stacked_g = stack_lanes(grad_mixed[here])
        probs = probabilities(stacked_q, keys2, allowed, row)
        grad_probs = dot(stacked_g, values2, NT)
        moved = grad_probs * probs
        left = probs[:, :row] * (
            grad_probs[:, :row] - jnp.sum(moved[:, :row], -1, keepdims=True)
        )
        right = probs[:, row:] * (
            grad_probs[:, row:] - jnp.sum(moved[:, row:], -1, keepdims=True)
        )
        grad_scores = jnp.concatenate([left, right], 1).astype(BF16)
        grad_value = one_head(dot(probs.astype(BF16), stacked_g, TN))
        grad_key = one_head(dot(grad_scores, stacked_q, TN)) * scale
        grad_query = unstack_lanes(dot(grad_scores, keys2), row)
        gqkv_ref[here, :width] = turn(grad_query, cosine[here], sine[here]).astype(BF16)
        gqkv_ref[here, width : width + 128] = turn(grad_key, cosine[here], sine[here]).astype(BF16)
        gqkv_ref[here, width + 128 :] = grad_value.astype(BF16)
    part = dot(gqkv_ref[...], wqkv_ref[...])
    x = x_ref[...].astype(F32)
    normed = x * lax.rsqrt(jnp.mean(x * x, -1, keepdims=True) + EPS)
    terms = jnp.sum(part * normed, 0, keepdims=True)

    @pl.when(step == 0)
    def _():
        gain_ref[...] = terms

    @pl.when(step > 0)
    def _():
        gain_ref[...] += terms

    quarters(part, send_refs, keep_ref)


def attn_backward(grads, x, qkv, cosine, sine, segment, wqkv, wo, row):
    tile, width = x[0].shape
    rows = lambda n: pl.BlockSpec((tile, n), lambda s: (tile_at(s), 0))
    half_specs, half_shapes = quarters_out(tile, width)
    return call(
        functools.partial(attn_backward_kernel, row),
        "attn_backward",
        (4,),
        [whole(one.shape) for one in (*grads, *x)]
        + [
            rows(qkv.shape[1]),
            rows(128),
            rows(128),
            pl.BlockSpec((1,) + segment.shape[1:], lambda s: (tile_at(s), 0, 0)),
            whole(wqkv.shape),
            whole(wo.shape),
        ],
        [rows(qkv.shape[1]), pl.BlockSpec((1, width), lambda s: (0, 0))] + half_specs,
        [jax.ShapeDtypeStruct(qkv.shape, BF16), jax.ShapeDtypeStruct((1, width), F32)]
        + half_shapes,
        [pltpu.VMEM((tile, width), BF16)] * 2,
    )(*grads, *x, qkv, cosine, sine, segment, wqkv, wo)


def units_kernel(*refs):
    inner_ref, dgate_ref, dup_ref, gate_ref, up_ref, h_ref = refs[12:]
    step = pl.program_id(0)
    pick(step, refs[:4], h_ref)

    @pl.when(step == 0)
    def _():
        assemble(refs[4:8], gate_ref, "a", gate_ref.shape[0] // 8)
        assemble(refs[8:12], up_ref, "b", up_ref.shape[0] // 8)

    gate = dot(h_ref[...], gate_ref[...], NT)
    up = dot(h_ref[...], up_ref[...], NT)
    sigmoid = 1.0 / (1.0 + jnp.exp(-gate))
    silu = gate * sigmoid
    inner_ref[...] = (silu * up).astype(BF16)
    dup_ref[...] = silu.astype(BF16)
    dgate_ref[...] = (up * (sigmoid * (1.0 + gate * (1.0 - sigmoid)))).astype(BF16)


def units(hidden, gate_parts, up_parts):
    tile, width = hidden[0].shape
    count = 4 * gate_parts[0].shape[0]
    rows = pl.BlockSpec((tile, count), lambda s: (s, 0))
    return call(
        units_kernel,
        "units",
        (4,),
        [whole(one.shape) for one in (*hidden, *gate_parts, *up_parts)],
        [rows] * 3,
        [jax.ShapeDtypeStruct((4 * tile, count), BF16)] * 3,
        [pltpu.VMEM((count, width), BF16)] * 2 + [pltpu.VMEM((tile, width), BF16)],
    )(*hidden, *gate_parts, *up_parts)


def unit_grads_kernel(first, *refs):
    dgate_ref, dup_ref = refs[4:6]
    gg_ref, gu_ref, down_ref, g_ref = refs[14:]
    step = pl.program_id(0)
    pick(step, refs[:4], g_ref)

    @pl.when(step == 0)
    def _():
        assemble_down(refs[6:14], down_ref, first)

    inner = dot(g_ref[...], down_ref[...], NT)
    gg_ref[...] = (inner * dgate_ref[...].astype(F32)).astype(BF16)
    gu_ref[...] = (inner * dup_ref[...].astype(F32)).astype(BF16)


def unit_grads(grads, down_parts, dgate, dup, first):
    tile, width = grads[0].shape
    count = dgate.shape[1]
    rows = pl.BlockSpec((tile, count), lambda s: (s, 0))
    return call(
        functools.partial(unit_grads_kernel, first),
        "unit_grads",
        (4,),
        [whole(one.shape) for one in grads]
        + [rows, rows]
        + [whole(one.shape) for one in down_parts],
        [rows] * 2,
        [jax.ShapeDtypeStruct((4 * tile, count), BF16)] * 2,
        [pltpu.VMEM((count, width), BF16), pltpu.VMEM((tile, width), BF16)],
    )(*grads, dgate, dup, *down_parts)


def sum_kernel(count, first, *refs):
    lefts, parts = refs[:count], refs[count : count + 8]
    *send_refs, keep_ref = refs[count + 8 : len(refs) - count]
    weights = refs[len(refs) - count :]
    step = pl.program_id(0)
    rows = weights[0].shape[0] // 8

    @pl.when(step == 0)
    def _():
        if count == 1:
            assemble_down(parts, weights[0], first)
        else:
            assemble(parts[:4], weights[0], "a", rows)
            assemble(parts[4:], weights[1], "b", rows)

    def pieces():
        size = keep_ref.shape[2]
        for low in range(0, size, SUM_COLUMNS):
            here = slice(low, min(low + SUM_COLUMNS, size))
            total = dot(lefts[0][...], weights[0][:, here])
            for left, weight in zip(lefts[1:], weights[1:]):
                total = total + dot(left[...], weight[:, here])
            yield here, total

    for here, total in pieces():
        if len(send_refs) == 3:
            quarters(total, send_refs, keep_ref, here)
        else:
            halves(total, send_refs[0], keep_ref, here)


def sum_rows(lefts, parts, name, first=0):
    tokens, count = lefts[0].shape
    width = parts[0].shape[-1]
    tile = tokens // 4
    out = halves_out if len(lefts) == 1 else quarters_out
    half_specs, half_shapes = out(tile, width)
    return call(
        functools.partial(sum_kernel, len(lefts), first),
        name,
        (4,),
        [pl.BlockSpec((tile, count), lambda s: (tile_at(s), 0)) for one in lefts]
        + [whole(one.shape) for one in parts],
        half_specs,
        half_shapes,
        [pltpu.VMEM((count, width), BF16)] * len(lefts),
    )(*lefts, *parts)


def put_owners(place, a_keep, a_send, b_keep, b_send):
    step = pl.program_id(0)

    @pl.when(step < 2)
    def _():
        place(a_keep, (0, 1, 2, 3))
        place(a_send, (4, 5, 6, 7))

    @pl.when(step >= 2)
    def _():
        place(b_keep, (0, 1, 4, 5))
        place(b_send, (2, 3, 6, 7))


def owners_out(rows, width):
    half = lambda place: pl.BlockSpec((4, rows, width // 4), lambda s: (0, 0, place(s)))
    early, late = half(lambda s: jnp.minimum(s, 1)), half(lambda s: jnp.maximum(s - 2, 0))
    return [early, early, late, late], [jax.ShapeDtypeStruct((4, rows, width // 2), BF16)] * 4


def weight_grad_kernel(rows, l_ref, *refs):
    right = jnp.concatenate([ref[...] for ref in refs[:4]], 0)
    grads = dot(l_ref[...], right, TN).astype(BF16)

    def place(ref, owners):
        for at, one in enumerate(owners):
            ref[at] = grads[one * rows : (one + 1) * rows]

    put_owners(place, *refs[4:])


def weight_grad(left, right, name):
    tokens, count = left.shape
    tile, width = right[0].shape
    specs, shapes = owners_out(count // 8, width)
    return call(
        functools.partial(weight_grad_kernel, count // 8),
        name,
        (4,),
        [whole(left.shape)] + [pl.BlockSpec((tile, width // 4), lambda s: (0, s))] * 4,
        specs,
        shapes,
    )(left, *right)


def attn_grads_kernel(head_rows, kv_rows, gqkv_ref, hid_ref, mixed_ref, moved_ref, *refs):
    first = dot(gqkv_ref[...], hid_ref[...], TN).astype(BF16)
    right = jnp.concatenate([ref[...] for ref in refs[:8]], 0)
    second = dot(mixed_ref[...], right, TN).astype(BF16)
    width = 8 * head_rows
    placed = {}
    for which in range(2):
        for side in range(2):
            low = width + (2 * which + side) * HEAD_DIM
            placed[which, side] = dot(moved_ref[...], first[low : low + HEAD_DIM])

    def place(ref, owners):
        for at, one in enumerate(owners):
            mid, sub, side = one // 4, one // 2 % 2, one % 2
            lows = [(mid * 4 + core * 2 + sub) * kv_rows for core in range(2)]
            kv = [placed[which, side][low : low + kv_rows] for low in lows for which in range(2)]
            here = slice(one * head_rows, (one + 1) * head_rows)
            ref[at, :head_rows] = first[here]
            ref[at, head_rows : head_rows + 4 * kv_rows] = jnp.concatenate(kv, 0).astype(BF16)
            ref[at, head_rows + 4 * kv_rows :] = second[here]

    put_owners(place, *refs[8:])


def attn_grads(gqkv, hidden, mixed, right, moved, head_rows, kv_rows):
    tokens, width = hidden.shape
    columns = width // 4
    specs, shapes = owners_out(2 * head_rows + 4 * kv_rows, width)
    return call(
        functools.partial(attn_grads_kernel, head_rows, kv_rows),
        "attn_grads",
        (4,),
        [
            whole(gqkv.shape),
            pl.BlockSpec((tokens, columns), lambda s: (0, s)),
            whole(mixed.shape),
            whole(moved.shape),
        ]
        + [pl.BlockSpec((tokens // 8, columns), lambda s: (0, s))] * 8,
        specs,
        shapes,
    )(gqkv, hidden, mixed, moved, *right)


def total_kernel(ka_ref, ga_ref, kb_ref, gb_ref, ta_ref, tb_ref, *refs):
    *last_refs, out_ref = refs
    half = ka_ref.shape[2]
    last = jnp.concatenate([ref[...].astype(F32) for ref in last_refs], 1)
    a, b = (
        keep[0].astype(F32) + got[0].astype(F32) + two[0].astype(F32)
        for keep, got, two in ((ka_ref, ga_ref, ta_ref), (kb_ref, gb_ref, tb_ref))
    )
    out_ref[:, :half] = a + last[:, :half]
    out_ref[:, half:] = b + last[:, half:]


def total_sum(pairs):
    _, rows, half = pairs[0].shape
    block = pl.BlockSpec((1, rows, half), lambda s: (0, 0, 0))
    return call(
        total_kernel,
        "total",
        (1,),
        [block] * 6 + [whole(one.shape) for one in pairs[6:]],
        pl.BlockSpec((rows, 2 * half), lambda s: (0, 0)),
        jax.ShapeDtypeStruct((rows, 2 * half), F32),
    )(*pairs)


def finish_kernel(x_ref, gain_ref, mid0_ref, mid1_ref, keep_ref, near_ref, zero_ref, one_ref,
                  resid_ref, okeep_ref, ogot_ref, ozero_ref, oone_ref, grad_ref, out_ref):
    rows = zero_ref.shape[0]
    for at, far_ref, mid_ref, ofar_ref in (
        (0, zero_ref, mid0_ref, ozero_ref),
        (1, one_ref, mid1_ref, oone_ref),
    ):
        here = slice(at * rows, (at + 1) * rows)
        x = x_ref[here].astype(F32)
        inverse = lax.rsqrt(jnp.mean(x * x, -1, keepdims=True) + EPS)
        grad = keep_ref[0, here].astype(F32) + near_ref[here].astype(F32)
        grad = grad + far_ref[...].astype(F32)
        grad = mid_ref[...] + norm_backward(grad, x * inverse, inverse, gain_ref[...])
        grad_ref[here] = grad.astype(BF16)
        out = okeep_ref[0, here].astype(F32) + ogot_ref[0, here].astype(F32)
        out_ref[here] = (resid_ref[here] + (out + ofar_ref[...].astype(F32))).astype(BF16)


def finish(x, gain, mid0, mid1, keep, near, zero, one, resid, out_keep, out_got, out_far):
    tile, width = x.shape
    first = pl.BlockSpec((1, tile, width), lambda s: (0, 0, 0))
    full = lambda array: whole(array.shape)
    return call(
        finish_kernel,
        "finish",
        (1,),
        [full(x), full(gain), full(mid0), full(mid1), first, full(near), full(zero), full(one)]
        + [full(resid), first, first, *map(full, out_far)],
        [pl.BlockSpec((tile, width), lambda s: (0, 0))] * 2,
        [jax.ShapeDtypeStruct((tile, width), BF16)] * 2,
    )(x, gain, mid0, mid1, keep, near, zero, one, resid, out_keep, out_got, *out_far)


def norm_forward(values, gain):
    inverse = lax.rsqrt(jnp.mean(values * values, -1, keepdims=True) + EPS)
    normed = values * inverse
    return (normed, inverse, (normed * gain).astype(BF16))


def norm_backward(grad_hidden, normed, inverse, gain):
    grad_normed = grad_hidden * gain
    return inverse * (grad_normed - normed * jnp.mean(grad_normed * normed, -1, keepdims=True))


def swap(value, axis):
    return lax.ppermute(value, axis, [(0, 1), (1, 0)])


def up32(value):
    return value.astype(F32)


def join(*values):
    return jnp.concatenate(values, 0)


class Live:
    def cut(self):
        names = sorted(vars(self))
        values = lax.optimization_barrier(tuple(getattr(self, name) for name in names))
        for name, value in zip(names, values):
            setattr(self, name, value)

    @property
    def pop(self):
        return Pop(self)


class Pop:
    def __init__(self, live):
        self.live = live

    def __getattr__(self, name):
        value = getattr(self.live, name)
        delattr(self.live, name)
        return value


def tables(lengths_all, row_count):
    seq_ends = jnp.cumsum(lengths_all, 1)
    token = jnp.arange(row_count, dtype=jnp.int32)
    passed = (token[None, :, None] >= seq_ends[:, None, :]).astype(jnp.int32)
    segment = jnp.sum(passed, 2)
    offsets = token[None, :] - jnp.sum(passed * lengths_all[:, None, :], 2)
    half = HEAD_DIM // 2
    lane = jnp.arange(128, dtype=jnp.int32)
    frequency = ROPE_BASE ** (-(lane % half).astype(F32) * 2.0 / HEAD_DIM)
    angles = offsets.reshape(-1, 1).astype(F32) * frequency[None, :]
    sign = jnp.where(lane % HEAD_DIM < half, -1.0, 1.0)
    return (segment.astype(F32), jnp.cos(angles), jnp.sin(angles) * sign[None, :])


def on_device_small(
    block_input,
    out_grad,
    seq_lengths,
    attn_gain,
    w_query,
    w_key,
    w_value,
    w_output,
    mlp_gain,
    w_gate,
    w_up,
    w_down,
):
    width = block_input.shape[2]
    row_count = block_input.shape[1]
    micro = block_input.shape[0]
    tokens = micro * row_count
    head_rows = w_query.shape[0]
    kv_rows = w_key.shape[0]
    gain_width = attn_gain.shape[0]
    packed = seq_lengths.shape[2]
    units_own = w_gate.shape[0]
    first = -(-units_own // 2 // 32) * 32
    second = units_own - first
    qkv_rows = head_rows + 2 * kv_rows
    place = {name: lax.axis_index(name) for name in AXES}
    place8 = place[MID] * 4 + place[CORE] * 2 + place[SUB]
    place32 = place[ZH] * 16 + place[ZL] * 8 + place8
    index = jnp.arange(8 * kv_rows, dtype=jnp.int32)
    block, inside = index // kv_rows, index % kv_rows
    moved = (block[:, None] == (block[None, :] ^ place8)) & (inside[:, None] == inside[None, :])
    moved = moved.astype(BF16)
    index = jnp.arange(32, dtype=jnp.int32)
    ordered = (index[:, None] == (index[None, :] ^ place32)).astype(BF16)

    def pair_sum(keep, got, at):
        return up32(keep[at]) + up32(got[at])

    v = Live()
    own_x = block_input.reshape(tokens, width)
    v.own_g = out_grad.reshape(tokens, width)

    pack = join(attn_gain, mlp_gain, seq_lengths.reshape(micro * packed).astype(BF16))
    v.pack = jnp.pad(pack.reshape(1, -1), ((0, 0), (0, 256 - pack.shape[0])))
    v.pack_far = swap(v.pack, ZL)
    v.a0 = join(w_query, w_key, w_value)
    a_rows = v.a0.shape[0]
    v.w_gate, v.w_up, v.w_down, v.w_output = w_gate, w_up, w_down, w_output
    v.got_x = swap(join(v.a0, w_gate), SUB)
    v.got_y = swap(join(w_output, w_up), MID)
    v.ao = swap(join(v.a0, w_output), ZH)
    v.own_x = own_x
    v.x_far = swap(v.own_x, ZL)
    v.cut()

    v.g0x, v.u0y = v.got_x[a_rows:], v.got_y[head_rows:]
    v.a1, v.o1 = v.ao[:a_rows], v.ao[a_rows:]
    v.o0s = join(v.pop.w_output, v.got_y[:head_rows], v.a1)
    v.a0s = join(v.pop.a0, v.got_x[:a_rows], v.o1)
    v.o0t, v.a0t = swap(v.o0s, SUB), swap(v.a0s, MID)
    packs = jnp.concatenate([v.pop.pack, v.pop.pack_far], 1)
    packs = jnp.concatenate([packs, swap(packs, CORE)], 1)
    v.packs = jnp.pad(packs, ((0, 15), (0, width - packs.shape[1])))
    v.gate_low = swap(join(v.w_gate[:second], v.packs), ZH)
    v.x_core, v.x_far_core = swap(v.own_x, CORE), swap(v.x_far, CORE)
    del v.ao, v.got_x, v.got_y
    v.cut()

    packs = jnp.concatenate([v.packs[:, :1024], v.gate_low[second:, :1024]], 1)
    v.o1s = join(v.pop.o1, v.a0t[2 * a_rows :], packs)
    v.a1s = join(v.pop.a1, v.o0t[2 * head_rows :], packs)
    v.o1t, v.a1t = swap(v.o1s, SUB), swap(v.a1s, MID)
    v.gate_high = swap(v.w_gate[second:], ZH)
    v.packs_near = packs[:1]
    v.packs_across = lax.ppermute(packs[:1], (MID, SUB), [(at, 3 - at) for at in range(4)])
    lengths = v.pop.packs[0, :1024].reshape(2, 2, 256)
    lengths = lengths[:, :, 2 * gain_width : 2 * gain_width + micro * packed]
    lengths_all = lengths.transpose(1, 0, 2).reshape(4 * micro, packed).astype(jnp.int32)
    segment, v.cosine, v.sine = tables(lengths_all, row_count)
    v.segment = segment.reshape(4, micro, row_count)
    v.x = (v.own_x, v.pop.x_core, v.pop.x_far, v.pop.x_far_core)
    v.cut()

    v.u0s, v.g0s = join(v.w_up, v.pop.u0y), join(v.w_gate, v.pop.g0x)
    v.u0t, v.g0t = swap(v.u0s, SUB), swap(v.g0s, MID)
    v.u1 = swap(v.w_up, ZH)
    a_parts = (v.pop.a0s, v.pop.a0t, v.pop.a1s, v.pop.a1t)
    o_parts = (v.pop.o0s, v.pop.o0t, v.pop.o1s, v.pop.o1t)
    kv_own = join(
        *(one[: 2 * a_rows].reshape(2, a_rows, width)[:, head_rows:] for one in a_parts)
    )
    kv_core = swap(kv_own, CORE)
    packs = join(
        v.pop.packs_near, o_parts[3][-16:-15], a_parts[3][-16:-15], v.pop.packs_across
    )
    gains_rel = packs.reshape(2, 2, 2, 2, 2, 256)[..., : 2 * gain_width]
    gains_rel = gains_rel.transpose(2, 4, 0, 3, 1, 5)
    gains_all = dot(ordered, gains_rel.reshape(32, 2 * gain_width))
    v.gain_one = gains_all[:, :gain_width].reshape(1, width)
    v.gain_two = gains_all[:, gain_width:].reshape(1, width)
    attn = attn_forward(
        v.x,
        v.gain_one,
        v.cosine,
        v.sine,
        v.segment,
        moved,
        kv_own,
        kv_core,
        a_parts,
        o_parts,
        head_rows,
        row_count,
    )
    v.hidden_one, v.qkv, v.mixed, v.part_send, v.part_keep, v.wqkv, v.full_o = attn
    v.cut()

    v.g1 = join(v.gate_low[:second], v.pop.gate_high)
    del v.gate_low
    v.got_x = swap(join(v.g1, v.w_down[:first]), SUB)
    v.got_y = swap(join(v.u1, v.w_down[first:]), MID)
    v.da1 = swap(v.w_down[:first], ZH)
    v.part_got = swap(v.pop.part_send, CORE)
    mid_far = pair_sum(v.part_keep, v.part_got, 1).astype(BF16)
    v.mid_far = swap(mid_far, ZL)
    v.cut()

    v.dax, v.dby = v.got_x[units_own:], v.got_y[units_own:]
    v.g1s, v.u1s = join(v.pop.g1, v.got_x[:units_own]), join(v.pop.u1, v.got_y[:units_own])
    v.g1t, v.u1t = swap(v.g1s, MID), swap(v.u1s, SUB)
    v.resid_mid = up32(v.own_x) + (
        pair_sum(v.pop.part_keep, v.pop.part_got, 0) + up32(v.pop.mid_far)
    )
    v.db1 = swap(v.w_down[first:], ZH)
    h_own = norm_forward(v.resid_mid, v.gain_two)[2]
    v.h_far, v.h_core = swap(h_own, ZL), swap(h_own, CORE)
    v.h_own = h_own
    del v.got_x, v.got_y
    v.cut()

    v.db0s = join(v.w_down[first:], v.pop.dby, v.da1)
    v.da0s = join(v.w_down[:first], v.pop.dax, v.db1)
    v.db0t, v.da0t = swap(v.db0s, SUB), swap(v.da0s, MID)
    v.g_far, v.g_core = swap(v.own_g, ZL), swap(v.own_g, CORE)
    v.h = (v.pop.h_own, v.pop.h_core, v.h_far, swap(v.h_far, CORE))
    del v.w_gate, v.w_up, v.w_down, v.h_far
    v.gate_parts = (v.pop.g0s, v.pop.g0t, v.pop.g1s, v.pop.g1t)
    v.up_parts = (v.pop.u0s, v.pop.u0t, v.pop.u1s, v.pop.u1t)
    v.inner, v.dgate, v.dup = units(v.h, v.gate_parts, v.up_parts)
    v.cut()

    v.da1s = join(v.pop.da1, v.db0t[2 * second :])
    v.db1s = join(v.pop.db1, v.da0t[2 * first :])
    v.da1t, v.db1t = swap(v.da1s, MID), swap(v.db1s, SUB)
    v.g = (v.own_g, v.pop.g_core, v.g_far, swap(v.g_far, CORE))
    del v.g_far
    v.dg = weight_grad(v.inner, v.g, "down_grad")
    v.cut()

    def step_one(grads):
        keep_a, send_a, keep_b, send_b = grads
        return (keep_a, swap(send_a, MID), keep_b, swap(send_b, SUB))

    def sums_one(pairs):
        keep_a, got_a, keep_b, got_b = pairs
        far = slice(2, 4)
        return pairs + (
            pair_sum(keep_a, got_a, far).astype(BF16),
            pair_sum(keep_b, got_b, far).astype(BF16),
        )

    def step_two(pairs):
        return pairs[:4] + (swap(pairs[4], SUB), swap(pairs[5], MID))

    def part_sum(pairs, at, low, high):
        half = pairs[0].shape[2]
        sums = []
        for side in range(2):
            here = slice(max(low - side * half, 0), min(high - side * half, half))
            if here.start < here.stop:
                keep, got, two = pairs[2 * side], pairs[2 * side + 1], pairs[4 + side]
                sums.append(up32(keep[at, :, here]) + up32(got[at, :, here]) + up32(two[at, :, here]))
        return sums[0] if len(sums) == 1 else jnp.concatenate(sums, 1)

    def last_send(pairs, low, high):
        return part_sum(pairs, 1, low, high).astype(BF16)

    def step_three(pairs, send):
        return pairs + (swap(send, ZH),)

    def total(pairs):
        last = jnp.concatenate([up32(one) for one in pairs[6:]], 1)
        return part_sum(pairs, 0, 0, width) + last

    even, early, most = width // 2, width * 5 // 8, width * 3 // 4

    def gain_step(name):
        at = 1 + AXES.index(name)
        low, high = jnp.split(v.gain_grads, 2, at)
        mine = jnp.where(place[name] == 0, low, high)
        sent = jnp.where(place[name] == 0, high, low)
        v.gain_grads = mine + swap(sent, name)

    def far_of(keep, got, micro_at):
        here = slice(micro_at * row_count, (micro_at + 1) * row_count)
        return (up32(keep[1, here]) + up32(got)).astype(BF16)

    def mid_grads(micro_at, far):
        here = slice(micro_at * row_count, (micro_at + 1) * row_count)
        gh2 = up32(v.gh2_keep[0, here]) + up32(v.gh2_near[here]) + up32(far)
        resid = v.resid_mid[here]
        inverse = lax.rsqrt(jnp.mean(resid * resid, -1, keepdims=True) + EPS)
        normed = resid * inverse
        grad_mid = up32(v.own_g[here]) + norm_backward(gh2, normed, inverse, v.gain_two)
        return grad_mid, grad_mid.astype(BF16), jnp.sum(gh2 * normed, 0, keepdims=True)

    v.dg = step_one(v.dg)
    v.down_parts = (
        *(v.pop.da0s, v.pop.da0t, v.pop.da1s, v.pop.da1t),
        *(v.pop.db0s, v.pop.db0t, v.pop.db1s, v.pop.db1t),
    )
    v.gg, v.gu = unit_grads(v.pop.g, v.down_parts, v.pop.dgate, v.pop.dup, first)
    *send, v.gh2_keep = sum_rows(
        (v.gg, v.gu), (*v.pop.gate_parts, *v.pop.up_parts), "hidden_grads"
    )
    v.gh2_near = send[0]
    v.gh2_far = (swap(send[1], CORE), swap(send[2], CORE))
    v.cut()
    v.dg = sums_one(v.dg)
    v.cut()

    v.dg = step_two(v.dg)
    v.gh2_zero = swap(far_of(v.gh2_keep, v.gh2_far[0], 0), ZL)
    v.gh2_near = swap(v.gh2_near, CORE)
    v.gh2_one = far_of(v.gh2_keep, v.gh2_far[1], 1)
    v.gw = weight_grad(v.pop.gg, v.h, "gate_grad")
    v.cut()

    v.gw = step_one(v.gw)
    v.gh2_one = swap(v.gh2_one, ZL)
    v.grad_mid0, v.gb0, v.mlp_terms = mid_grads(0, v.pop.gh2_zero)
    v.gb0_far = swap(v.gb0, ZL)
    v.dg_send = last_send(v.dg, early, width)
    v.dg = step_three(v.dg, last_send(v.dg, 0, early))
    v.out_send, v.out_keep = sum_rows((v.pop.inner,), v.pop.down_parts, "block_out", first)
    v.cut()

    v.grad_mid1, v.gb1, terms = mid_grads(1, v.pop.gh2_one)
    v.mlp_terms = v.mlp_terms + terms
    v.gb1_far = swap(v.gb1, ZL)
    del v.gh2_keep, v.gh2_near, v.gh2_far
    v.gw = step_two(sums_one(v.gw))
    v.dg = step_three(v.dg, v.pop.dg_send)
    v.out_got = swap(v.pop.out_send, CORE)
    v.uw = weight_grad(v.pop.gu, v.pop.h, "up_grad")
    v.cut()

    v.uw = step_one(v.uw)
    v.gw_send = last_send(v.gw, most, width)
    v.gw = step_three(v.gw, last_send(v.gw, 0, most))
    v.out_zero = far_of(v.out_keep, v.out_got[1, :row_count], 0)
    v.out_zero = swap(v.out_zero, ZL)
    gb = (v.pop.gb0, v.pop.gb1), (v.pop.gb0_far, v.pop.gb1_far)
    v.gb = tuple(
        one for rows in gb for one in (*rows, *(swap(piece, CORE) for piece in rows))
    )
    v.gqkv, attn_terms, *send, v.gh1_keep = attn_backward(
        v.gb,
        v.pop.x,
        v.pop.qkv,
        v.pop.cosine,
        v.pop.sine,
        v.pop.segment,
        v.pop.wqkv,
        v.pop.full_o,
        row_count,
    )
    v.gh1_near = send[0]
    v.gh1_far = (swap(send[1], CORE), swap(send[2], CORE))
    gain_grads = join(attn_terms, v.pop.mlp_terms)
    v.gain_grads = gain_grads.reshape(2, 2, 2, 2, 2, 2, gain_width)
    v.cut()
    v.uw = sums_one(v.uw)
    v.cut()

    v.uw = step_two(v.uw)
    v.gh1_zero = swap(far_of(v.gh1_keep, v.gh1_far[0], 0), ZL)
    v.gh1_near = swap(v.gh1_near, CORE)
    v.gw = step_three(v.gw, v.pop.gw_send)
    v.aw = attn_grads(
        v.pop.gqkv, v.pop.hidden_one, v.pop.mixed, v.pop.gb, moved, head_rows, kv_rows
    )
    v.gh1_one = far_of(v.gh1_keep, v.gh1_far[1], 1)
    v.out_one = far_of(v.out_keep, v.out_got[1, row_count:], 1)
    v.cut()

    v.aw = step_one(v.aw)
    v.gh1_one = swap(v.gh1_one, ZL)
    v.uw_send = last_send(v.uw, early, width)
    v.uw = step_three(v.uw, last_send(v.uw, 0, early))
    v.cut()
    v.aw = sums_one(v.aw)
    v.cut()

    v.aw = step_two(v.aw)
    v.uw = step_three(v.uw, v.pop.uw_send)
    v.out_one = swap(v.out_one, ZL)
    gain_step(ZH)
    v.cut()

    aw = step_three(v.aw, last_send(v.aw, 0, even))
    aw = step_three(aw, last_send(v.aw, even, width))
    gain_step(MID)
    gain_step(SUB)
    gain_step(CORE)
    gain_step(ZL)
    input_grad, block_out = finish(
        v.own_x,
        v.gain_one,
        v.pop.grad_mid0,
        v.pop.grad_mid1,
        v.pop.gh1_keep,
        v.pop.gh1_near,
        v.pop.gh1_zero,
        v.pop.gh1_one,
        v.pop.resid_mid,
        v.pop.out_keep,
        v.pop.out_got,
        (v.pop.out_zero, v.pop.out_one),
    )
    down_grad, gate_grad, up_grad = (
        total_sum(v.pop.dg), total_sum(v.pop.gw), total_sum(v.pop.uw)
    )
    grads = total(aw)
    kv_grads = grads[head_rows:qkv_rows] + swap(grads[qkv_rows : qkv_rows + 2 * kv_rows], CORE)
    return (
        block_out.reshape(block_input.shape),
        input_grad.reshape(block_input.shape),
        v.gain_grads[0].reshape(gain_width),
        grads[:head_rows],
        kv_grads[:kv_rows],
        kv_grads[kv_rows:],
        grads[qkv_rows + 2 * kv_rows :],
        v.gain_grads[1].reshape(gain_width),
        gate_grad,
        up_grad,
        down_grad,
    )


def positions(lengths_row, row_count):
    seq_ends = jnp.cumsum(lengths_row)
    starts = seq_ends - lengths_row
    token_index = jnp.arange(row_count, dtype=jnp.int32)
    segment = jnp.sum((token_index[:, None] >= seq_ends[None, :]).astype(jnp.int32), 1)
    chosen = segment[:, None] == jnp.arange(lengths_row.shape[0], dtype=jnp.int32)[None, :]
    offsets = token_index - jnp.sum(jnp.where(chosen, starts[None, :], 0), 1)
    allowed = (segment[:, None] == segment[None, :]) & (
        token_index[None, :] <= token_index[:, None]
    )
    return (offsets, allowed)


def rotary_tables(offsets, width):
    half_width = width // 2
    frequency = ROPE_BASE ** (-jnp.arange(half_width, dtype=jnp.float32) * 2.0 / width)
    angles = offsets.astype(jnp.float32)[:, None] * frequency[None, :]
    return (jnp.cos(angles)[:, None, :], jnp.sin(angles)[:, None, :])


def rotate(values, cosine, sine_table):
    half_width = values.shape[-1] // 2
    first_half = values[..., :half_width]
    second_half = values[..., half_width:]
    return jnp.concatenate(
        [
            first_half * cosine - second_half * sine_table,
            second_half * cosine + first_half * sine_table,
        ],
        -1,
    )


def rotate_back(grads, cosine, sine_table):
    half_width = grads.shape[-1] // 2
    upper_half = grads[..., :half_width]
    lower_half = grads[..., half_width:]
    return jnp.concatenate(
        [
            upper_half * cosine + lower_half * sine_table,
            lower_half * cosine - upper_half * sine_table,
        ],
        -1,
    )


def project(activity, weight):
    return lax.dot_general(
        activity, weight, (((1,), (1,)), ((), ())), preferred_element_type=jnp.float32
    )


def apply_rows(activity, weight):
    return jnp.dot(activity, weight, preferred_element_type=jnp.float32)


def general_norm_forward(values, gain_row):
    inverse = lax.rsqrt(jnp.mean(values * values, -1, keepdims=True) + EPS)
    normed = values * inverse
    return (normed, inverse, (normed * gain_row.astype(jnp.float32)).astype(jnp.bfloat16))


def general_norm_backward(grad_hidden, normed, inverse, gain_row):
    grad_normed = grad_hidden * gain_row.astype(jnp.float32)
    return inverse * (grad_normed - normed * jnp.mean(grad_normed * normed, -1, keepdims=True))


def attention_scores(query_rot, key_rot, allowed):
    scores = jnp.einsum(
        "qhgd,khd->hgqk", query_rot, key_rot, preferred_element_type=jnp.float32
    ) * HEAD_DIM ** (-0.5)
    return jnp.where(allowed, scores, NEG_LARGE)


def forward_pass(block_rows, lengths_row, gathered):
    attn_gain, w_query, w_key, w_value, w_output, mlp_gain, w_gate, w_up, w_down = gathered
    row_count = block_rows.shape[0]
    query_heads = w_query.shape[0] // HEAD_DIM
    key_heads = w_key.shape[0] // HEAD_DIM
    group_size = query_heads // key_heads
    offsets, allowed = positions(lengths_row, row_count)
    cosine, sine_table = rotary_tables(offsets, HEAD_DIM)
    resid_in = block_rows.astype(jnp.float32)
    normed_one, inverse_one, hidden_one = general_norm_forward(resid_in, attn_gain)
    query_lin = project(hidden_one, w_query).reshape(row_count, query_heads, HEAD_DIM)
    key_lin = project(hidden_one, w_key).reshape(row_count, key_heads, HEAD_DIM)
    value_rows = (
        project(hidden_one, w_value).astype(jnp.bfloat16).reshape(row_count, key_heads, HEAD_DIM)
    )
    query_rot = (
        rotate(query_lin, cosine, sine_table)
        .astype(jnp.bfloat16)
        .reshape(row_count, key_heads, group_size, HEAD_DIM)
    )
    key_rot = rotate(key_lin, cosine, sine_table).astype(jnp.bfloat16)
    scores = attention_scores(query_rot, key_rot, allowed)
    top_score = jnp.max(scores, -1, keepdims=True)
    exp_scores = jnp.exp(scores - top_score)
    row_total = jnp.sum(exp_scores, -1, keepdims=True)
    prob_low = (exp_scores / row_total).astype(jnp.bfloat16)
    log_total = top_score + jnp.log(row_total)
    mixed = jnp.einsum("hgqk,khd->qhgd", prob_low, value_rows, preferred_element_type=jnp.float32)
    mixed = mixed.astype(jnp.bfloat16).reshape(row_count, query_heads * HEAD_DIM)
    resid_mid = resid_in + apply_rows(mixed, w_output)
    normed_two, inverse_two, hidden_two = general_norm_forward(resid_mid, mlp_gain)
    gate_rows = project(hidden_two, w_gate)
    up_rows = project(hidden_two, w_up)
    inner = (jax.nn.silu(gate_rows) * up_rows).astype(jnp.bfloat16)
    block_out = (resid_mid + apply_rows(inner, w_down)).astype(jnp.bfloat16)
    saved = (
        allowed,
        cosine,
        sine_table,
        normed_one,
        inverse_one,
        hidden_one,
        value_rows,
        query_rot,
        key_rot,
        log_total,
        mixed,
        normed_two,
        inverse_two,
        hidden_two,
        gate_rows,
        up_rows,
        inner,
    )
    return (block_out, saved)


def backward_pass(grad_rows, saved, gathered):
    attn_gain, w_query, w_key, w_value, w_output, mlp_gain, w_gate, w_up, w_down = gathered
    (
        allowed,
        cosine,
        sine_table,
        normed_one,
        inverse_one,
        hidden_one,
        value_rows,
        query_rot,
        key_rot,
        log_total,
        mixed,
        normed_two,
        inverse_two,
        hidden_two,
        gate_rows,
        up_rows,
        inner,
    ) = saved
    row_count = grad_rows.shape[0]
    grad_out = grad_rows.astype(jnp.float32)
    grad_inner = project(grad_rows, w_down)
    sigmoid_gate = jax.nn.sigmoid(gate_rows)
    silu_gate = gate_rows * sigmoid_gate
    grad_gate = (
        grad_inner * up_rows * sigmoid_gate * (1.0 + gate_rows * (1.0 - sigmoid_gate))
    ).astype(jnp.bfloat16)
    grad_up = (grad_inner * silu_gate).astype(jnp.bfloat16)
    grad_hidden_two = apply_rows(grad_gate, w_gate) + apply_rows(grad_up, w_up)
    grad_mid = grad_out + general_norm_backward(grad_hidden_two, normed_two, inverse_two, mlp_gain)
    grad_branch = grad_mid.astype(jnp.bfloat16)
    grad_mixed = project(grad_branch, w_output).astype(jnp.bfloat16).reshape(query_rot.shape)
    scores = attention_scores(query_rot, key_rot, allowed)
    attn_probs = jnp.exp(scores - log_total)
    prob_low = attn_probs.astype(jnp.bfloat16)
    grad_probs = jnp.einsum(
        "qhgd,khd->hgqk", grad_mixed, value_rows, preferred_element_type=jnp.float32
    )
    grad_scores = attn_probs * (grad_probs - jnp.sum(grad_probs * attn_probs, -1, keepdims=True))
    grad_scores = grad_scores.astype(jnp.bfloat16)
    grad_value = jnp.einsum(
        "hgqk,qhgd->khd", prob_low, grad_mixed, preferred_element_type=jnp.float32
    )
    grad_value = grad_value.astype(jnp.bfloat16).reshape(row_count, -1)
    score_scale = HEAD_DIM ** (-0.5)
    grad_qrot = (
        jnp.einsum("hgqk,khd->qhgd", grad_scores, key_rot, preferred_element_type=jnp.float32)
        * score_scale
    )
    grad_krot = (
        jnp.einsum("hgqk,qhgd->khd", grad_scores, query_rot, preferred_element_type=jnp.float32)
        * score_scale
    )
    grad_query = rotate_back(grad_qrot.reshape(row_count, -1, HEAD_DIM), cosine, sine_table)
    grad_query = grad_query.astype(jnp.bfloat16).reshape(row_count, -1)
    grad_key = (
        rotate_back(grad_krot, cosine, sine_table).astype(jnp.bfloat16).reshape(row_count, -1)
    )
    grad_hidden_one = (
        apply_rows(grad_query, w_query)
        + apply_rows(grad_key, w_key)
        + apply_rows(grad_value, w_value)
    )
    grad_input = (
        grad_mid + general_norm_backward(grad_hidden_one, normed_one, inverse_one, attn_gain)
    ).astype(jnp.bfloat16)
    gain_terms = jnp.stack(
        [jnp.sum(grad_hidden_one * normed_one, 0), jnp.sum(grad_hidden_two * normed_two, 0)]
    )
    stored = (
        grad_query,
        hidden_one,
        grad_key,
        grad_value,
        mixed,
        grad_branch,
        grad_gate,
        hidden_two,
        grad_up,
        inner,
        grad_rows,
    )
    return (grad_input, stored, gain_terms)


def slice_term(left_rows, right_rows, owner, width):
    piece = lax.dynamic_slice_in_dim(left_rows, owner * width, width, 1)
    return lax.dot_general(
        piece, right_rows, (((0,), (0,)), ((), ())), preferred_element_type=jnp.float32
    )


def on_device_general(
    block_input,
    out_grad,
    seq_lengths,
    attn_gain,
    w_query,
    w_key,
    w_value,
    w_output,
    mlp_gain,
    w_gate,
    w_up,
    w_down,
):
    block_outs = []
    grad_inputs = []
    collected = [[] for member in range(11)]
    gain_total = jnp.zeros((2, block_input.shape[2]), jnp.float32)
    for batch_index in range(block_input.shape[0]):
        forward_layer = (
            lax.all_gather(attn_gain, DEVICES, axis=0, tiled=True),
            lax.all_gather(w_query, DEVICES, axis=0, tiled=True),
            lax.all_gather(w_key, DEVICES, axis=0, tiled=True),
            lax.all_gather(w_value, DEVICES, axis=0, tiled=True),
            lax.all_gather(w_output, DEVICES, axis=0, tiled=True),
            lax.all_gather(mlp_gain, DEVICES, axis=0, tiled=True),
            lax.all_gather(w_gate, DEVICES, axis=0, tiled=True),
            lax.all_gather(w_up, DEVICES, axis=0, tiled=True),
            lax.all_gather(w_down, DEVICES, axis=0, tiled=True),
        )
        block_out, saved = forward_pass(
            block_input[batch_index], seq_lengths[batch_index, 0], forward_layer
        )
        backward_layer = (
            lax.all_gather(attn_gain, DEVICES, axis=0, tiled=True),
            lax.all_gather(w_query, DEVICES, axis=0, tiled=True),
            lax.all_gather(w_key, DEVICES, axis=0, tiled=True),
            lax.all_gather(w_value, DEVICES, axis=0, tiled=True),
            lax.all_gather(w_output, DEVICES, axis=0, tiled=True),
            lax.all_gather(mlp_gain, DEVICES, axis=0, tiled=True),
            lax.all_gather(w_gate, DEVICES, axis=0, tiled=True),
            lax.all_gather(w_up, DEVICES, axis=0, tiled=True),
            lax.all_gather(w_down, DEVICES, axis=0, tiled=True),
        )
        grad_input, stored, gain_terms = backward_pass(out_grad[batch_index], saved, backward_layer)
        block_outs.append(block_out)
        grad_inputs.append(grad_input)
        gain_total = gain_total + gain_terms
        for member in range(11):
            collected[member].append(stored[member])
    joined = [jnp.concatenate(member_list, 0) for member_list in collected]
    model_width = block_input.shape[2]
    query_width = w_query.shape[0]
    key_width = w_key.shape[0]
    hidden_width = w_gate.shape[0]
    gain_width = attn_gain.shape[0]
    own_rows = 2 * query_width + 2 * key_width + 3 * hidden_width + 1
    filler = jnp.zeros((model_width - 2 * gain_width,), jnp.float32)

    def owner_block(owner):
        gain_row = jnp.concatenate(
            [
                lax.dynamic_slice_in_dim(gain_total[0], owner * gain_width, gain_width, 0),
                lax.dynamic_slice_in_dim(gain_total[1], owner * gain_width, gain_width, 0),
                filler,
            ],
            0,
        )
        return jnp.concatenate(
            [
                slice_term(joined[0], joined[1], owner, query_width),
                slice_term(joined[2], joined[1], owner, key_width),
                slice_term(joined[3], joined[1], owner, key_width),
                slice_term(joined[4], joined[5], owner, query_width),
                slice_term(joined[6], joined[7], owner, hidden_width),
                slice_term(joined[8], joined[7], owner, hidden_width),
                slice_term(joined[9], joined[10], owner, hidden_width),
                gain_row[None, :],
            ],
            0,
        )

    owner_count = own_rows * lax.axis_size(DEVICES) // own_rows
    owners = jnp.arange(owner_count, dtype=jnp.int32)
    blocks = lax.map(owner_block, owners)
    owned = lax.psum_scatter(
        blocks.reshape(owner_count * own_rows, model_width),
        DEVICES,
        scatter_dimension=0,
        tiled=True,
    )
    cuts = [
        query_width,
        key_width,
        key_width,
        query_width,
        hidden_width,
        hidden_width,
        hidden_width,
    ]
    pieces = []
    offset = 0
    for width in cuts:
        pieces.append(owned[offset : offset + width])
        offset = offset + width
    gain_row = owned[offset]
    return (
        jnp.stack(block_outs),
        jnp.stack(grad_inputs),
        gain_row[:gain_width],
        pieces[0],
        pieces[1],
        pieces[2],
        pieces[3],
        gain_row[gain_width : 2 * gain_width],
        pieces[4],
        pieces[5],
        pieces[6],
    )


def solution(mesh):
    groups, sub = mesh.shape["dp"], mesh.shape["sub"]
    rows, weight, gain = P(None, DEVICES, None), P(DEVICES, None), P(DEVICES)
    body = on_device_general
    if groups == 16 and sub == 2:
        mesh = Mesh(mesh.devices.reshape(2, 2, groups // 8, 2, sub), AXES)
        rows, weight, gain = P(None, AXES, None), P(AXES, None), P(AXES)
        body = on_device_small
    return jax.shard_map(
        body,
        mesh=mesh,
        in_specs=(rows, rows, rows, gain) + (weight,) * 4 + (gain,) + (weight,) * 3,
        out_specs=(rows, rows, gain) + (weight,) * 4 + (gain,) + (weight,) * 3,
        check_vma=False,
    )
```

```python
import functools
import jax
import jax.numpy as jnp
from jax import lax
from jax.experimental import pallas as pl
from jax.experimental.pallas import tpu as pltpu
from jax.sharding import Mesh
from jax.sharding import PartitionSpec as P

ZH, ZL, MID, CORE, SUB = AXES = ("zh", "zl", "mid", "core", "sub")
DEVICES = ("dp", "sub")

HEAD_DIM = 64
EPS = 1e-05
ROPE_BASE = 10000.0
NEG_LARGE = -1e30
SUM_STEPS = 4
F32 = jnp.float32
BF16 = jnp.bfloat16
NT = (((1,), (1,)), ((), ()))
NN = (((1,), (0,)), ((), ()))
TN = (((0,), (0,)), ((), ()))


def dot(a, b, dims=NN):
    return lax.dot_general(a, b, dims, preferred_element_type=F32)


def call(kernel, name, grid, in_specs, out_specs, out_shape, scratch=()):
    return pl.pallas_call(
        kernel,
        grid=grid,
        in_specs=in_specs,
        out_specs=out_specs,
        out_shape=out_shape,
        scratch_shapes=scratch,
        name=name,
        cost_estimate=pl.CostEstimate(flops=1000, bytes_accessed=1000, transcendentals=0),
        compiler_params=pltpu.CompilerParams(
            dimension_semantics=("arbitrary",) * len(grid), vmem_limit_bytes=56 << 20
        ),
    )


def whole(shape):
    zeros = (0,) * len(shape)
    return pl.BlockSpec(shape, lambda *_: zeros, pipeline_mode=pl.Buffered(1))


def turn(values, cosine, sine):
    lane = lax.broadcasted_iota(jnp.int32, (values.shape[0], 128), 1)
    low = lane % HEAD_DIM < HEAD_DIM // 2
    blocks = []
    for at in range(0, values.shape[1], 128):
        block = values[:, at : at + 128]
        other = jnp.where(
            low,
            pltpu.roll(block, 128 - HEAD_DIM // 2, 1),
            pltpu.roll(block, HEAD_DIM // 2, 1),
        )
        blocks.append(block * cosine + other * sine)
    return jnp.concatenate(blocks, 1) if len(blocks) > 1 else blocks[0]


def two_heads(rows):
    low = lax.broadcasted_iota(jnp.int32, rows.shape, 1) < HEAD_DIM
    zero = jnp.zeros_like(rows)
    return jnp.concatenate([jnp.where(low, rows, zero), jnp.where(low, zero, rows)], 0)


def one_head(rows):
    half = rows.shape[0] // 2
    low = lax.broadcasted_iota(jnp.int32, (half, 128), 1) < HEAD_DIM
    return jnp.where(low, rows[:half], rows[half:])


def stack_lanes(values):
    return jnp.concatenate([values[:, at : at + 128] for at in range(0, values.shape[1], 128)], 0)


def unstack_lanes(values, rows):
    return jnp.concatenate([values[at : at + rows] for at in range(0, values.shape[0], rows)], 1)


def mask_of(segment):
    row = segment.shape[1]
    query = lax.broadcasted_iota(jnp.int32, (row, row), 0)
    key = lax.broadcasted_iota(jnp.int32, (row, row), 1)
    across = jnp.broadcast_to(segment, (row, row))
    return (across == across.T) & (key <= query)


def probabilities(stacked_q, keys2, allowed, row):
    scores = dot(stacked_q, keys2, NT)
    blocks = []
    for at in range(0, scores.shape[0], row):
        halves = []
        for side in range(2):
            part = scores[at : at + row, side * row : (side + 1) * row]
            part = jnp.where(allowed, part, NEG_LARGE)
            part = jnp.exp(part - jnp.max(part, -1, keepdims=True))
            halves.append(part * (1.0 / jnp.sum(part, -1, keepdims=True)))
        blocks.append(jnp.concatenate(halves, 1))
    return jnp.concatenate(blocks, 0)


def owner(mid, sub, zh):
    return 4 * mid + 2 * sub + zh


def assemble(parts, into, kind, rows, step=None, stride=None, offset=0):
    step = rows if step is None else step
    stride = rows if stride is None else stride
    for zh in range(2):
        for far in range(2):
            for inner in range(2):
                at = owner(far, inner, zh) if kind == "a" else owner(inner, far, zh)
                at = at * stride + offset
                into[at : at + rows] = parts[2 * zh + far][inner * step : inner * step + rows]


def assemble_down(parts, into, first):
    stride = into.shape[0] // 8
    assemble(parts[:4], into, "a", first, stride=stride)
    assemble(parts[4:], into, "b", stride - first, stride=stride, offset=first)


def tile_at(step):
    return (2 * step + 1) % 5


def pick(tile, refs, into):
    for at, ref in enumerate(refs):

        @pl.when(tile == at)
        def _(ref=ref):
            into[...] = ref[...]


def halves(part, send_ref, keep_ref, here=slice(None)):
    step = pl.program_id(0)

    @pl.when(step < 2)
    def _():
        send_ref[0, :, here] = part.astype(BF16)

    @pl.when(step >= 2)
    def _():
        keep_ref[0, :, here] = part.astype(BF16)


def halves_out(tile, width):
    specs = [
        pl.BlockSpec((1, tile, width), lambda s: (jnp.minimum(s, 1), 0, 0)),
        pl.BlockSpec((1, tile, width), lambda s: (jnp.maximum(s - 2, 0), 0, 0)),
    ]
    return specs, [jax.ShapeDtypeStruct((2, tile, width), BF16)] * 2


def quarters(part, send_refs, keep_ref, here=slice(None)):
    step = pl.program_id(0)
    near_ref, zero_ref, one_ref = send_refs
    rows = zero_ref.shape[0]

    @pl.when(step == 0)
    def _():
        near_ref[:, here] = part.astype(BF16)

    @pl.when(step == 1)
    def _():
        zero_ref[:, here] = part[:rows].astype(BF16)
        one_ref[:, here] = part[rows:].astype(BF16)

    @pl.when(step >= 2)
    def _():
        keep_ref[0, :, here] = part.astype(BF16)


def quarters_out(tile, width):
    specs, shapes = halves_out(tile, width)
    sizes = [(tile, width)] + [(tile // 2, width)] * 2
    return (
        [pl.BlockSpec(size, lambda s: (0, 0)) for size in sizes] + specs[1:],
        [jax.ShapeDtypeStruct(size, BF16) for size in sizes] + shapes[1:],
    )


def pick_two(tile, refs, into):
    rows = refs[0].shape[0]
    for at in range(4):

        @pl.when(tile == at)
        def _(at=at):
            into[:rows] = refs[2 * at][...]
            into[rows:] = refs[2 * at + 1][...]


def attn_forward_kernel(row, head_rows, *refs):
    x_refs, (gain_ref, cos_ref, sin_ref, seg_ref, moved_ref, kv_own_ref, kv_core_ref) = (
        refs[:4],
        refs[4:11],
    )
    a_refs, o_refs = refs[11:15], refs[15:19]
    hid_ref, qkv_ref, mixed_ref, send_ref, keep_ref, wqkv_ref, wo_ref, x_ref = refs[19:]
    step = pl.program_id(0)
    width = 8 * head_rows
    pick(tile_at(step), x_refs, x_ref)

    @pl.when(step == 0)
    def _():
        assemble(a_refs, wqkv_ref, "a", head_rows, step=head_rows + HEAD_DIM // 4)
        assemble(o_refs, wo_ref, "b", head_rows)
        kv_rows = HEAD_DIM // 8
        for side in range(2):
            both = [
                [ref[4 * side + at].astype(F32) for ref in (kv_own_ref, kv_core_ref)]
                for at in range(4)
            ]
            for which in range(2):
                here = slice(which * kv_rows, (which + 1) * kv_rows)
                parts = [
                    both[mid * 2 + sub][core][here]
                    for mid in range(2)
                    for core in range(2)
                    for sub in range(2)
                ]
                placed = dot(moved_ref[...], jnp.concatenate(parts, 0).astype(BF16)).astype(BF16)
                low = width + (2 * which + side) * HEAD_DIM
                wqkv_ref[low : low + HEAD_DIM] = placed

    x = x_ref[...].astype(F32)
    inverse = lax.rsqrt(jnp.mean(x * x, -1, keepdims=True) + EPS)
    hidden = (x * inverse * gain_ref[...]).astype(BF16)
    hid_ref[...] = hidden
    lin = dot(hidden, wqkv_ref[...], NT)
    cosine, sine = cos_ref[...], sin_ref[...]
    qk = turn(lin[:, : width + 128], cosine, sine).astype(BF16)
    v_rows = lin[:, width + 128 :].astype(BF16)
    qkv_ref[:, : width + 128] = qk
    qkv_ref[:, width + 128 :] = v_rows
    scale = HEAD_DIM ** (-0.5)
    for at in range(0, x.shape[0], row):
        allowed = mask_of(seg_ref[0, at // row : at // row + 1])
        keys2 = two_heads(qk[at : at + row, width:] * jnp.asarray(scale, BF16))
        values2 = two_heads(v_rows[at : at + row])
        probs = probabilities(stack_lanes(qk[at : at + row, :width]), keys2, allowed, row)
        mixed = dot(probs.astype(BF16), values2).astype(BF16)
        mixed_ref[at : at + row] = unstack_lanes(mixed, row)
    halves(dot(mixed_ref[...], wo_ref[...]), send_ref, keep_ref)


def attn_forward(x, gain, cosine, sine, segment, moved, kv_own, kv_core, a_parts, o_parts,
                 head_rows, row):
    tile, width = x[0].shape
    rows = lambda n: pl.BlockSpec((tile, n), lambda s: (tile_at(s), 0))
    full = lambda n: pl.BlockSpec((n, width), lambda s: (0, 0))
    q_width = 8 * head_rows
    shape = lambda *dims: jax.ShapeDtypeStruct(dims, BF16)
    half_specs, half_shapes = halves_out(tile, width)
    return call(
        functools.partial(attn_forward_kernel, row, head_rows),
        "attn_forward",
        (4,),
        [whole(one.shape) for one in x]
        + [
            whole((1, width)),
            rows(128),
            rows(128),
            pl.BlockSpec((1,) + segment.shape[1:], lambda s: (tile_at(s), 0, 0)),
        ]
        + [whole(one.shape) for one in (moved, kv_own, kv_core, *a_parts, *o_parts)],
        [rows(width), rows(q_width + 256), rows(q_width)]
        + half_specs
        + [full(q_width + 256), full(q_width)],
        [shape(4 * tile, width), shape(4 * tile, q_width + 256), shape(4 * tile, q_width)]
        + half_shapes
        + [shape(q_width + 256, width), shape(q_width, width)],
        [pltpu.VMEM((tile, width), BF16)],
    )(*x, gain, cosine, sine, segment, moved, kv_own, kv_core, *a_parts, *o_parts)


def attn_backward_kernel(row, *refs):
    g_refs, x_refs = refs[:8], refs[8:12]
    qkv_ref, cos_ref, sin_ref, seg_ref, wqkv_ref, wo_ref = refs[12:18]
    gqkv_ref, gain_ref, *send_refs, keep_ref, g_ref, x_ref = refs[18:]
    step = pl.program_id(0)
    pick_two(tile_at(step), g_refs, g_ref)
    pick(tile_at(step), x_refs, x_ref)
    grad_mixed = dot(g_ref[...], wo_ref[...], NT).astype(BF16)
    width = grad_mixed.shape[1]
    qkv = qkv_ref[...]
    cosine, sine = cos_ref[...], -sin_ref[...]
    scale = HEAD_DIM ** (-0.5)
    for at in range(0, grad_mixed.shape[0], row):
        here = slice(at, at + row)
        allowed = mask_of(seg_ref[0, at // row : at // row + 1])
        keys2 = two_heads(qkv[here, width : width + 128] * jnp.asarray(scale, BF16))
        values2 = two_heads(qkv[here, width + 128 :])
        stacked_q = stack_lanes(qkv[here, :width])
        stacked_g = stack_lanes(grad_mixed[here])
        probs = probabilities(stacked_q, keys2, allowed, row)
        grad_probs = dot(stacked_g, values2, NT)
        moved = grad_probs * probs
        left = probs[:, :row] * (
            grad_probs[:, :row] - jnp.sum(moved[:, :row], -1, keepdims=True)
        )
        right = probs[:, row:] * (
            grad_probs[:, row:] - jnp.sum(moved[:, row:], -1, keepdims=True)
        )
        grad_scores = jnp.concatenate([left, right], 1).astype(BF16)
        grad_value = one_head(dot(probs.astype(BF16), stacked_g, TN))
        grad_key = one_head(dot(grad_scores, stacked_q, TN)) * scale
        grad_query = unstack_lanes(dot(grad_scores, keys2), row)
        gqkv_ref[here, :width] = turn(grad_query, cosine[here], sine[here]).astype(BF16)
        gqkv_ref[here, width : width + 128] = turn(grad_key, cosine[here], sine[here]).astype(BF16)
        gqkv_ref[here, width + 128 :] = grad_value.astype(BF16)
    part = dot(gqkv_ref[...], wqkv_ref[...])
    x = x_ref[...].astype(F32)
    normed = x * lax.rsqrt(jnp.mean(x * x, -1, keepdims=True) + EPS)
    terms = jnp.sum(part * normed, 0, keepdims=True)

    @pl.when(step == 0)
    def _():
        gain_ref[...] = terms

    @pl.when(step > 0)
    def _():
        gain_ref[...] += terms

    quarters(part, send_refs, keep_ref)


def attn_backward(grads, x, qkv, cosine, sine, segment, wqkv, wo, row):
    tile, width = x[0].shape
    rows = lambda n: pl.BlockSpec((tile, n), lambda s: (tile_at(s), 0))
    half_specs, half_shapes = quarters_out(tile, width)
    return call(
        functools.partial(attn_backward_kernel, row),
        "attn_backward",
        (4,),
        [whole(one.shape) for one in (*grads, *x)]
        + [
            rows(qkv.shape[1]),
            rows(128),
            rows(128),
            pl.BlockSpec((1,) + segment.shape[1:], lambda s: (tile_at(s), 0, 0)),
            whole(wqkv.shape),
            whole(wo.shape),
        ],
        [rows(qkv.shape[1]), pl.BlockSpec((1, width), lambda s: (0, 0))] + half_specs,
        [jax.ShapeDtypeStruct(qkv.shape, BF16), jax.ShapeDtypeStruct((1, width), F32)]
        + half_shapes,
        [pltpu.VMEM((tile, width), BF16)] * 2,
    )(*grads, *x, qkv, cosine, sine, segment, wqkv, wo)


def units_kernel(*refs):
    inner_ref, dgate_ref, dup_ref, gate_ref, up_ref, h_ref = refs[12:]
    step = pl.program_id(0)
    pick(step, refs[:4], h_ref)

    @pl.when(step == 0)
    def _():
        assemble(refs[4:8], gate_ref, "a", gate_ref.shape[0] // 8)
        assemble(refs[8:12], up_ref, "b", up_ref.shape[0] // 8)

    gate = dot(h_ref[...], gate_ref[...], NT)
    up = dot(h_ref[...], up_ref[...], NT)
    sigmoid = 1.0 / (1.0 + jnp.exp(-gate))
    silu = gate * sigmoid
    inner_ref[...] = (silu * up).astype(BF16)
    dup_ref[...] = silu.astype(BF16)
    dgate_ref[...] = (up * (sigmoid * (1.0 + gate * (1.0 - sigmoid)))).astype(BF16)


def units(hidden, gate_parts, up_parts):
    tile, width = hidden[0].shape
    count = 4 * gate_parts[0].shape[0]
    rows = pl.BlockSpec((tile, count), lambda s: (s, 0))
    return call(
        units_kernel,
        "units",
        (4,),
        [whole(one.shape) for one in (*hidden, *gate_parts, *up_parts)],
        [rows] * 3,
        [jax.ShapeDtypeStruct((4 * tile, count), BF16)] * 3,
        [pltpu.VMEM((count, width), BF16)] * 2 + [pltpu.VMEM((tile, width), BF16)],
    )(*hidden, *gate_parts, *up_parts)


def unit_grads_kernel(first, *refs):
    dgate_ref, dup_ref = refs[4:6]
    gg_ref, gu_ref, down_ref, g_ref = refs[14:]
    step = pl.program_id(0)
    pick(step, refs[:4], g_ref)

    @pl.when(step == 0)
    def _():
        assemble_down(refs[6:14], down_ref, first)

    inner = dot(g_ref[...], down_ref[...], NT)
    gg_ref[...] = (inner * dgate_ref[...].astype(F32)).astype(BF16)
    gu_ref[...] = (inner * dup_ref[...].astype(F32)).astype(BF16)


def unit_grads(grads, down_parts, dgate, dup, first):
    tile, width = grads[0].shape
    count = dgate.shape[1]
    rows = pl.BlockSpec((tile, count), lambda s: (s, 0))
    return call(
        functools.partial(unit_grads_kernel, first),
        "unit_grads",
        (4,),
        [whole(one.shape) for one in grads]
        + [rows, rows]
        + [whole(one.shape) for one in down_parts],
        [rows] * 2,
        [jax.ShapeDtypeStruct((4 * tile, count), BF16)] * 2,
        [pltpu.VMEM((count, width), BF16), pltpu.VMEM((tile, width), BF16)],
    )(*grads, dgate, dup, *down_parts)


def sum_kernel(count, first, *refs):
    lefts, parts = refs[:count], refs[count : count + 8]
    *send_refs, keep_ref = refs[count + 8 : len(refs) - count]
    weights = refs[len(refs) - count :]
    rows = weights[0].shape[0] // 8
    if count == 1:
        assemble_down(parts, weights[0], first)
    else:
        assemble(parts[:4], weights[0], "a", rows)
        assemble(parts[4:], weights[1], "b", rows)
    total = dot(lefts[0][...], weights[0][...])
    for left, weight in zip(lefts[1:], weights[1:]):
        total = total + dot(left[...], weight[...])
    tile = keep_ref.shape[1]
    near, far = total[tile : 2 * tile].astype(BF16), total[3 * tile :].astype(BF16)
    keep_ref[0] = total[:tile].astype(BF16)
    keep_ref[1] = total[2 * tile : 3 * tile].astype(BF16)
    if len(send_refs) == 1:
        send_refs[0][0] = near
        send_refs[0][1] = far
    else:
        near_ref, zero_ref, one_ref = send_refs
        near_ref[...] = near
        zero_ref[...] = far[: tile // 2]
        one_ref[...] = far[tile // 2 :]


def sum_rows(lefts, parts, name, first=0):
    tokens, count = lefts[0].shape
    width = parts[0].shape[1]
    tile, columns = tokens // 4, width // SUM_STEPS
    both = (2, tile)
    sizes = [both, both] if len(lefts) == 1 else [(tile,), (tile // 2,), (tile // 2,), both]
    shape = jax.ShapeDtypeStruct

    def block(size):
        zeros = (0,) * len(size)
        return pl.BlockSpec((*size, columns), lambda s: (*zeros, s))

    return call(
        functools.partial(sum_kernel, len(lefts), first),
        name,
        (SUM_STEPS,),
        [whole(one.shape) for one in lefts]
        + [pl.BlockSpec((one.shape[0], columns), lambda s: (0, s)) for one in parts],
        [block(size) for size in sizes],
        [shape((*size, width), BF16) for size in sizes],
        [pltpu.VMEM((count, columns), BF16)] * len(lefts),
    )(*lefts, *parts)


def put_owners(place, a_keep, a_send, b_keep, b_send):
    step = pl.program_id(0)

    @pl.when(step < 2)
    def _():
        place(a_keep, (0, 1, 2, 3))
        place(a_send, (4, 5, 6, 7))

    @pl.when(step >= 2)
    def _():
        place(b_keep, (0, 1, 4, 5))
        place(b_send, (2, 3, 6, 7))


def owners_out(rows, width):
    half = lambda place: pl.BlockSpec((4, rows, width // 4), lambda s: (0, 0, place(s)))
    early, late = half(lambda s: jnp.minimum(s, 1)), half(lambda s: jnp.maximum(s - 2, 0))
    return [early, early, late, late], [jax.ShapeDtypeStruct((4, rows, width // 2), BF16)] * 4


def weight_grad_kernel(rows, l_ref, *refs):
    right = jnp.concatenate([ref[...] for ref in refs[:4]], 0)
    grads = dot(l_ref[...], right, TN).astype(BF16)

    def place(ref, owners):
        for at, one in enumerate(owners):
            ref[at] = grads[one * rows : (one + 1) * rows]

    put_owners(place, *refs[4:])


def weight_grad(left, right, name):
    tokens, count = left.shape
    tile, width = right[0].shape
    specs, shapes = owners_out(count // 8, width)
    return call(
        functools.partial(weight_grad_kernel, count // 8),
        name,
        (4,),
        [whole(left.shape)] + [pl.BlockSpec((tile, width // 4), lambda s: (0, s))] * 4,
        specs,
        shapes,
    )(left, *right)


def attn_grads_kernel(head_rows, kv_rows, gqkv_ref, hid_ref, mixed_ref, moved_ref, *refs):
    first = dot(gqkv_ref[...], hid_ref[...], TN).astype(BF16)
    right = jnp.concatenate([ref[...] for ref in refs[:8]], 0)
    second = dot(mixed_ref[...], right, TN).astype(BF16)
    width = 8 * head_rows
    placed = {}
    for which in range(2):
        for side in range(2):
            low = width + (2 * which + side) * HEAD_DIM
            placed[which, side] = dot(moved_ref[...], first[low : low + HEAD_DIM])

    def place(ref, owners):
        for at, one in enumerate(owners):
            mid, sub, side = one // 4, one // 2 % 2, one % 2
            lows = [(mid * 4 + core * 2 + sub) * kv_rows for core in range(2)]
            kv = [placed[which, side][low : low + kv_rows] for low in lows for which in range(2)]
            here = slice(one * head_rows, (one + 1) * head_rows)
            ref[at, :head_rows] = first[here]
            ref[at, head_rows : head_rows + 4 * kv_rows] = jnp.concatenate(kv, 0).astype(BF16)
            ref[at, head_rows + 4 * kv_rows :] = second[here]

    put_owners(place, *refs[8:])


def attn_grads(gqkv, hidden, mixed, right, moved, head_rows, kv_rows):
    tokens, width = hidden.shape
    columns = width // 4
    specs, shapes = owners_out(2 * head_rows + 4 * kv_rows, width)
    return call(
        functools.partial(attn_grads_kernel, head_rows, kv_rows),
        "attn_grads",
        (4,),
        [
            whole(gqkv.shape),
            pl.BlockSpec((tokens, columns), lambda s: (0, s)),
            whole(mixed.shape),
            whole(moved.shape),
        ]
        + [pl.BlockSpec((tokens // 8, columns), lambda s: (0, s))] * 8,
        specs,
        shapes,
    )(gqkv, hidden, mixed, moved, *right)


def total_kernel(ka_ref, ga_ref, kb_ref, gb_ref, ta_ref, tb_ref, *refs):
    *last_refs, out_ref = refs
    half = ka_ref.shape[2]
    last = jnp.concatenate([ref[...].astype(F32) for ref in last_refs], 1)
    a, b = (
        keep[0].astype(F32) + got[0].astype(F32) + two[0].astype(F32)
        for keep, got, two in ((ka_ref, ga_ref, ta_ref), (kb_ref, gb_ref, tb_ref))
    )
    out_ref[:, :half] = a + last[:, :half]
    out_ref[:, half:] = b + last[:, half:]


def total_sum(pairs):
    _, rows, half = pairs[0].shape
    block = pl.BlockSpec((1, rows, half), lambda s: (0, 0, 0))
    return call(
        total_kernel,
        "total",
        (1,),
        [block] * 6 + [whole(one.shape) for one in pairs[6:]],
        pl.BlockSpec((rows, 2 * half), lambda s: (0, 0)),
        jax.ShapeDtypeStruct((rows, 2 * half), F32),
    )(*pairs)


def finish_kernel(x_ref, gain_ref, mid0_ref, mid1_ref, keep_ref, near_ref, zero_ref, one_ref,
                  resid_ref, okeep_ref, ogot_ref, ozero_ref, oone_ref, grad_ref, out_ref):
    rows = zero_ref.shape[0]
    for at, far_ref, mid_ref, ofar_ref in (
        (0, zero_ref, mid0_ref, ozero_ref),
        (1, one_ref, mid1_ref, oone_ref),
    ):
        here = slice(at * rows, (at + 1) * rows)
        x = x_ref[here].astype(F32)
        inverse = lax.rsqrt(jnp.mean(x * x, -1, keepdims=True) + EPS)
        grad = keep_ref[0, here].astype(F32) + near_ref[here].astype(F32)
        grad = grad + far_ref[...].astype(F32)
        grad = mid_ref[...] + norm_backward(grad, x * inverse, inverse, gain_ref[...])
        grad_ref[here] = grad.astype(BF16)
        out = okeep_ref[0, here].astype(F32) + ogot_ref[0, here].astype(F32)
        out_ref[here] = (resid_ref[here] + (out + ofar_ref[...].astype(F32))).astype(BF16)


def finish(x, gain, mid0, mid1, keep, near, zero, one, resid, out_keep, out_got, out_far):
    tile, width = x.shape
    first = pl.BlockSpec((1, tile, width), lambda s: (0, 0, 0))
    full = lambda array: whole(array.shape)
    return call(
        finish_kernel,
        "finish",
        (1,),
        [full(x), full(gain), full(mid0), full(mid1), first, full(near), full(zero), full(one)]
        + [full(resid), first, first, *map(full, out_far)],
        [pl.BlockSpec((tile, width), lambda s: (0, 0))] * 2,
        [jax.ShapeDtypeStruct((tile, width), BF16)] * 2,
    )(x, gain, mid0, mid1, keep, near, zero, one, resid, out_keep, out_got, *out_far)


def norm_forward(values, gain):
    inverse = lax.rsqrt(jnp.mean(values * values, -1, keepdims=True) + EPS)
    normed = values * inverse
    return (normed, inverse, (normed * gain).astype(BF16))


def norm_backward(grad_hidden, normed, inverse, gain):
    grad_normed = grad_hidden * gain
    return inverse * (grad_normed - normed * jnp.mean(grad_normed * normed, -1, keepdims=True))


def swap(value, axis):
    return lax.ppermute(value, axis, [(0, 1), (1, 0)])


def up32(value):
    return value.astype(F32)


def join(*values):
    return jnp.concatenate(values, 0)


class Live:
    def cut(self):
        names = sorted(vars(self))
        values = lax.optimization_barrier(tuple(getattr(self, name) for name in names))
        for name, value in zip(names, values):
            setattr(self, name, value)

    @property
    def pop(self):
        return Pop(self)


class Pop:
    def __init__(self, live):
        self.live = live

    def __getattr__(self, name):
        value = getattr(self.live, name)
        delattr(self.live, name)
        return value


def tables(lengths_all, row_count):
    seq_ends = jnp.cumsum(lengths_all, 1)
    token = jnp.arange(row_count, dtype=jnp.int32)
    passed = (token[None, :, None] >= seq_ends[:, None, :]).astype(jnp.int32)
    segment = jnp.sum(passed, 2)
    offsets = token[None, :] - jnp.sum(passed * lengths_all[:, None, :], 2)
    half = HEAD_DIM // 2
    lane = jnp.arange(128, dtype=jnp.int32)
    frequency = ROPE_BASE ** (-(lane % half).astype(F32) * 2.0 / HEAD_DIM)
    angles = offsets.reshape(-1, 1).astype(F32) * frequency[None, :]
    sign = jnp.where(lane % HEAD_DIM < half, -1.0, 1.0)
    return (segment.astype(F32), jnp.cos(angles), jnp.sin(angles) * sign[None, :])


def on_device_small(
    block_input,
    out_grad,
    seq_lengths,
    attn_gain,
    w_query,
    w_key,
    w_value,
    w_output,
    mlp_gain,
    w_gate,
    w_up,
    w_down,
):
    width = block_input.shape[2]
    row_count = block_input.shape[1]
    micro = block_input.shape[0]
    tokens = micro * row_count
    head_rows = w_query.shape[0]
    kv_rows = w_key.shape[0]
    gain_width = attn_gain.shape[0]
    packed = seq_lengths.shape[2]
    units_own = w_gate.shape[0]
    first = -(-units_own // 2 // 32) * 32
    second = units_own - first
    qkv_rows = head_rows + 2 * kv_rows
    place = {name: lax.axis_index(name) for name in AXES}
    place8 = place[MID] * 4 + place[CORE] * 2 + place[SUB]
    place32 = place[ZH] * 16 + place[ZL] * 8 + place8
    index = jnp.arange(8 * kv_rows, dtype=jnp.int32)
    block, inside = index // kv_rows, index % kv_rows
    moved = (block[:, None] == (block[None, :] ^ place8)) & (inside[:, None] == inside[None, :])
    moved = moved.astype(BF16)
    index = jnp.arange(32, dtype=jnp.int32)
    ordered = (index[:, None] == (index[None, :] ^ place32)).astype(BF16)

    def pair_sum(keep, got, at):
        return up32(keep[at]) + up32(got[at])

    v = Live()
    own_x = block_input.reshape(tokens, width)
    v.own_g = out_grad.reshape(tokens, width)

    pack = join(attn_gain, mlp_gain, seq_lengths.reshape(micro * packed).astype(BF16))
    v.pack = jnp.pad(pack.reshape(1, -1), ((0, 0), (0, 256 - pack.shape[0])))
    v.pack_far = swap(v.pack, ZL)
    v.a0 = join(w_query, w_key, w_value)
    a_rows = v.a0.shape[0]
    v.w_gate, v.w_up, v.w_down, v.w_output = w_gate, w_up, w_down, w_output
    v.got_x = swap(join(v.a0, w_gate), SUB)
    v.got_y = swap(join(w_output, w_up), MID)
    v.ao = swap(join(v.a0, w_output), ZH)
    v.own_x = own_x
    v.x_far = swap(v.own_x, ZL)
    v.cut()

    v.g0x, v.u0y = v.got_x[a_rows:], v.got_y[head_rows:]
    v.a1, v.o1 = v.ao[:a_rows], v.ao[a_rows:]
    v.o0s = join(v.pop.w_output, v.got_y[:head_rows], v.a1)
    v.a0s = join(v.pop.a0, v.got_x[:a_rows], v.o1)
    v.o0t, v.a0t = swap(v.o0s, SUB), swap(v.a0s, MID)
    packs = jnp.concatenate([v.pop.pack, v.pop.pack_far], 1)
    packs = jnp.concatenate([packs, swap(packs, CORE)], 1)
    v.packs = jnp.pad(packs, ((0, 15), (0, width - packs.shape[1])))
    v.gate_low = swap(join(v.w_gate[:second], v.packs), ZH)
    v.x_core, v.x_far_core = swap(v.own_x, CORE), swap(v.x_far, CORE)
    del v.ao, v.got_x, v.got_y
    v.cut()

    packs = jnp.concatenate([v.packs[:, :1024], v.gate_low[second:, :1024]], 1)
    v.o1s = join(v.pop.o1, v.a0t[2 * a_rows :], packs)
    v.a1s = join(v.pop.a1, v.o0t[2 * head_rows :], packs)
    v.o1t, v.a1t = swap(v.o1s, SUB), swap(v.a1s, MID)
    v.gate_high = swap(v.w_gate[second:], ZH)
    v.packs_near = packs[:1]
    v.packs_across = lax.ppermute(packs[:1], (MID, SUB), [(at, 3 - at) for at in range(4)])
    lengths = v.pop.packs[0, :1024].reshape(2, 2, 256)
    lengths = lengths[:, :, 2 * gain_width : 2 * gain_width + micro * packed]
    lengths_all = lengths.transpose(1, 0, 2).reshape(4 * micro, packed).astype(jnp.int32)
    segment, v.cosine, v.sine = tables(lengths_all, row_count)
    v.segment = segment.reshape(4, micro, row_count)
    v.x = (v.own_x, v.pop.x_core, v.pop.x_far, v.pop.x_far_core)
    v.cut()

    v.u0s, v.g0s = join(v.w_up, v.pop.u0y), join(v.w_gate, v.pop.g0x)
    v.u0t, v.g0t = swap(v.u0s, SUB), swap(v.g0s, MID)
    v.u1 = swap(v.w_up, ZH)
    a_parts = (v.pop.a0s, v.pop.a0t, v.pop.a1s, v.pop.a1t)
    o_parts = (v.pop.o0s, v.pop.o0t, v.pop.o1s, v.pop.o1t)
    kv_own = join(
        *(one[: 2 * a_rows].reshape(2, a_rows, width)[:, head_rows:] for one in a_parts)
    )
    kv_core = swap(kv_own, CORE)
    packs = join(
        v.pop.packs_near, o_parts[3][-16:-15], a_parts[3][-16:-15], v.pop.packs_across
    )
    gains_rel = packs.reshape(2, 2, 2, 2, 2, 256)[..., : 2 * gain_width]
    gains_rel = gains_rel.transpose(2, 4, 0, 3, 1, 5)
    gains_all = dot(ordered, gains_rel.reshape(32, 2 * gain_width))
    v.gain_one = gains_all[:, :gain_width].reshape(1, width)
    v.gain_two = gains_all[:, gain_width:].reshape(1, width)
    attn = attn_forward(
        v.x,
        v.gain_one,
        v.cosine,
        v.sine,
        v.segment,
        moved,
        kv_own,
        kv_core,
        a_parts,
        o_parts,
        head_rows,
        row_count,
    )
    v.hidden_one, v.qkv, v.mixed, v.part_send, v.part_keep, v.wqkv, v.full_o = attn
    v.cut()

    v.g1 = join(v.gate_low[:second], v.pop.gate_high)
    del v.gate_low
    v.got_x = swap(join(v.g1, v.w_down[:first]), SUB)
    v.got_y = swap(join(v.u1, v.w_down[first:]), MID)
    v.da1 = swap(v.w_down[:first], ZH)
    v.part_got = swap(v.pop.part_send, CORE)
    mid_far = pair_sum(v.part_keep, v.part_got, 1).astype(BF16)
    v.mid_far = swap(mid_far, ZL)
    v.cut()

    v.dax, v.dby = v.got_x[units_own:], v.got_y[units_own:]
    v.g1s, v.u1s = join(v.pop.g1, v.got_x[:units_own]), join(v.pop.u1, v.got_y[:units_own])
    v.g1t, v.u1t = swap(v.g1s, MID), swap(v.u1s, SUB)
    v.resid_mid = up32(v.own_x) + (
        pair_sum(v.pop.part_keep, v.pop.part_got, 0) + up32(v.pop.mid_far)
    )
    v.db1 = swap(v.w_down[first:], ZH)
    h_own = norm_forward(v.resid_mid, v.gain_two)[2]
    v.h_far, v.h_core = swap(h_own, ZL), swap(h_own, CORE)
    v.h_own = h_own
    del v.got_x, v.got_y
    v.cut()

    v.db0s = join(v.w_down[first:], v.pop.dby, v.da1)
    v.da0s = join(v.w_down[:first], v.pop.dax, v.db1)
    v.db0t, v.da0t = swap(v.db0s, SUB), swap(v.da0s, MID)
    v.g_far, v.g_core = swap(v.own_g, ZL), swap(v.own_g, CORE)
    v.h = (v.pop.h_own, v.pop.h_core, v.h_far, swap(v.h_far, CORE))
    del v.w_gate, v.w_up, v.w_down, v.h_far
    v.gate_parts = (v.pop.g0s, v.pop.g0t, v.pop.g1s, v.pop.g1t)
    v.up_parts = (v.pop.u0s, v.pop.u0t, v.pop.u1s, v.pop.u1t)
    v.inner, v.dgate, v.dup = units(v.h, v.gate_parts, v.up_parts)
    v.cut()

    v.da1s = join(v.pop.da1, v.db0t[2 * second :])
    v.db1s = join(v.pop.db1, v.da0t[2 * first :])
    v.da1t, v.db1t = swap(v.da1s, MID), swap(v.db1s, SUB)
    v.g = (v.own_g, v.pop.g_core, v.g_far, swap(v.g_far, CORE))
    del v.g_far
    v.dg = weight_grad(v.inner, v.g, "down_grad")
    v.cut()

    def step_one(grads):
        keep_a, send_a, keep_b, send_b = grads
        return (keep_a, swap(send_a, MID), keep_b, swap(send_b, SUB))

    def sums_one(pairs):
        keep_a, got_a, keep_b, got_b = pairs
        far = slice(2, 4)
        return pairs + (
            pair_sum(keep_a, got_a, far).astype(BF16),
            pair_sum(keep_b, got_b, far).astype(BF16),
        )

    def step_two(pairs):
        return pairs[:4] + (swap(pairs[4], SUB), swap(pairs[5], MID))

    def part_sum(pairs, at, low, high):
        half = pairs[0].shape[2]
        sums = []
        for side in range(2):
            here = slice(max(low - side * half, 0), min(high - side * half, half))
            if here.start < here.stop:
                keep, got, two = pairs[2 * side], pairs[2 * side + 1], pairs[4 + side]
                sums.append(up32(keep[at, :, here]) + up32(got[at, :, here]) + up32(two[at, :, here]))
        return sums[0] if len(sums) == 1 else jnp.concatenate(sums, 1)

    def last_send(pairs, low, high):
        return part_sum(pairs, 1, low, high).astype(BF16)

    def step_three(pairs, send):
        return pairs + (swap(send, ZH),)

    def total(pairs):
        last = jnp.concatenate([up32(one) for one in pairs[6:]], 1)
        return part_sum(pairs, 0, 0, width) + last

    even, early, most = width // 2, width * 5 // 8, width * 3 // 4

    def gain_step(name):
        at = 1 + AXES.index(name)
        low, high = jnp.split(v.gain_grads, 2, at)
        mine = jnp.where(place[name] == 0, low, high)
        sent = jnp.where(place[name] == 0, high, low)
        v.gain_grads = mine + swap(sent, name)

    def far_of(keep, got, micro_at):
        here = slice(micro_at * row_count, (micro_at + 1) * row_count)
        return (up32(keep[1, here]) + up32(got)).astype(BF16)

    def mid_grads(micro_at, far):
        here = slice(micro_at * row_count, (micro_at + 1) * row_count)
        gh2 = up32(v.gh2_keep[0, here]) + up32(v.gh2_near[here]) + up32(far)
        resid = v.resid_mid[here]
        inverse = lax.rsqrt(jnp.mean(resid * resid, -1, keepdims=True) + EPS)
        normed = resid * inverse
        grad_mid = up32(v.own_g[here]) + norm_backward(gh2, normed, inverse, v.gain_two)
        return grad_mid, grad_mid.astype(BF16), jnp.sum(gh2 * normed, 0, keepdims=True)

    v.dg = step_one(v.dg)
    v.down_parts = (
        *(v.pop.da0s, v.pop.da0t, v.pop.da1s, v.pop.da1t),
        *(v.pop.db0s, v.pop.db0t, v.pop.db1s, v.pop.db1t),
    )
    v.gg, v.gu = unit_grads(v.pop.g, v.down_parts, v.pop.dgate, v.pop.dup, first)
    *send, v.gh2_keep = sum_rows(
        (v.gg, v.gu), (*v.pop.gate_parts, *v.pop.up_parts), "hidden_grads"
    )
    v.gh2_near = send[0]
    v.gh2_far = (swap(send[1], CORE), swap(send[2], CORE))
    v.cut()
    v.dg = sums_one(v.dg)
    v.cut()

    v.dg = step_two(v.dg)
    v.gh2_zero = swap(far_of(v.gh2_keep, v.gh2_far[0], 0), ZL)
    v.gh2_near = swap(v.gh2_near, CORE)
    v.gh2_one = far_of(v.gh2_keep, v.gh2_far[1], 1)
    v.gw = weight_grad(v.pop.gg, v.h, "gate_grad")
    v.cut()

    v.gw = step_one(v.gw)
    v.gh2_one = swap(v.gh2_one, ZL)
    v.grad_mid0, v.gb0, v.mlp_terms = mid_grads(0, v.pop.gh2_zero)
    v.gb0_far = swap(v.gb0, ZL)
    v.dg_send = last_send(v.dg, early, width)
    v.dg = step_three(v.dg, last_send(v.dg, 0, early))
    v.out_send, v.out_keep = sum_rows((v.pop.inner,), v.pop.down_parts, "block_out", first)
    v.cut()

    v.grad_mid1, v.gb1, terms = mid_grads(1, v.pop.gh2_one)
    v.mlp_terms = v.mlp_terms + terms
    v.gb1_far = swap(v.gb1, ZL)
    del v.gh2_keep, v.gh2_near, v.gh2_far
    v.gw = step_two(sums_one(v.gw))
    v.dg = step_three(v.dg, v.pop.dg_send)
    v.out_got = swap(v.pop.out_send, CORE)
    v.uw = weight_grad(v.pop.gu, v.pop.h, "up_grad")
    v.cut()

    v.uw = step_one(v.uw)
    v.gw_send = last_send(v.gw, most, width)
    v.gw = step_three(v.gw, last_send(v.gw, 0, most))
    v.out_zero = far_of(v.out_keep, v.out_got[1, :row_count], 0)
    v.out_zero = swap(v.out_zero, ZL)
    gb = (v.pop.gb0, v.pop.gb1), (v.pop.gb0_far, v.pop.gb1_far)
    v.gb = tuple(
        one for rows in gb for one in (*rows, *(swap(piece, CORE) for piece in rows))
    )
    v.gqkv, attn_terms, *send, v.gh1_keep = attn_backward(
        v.gb,
        v.pop.x,
        v.pop.qkv,
        v.pop.cosine,
        v.pop.sine,
        v.pop.segment,
        v.pop.wqkv,
        v.pop.full_o,
        row_count,
    )
    v.gh1_near = send[0]
    v.gh1_far = (swap(send[1], CORE), swap(send[2], CORE))
    gain_grads = join(attn_terms, v.pop.mlp_terms)
    v.gain_grads = gain_grads.reshape(2, 2, 2, 2, 2, 2, gain_width)
    v.cut()
    v.uw = sums_one(v.uw)
    v.cut()

    v.uw = step_two(v.uw)
    v.gh1_zero = swap(far_of(v.gh1_keep, v.gh1_far[0], 0), ZL)
    v.gh1_near = swap(v.gh1_near, CORE)
    v.gw = step_three(v.gw, v.pop.gw_send)
    v.aw = attn_grads(
        v.pop.gqkv, v.pop.hidden_one, v.pop.mixed, v.pop.gb, moved, head_rows, kv_rows
    )
    v.gh1_one = far_of(v.gh1_keep, v.gh1_far[1], 1)
    v.out_one = far_of(v.out_keep, v.out_got[1, row_count:], 1)
    v.cut()

    v.aw = step_one(v.aw)
    v.gh1_one = swap(v.gh1_one, ZL)
    v.uw_send = last_send(v.uw, early, width)
    v.uw = step_three(v.uw, last_send(v.uw, 0, early))
    v.cut()
    v.aw = sums_one(v.aw)
    v.cut()

    v.aw = step_two(v.aw)
    v.uw = step_three(v.uw, v.pop.uw_send)
    v.out_one = swap(v.out_one, ZL)
    gain_step(ZH)
    v.cut()

    aw = step_three(v.aw, last_send(v.aw, 0, even))
    aw = step_three(aw, last_send(v.aw, even, width))
    gain_step(MID)
    gain_step(SUB)
    gain_step(CORE)
    gain_step(ZL)
    input_grad, block_out = finish(
        v.own_x,
        v.gain_one,
        v.pop.grad_mid0,
        v.pop.grad_mid1,
        v.pop.gh1_keep,
        v.pop.gh1_near,
        v.pop.gh1_zero,
        v.pop.gh1_one,
        v.pop.resid_mid,
        v.pop.out_keep,
        v.pop.out_got,
        (v.pop.out_zero, v.pop.out_one),
    )
    down_grad, gate_grad, up_grad = (
        total_sum(v.pop.dg), total_sum(v.pop.gw), total_sum(v.pop.uw)
    )
    grads = total(aw)
    kv_grads = grads[head_rows:qkv_rows] + swap(grads[qkv_rows : qkv_rows + 2 * kv_rows], CORE)
    return (
        block_out.reshape(block_input.shape),
        input_grad.reshape(block_input.shape),
        v.gain_grads[0].reshape(gain_width),
        grads[:head_rows],
        kv_grads[:kv_rows],
        kv_grads[kv_rows:],
        grads[qkv_rows + 2 * kv_rows :],
        v.gain_grads[1].reshape(gain_width),
        gate_grad,
        up_grad,
        down_grad,
    )


def positions(lengths_row, row_count):
    seq_ends = jnp.cumsum(lengths_row)
    starts = seq_ends - lengths_row
    token_index = jnp.arange(row_count, dtype=jnp.int32)
    segment = jnp.sum((token_index[:, None] >= seq_ends[None, :]).astype(jnp.int32), 1)
    chosen = segment[:, None] == jnp.arange(lengths_row.shape[0], dtype=jnp.int32)[None, :]
    offsets = token_index - jnp.sum(jnp.where(chosen, starts[None, :], 0), 1)
    allowed = (segment[:, None] == segment[None, :]) & (
        token_index[None, :] <= token_index[:, None]
    )
    return (offsets, allowed)


def rotary_tables(offsets, width):
    half_width = width // 2
    frequency = ROPE_BASE ** (-jnp.arange(half_width, dtype=jnp.float32) * 2.0 / width)
    angles = offsets.astype(jnp.float32)[:, None] * frequency[None, :]
    return (jnp.cos(angles)[:, None, :], jnp.sin(angles)[:, None, :])


def rotate(values, cosine, sine_table):
    half_width = values.shape[-1] // 2
    first_half = values[..., :half_width]
    second_half = values[..., half_width:]
    return jnp.concatenate(
        [
            first_half * cosine - second_half * sine_table,
            second_half * cosine + first_half * sine_table,
        ],
        -1,
    )


def rotate_back(grads, cosine, sine_table):
    half_width = grads.shape[-1] // 2
    upper_half = grads[..., :half_width]
    lower_half = grads[..., half_width:]
    return jnp.concatenate(
        [
            upper_half * cosine + lower_half * sine_table,
            lower_half * cosine - upper_half * sine_table,
        ],
        -1,
    )


def project(activity, weight):
    return lax.dot_general(
        activity, weight, (((1,), (1,)), ((), ())), preferred_element_type=jnp.float32
    )


def apply_rows(activity, weight):
    return jnp.dot(activity, weight, preferred_element_type=jnp.float32)


def general_norm_forward(values, gain_row):
    inverse = lax.rsqrt(jnp.mean(values * values, -1, keepdims=True) + EPS)
    normed = values * inverse
    return (normed, inverse, (normed * gain_row.astype(jnp.float32)).astype(jnp.bfloat16))


def general_norm_backward(grad_hidden, normed, inverse, gain_row):
    grad_normed = grad_hidden * gain_row.astype(jnp.float32)
    return inverse * (grad_normed - normed * jnp.mean(grad_normed * normed, -1, keepdims=True))


def attention_scores(query_rot, key_rot, allowed):
    scores = jnp.einsum(
        "qhgd,khd->hgqk", query_rot, key_rot, preferred_element_type=jnp.float32
    ) * HEAD_DIM ** (-0.5)
    return jnp.where(allowed, scores, NEG_LARGE)


def forward_pass(block_rows, lengths_row, gathered):
    attn_gain, w_query, w_key, w_value, w_output, mlp_gain, w_gate, w_up, w_down = gathered
    row_count = block_rows.shape[0]
    query_heads = w_query.shape[0] // HEAD_DIM
    key_heads = w_key.shape[0] // HEAD_DIM
    group_size = query_heads // key_heads
    offsets, allowed = positions(lengths_row, row_count)
    cosine, sine_table = rotary_tables(offsets, HEAD_DIM)
    resid_in = block_rows.astype(jnp.float32)
    normed_one, inverse_one, hidden_one = general_norm_forward(resid_in, attn_gain)
    query_lin = project(hidden_one, w_query).reshape(row_count, query_heads, HEAD_DIM)
    key_lin = project(hidden_one, w_key).reshape(row_count, key_heads, HEAD_DIM)
    value_rows = (
        project(hidden_one, w_value).astype(jnp.bfloat16).reshape(row_count, key_heads, HEAD_DIM)
    )
    query_rot = (
        rotate(query_lin, cosine, sine_table)
        .astype(jnp.bfloat16)
        .reshape(row_count, key_heads, group_size, HEAD_DIM)
    )
    key_rot = rotate(key_lin, cosine, sine_table).astype(jnp.bfloat16)
    scores = attention_scores(query_rot, key_rot, allowed)
    top_score = jnp.max(scores, -1, keepdims=True)
    exp_scores = jnp.exp(scores - top_score)
    row_total = jnp.sum(exp_scores, -1, keepdims=True)
    prob_low = (exp_scores / row_total).astype(jnp.bfloat16)
    log_total = top_score + jnp.log(row_total)
    mixed = jnp.einsum("hgqk,khd->qhgd", prob_low, value_rows, preferred_element_type=jnp.float32)
    mixed = mixed.astype(jnp.bfloat16).reshape(row_count, query_heads * HEAD_DIM)
    resid_mid = resid_in + apply_rows(mixed, w_output)
    normed_two, inverse_two, hidden_two = general_norm_forward(resid_mid, mlp_gain)
    gate_rows = project(hidden_two, w_gate)
    up_rows = project(hidden_two, w_up)
    inner = (jax.nn.silu(gate_rows) * up_rows).astype(jnp.bfloat16)
    block_out = (resid_mid + apply_rows(inner, w_down)).astype(jnp.bfloat16)
    saved = (
        allowed,
        cosine,
        sine_table,
        normed_one,
        inverse_one,
        hidden_one,
        value_rows,
        query_rot,
        key_rot,
        log_total,
        mixed,
        normed_two,
        inverse_two,
        hidden_two,
        gate_rows,
        up_rows,
        inner,
    )
    return (block_out, saved)


def backward_pass(grad_rows, saved, gathered):
    attn_gain, w_query, w_key, w_value, w_output, mlp_gain, w_gate, w_up, w_down = gathered
    (
        allowed,
        cosine,
        sine_table,
        normed_one,
        inverse_one,
        hidden_one,
        value_rows,
        query_rot,
        key_rot,
        log_total,
        mixed,
        normed_two,
        inverse_two,
        hidden_two,
        gate_rows,
        up_rows,
        inner,
    ) = saved
    row_count = grad_rows.shape[0]
    grad_out = grad_rows.astype(jnp.float32)
    grad_inner = project(grad_rows, w_down)
    sigmoid_gate = jax.nn.sigmoid(gate_rows)
    silu_gate = gate_rows * sigmoid_gate
    grad_gate = (
        grad_inner * up_rows * sigmoid_gate * (1.0 + gate_rows * (1.0 - sigmoid_gate))
    ).astype(jnp.bfloat16)
    grad_up = (grad_inner * silu_gate).astype(jnp.bfloat16)
    grad_hidden_two = apply_rows(grad_gate, w_gate) + apply_rows(grad_up, w_up)
    grad_mid = grad_out + general_norm_backward(grad_hidden_two, normed_two, inverse_two, mlp_gain)
    grad_branch = grad_mid.astype(jnp.bfloat16)
    grad_mixed = project(grad_branch, w_output).astype(jnp.bfloat16).reshape(query_rot.shape)
    scores = attention_scores(query_rot, key_rot, allowed)
    attn_probs = jnp.exp(scores - log_total)
    prob_low = attn_probs.astype(jnp.bfloat16)
    grad_probs = jnp.einsum(
        "qhgd,khd->hgqk", grad_mixed, value_rows, preferred_element_type=jnp.float32
    )
    grad_scores = attn_probs * (grad_probs - jnp.sum(grad_probs * attn_probs, -1, keepdims=True))
    grad_scores = grad_scores.astype(jnp.bfloat16)
    grad_value = jnp.einsum(
        "hgqk,qhgd->khd", prob_low, grad_mixed, preferred_element_type=jnp.float32
    )
    grad_value = grad_value.astype(jnp.bfloat16).reshape(row_count, -1)
    score_scale = HEAD_DIM ** (-0.5)
    grad_qrot = (
        jnp.einsum("hgqk,khd->qhgd", grad_scores, key_rot, preferred_element_type=jnp.float32)
        * score_scale
    )
    grad_krot = (
        jnp.einsum("hgqk,qhgd->khd", grad_scores, query_rot, preferred_element_type=jnp.float32)
        * score_scale
    )
    grad_query = rotate_back(grad_qrot.reshape(row_count, -1, HEAD_DIM), cosine, sine_table)
    grad_query = grad_query.astype(jnp.bfloat16).reshape(row_count, -1)
    grad_key = (
        rotate_back(grad_krot, cosine, sine_table).astype(jnp.bfloat16).reshape(row_count, -1)
    )
    grad_hidden_one = (
        apply_rows(grad_query, w_query)
        + apply_rows(grad_key, w_key)
        + apply_rows(grad_value, w_value)
    )
    grad_input = (
        grad_mid + general_norm_backward(grad_hidden_one, normed_one, inverse_one, attn_gain)
    ).astype(jnp.bfloat16)
    gain_terms = jnp.stack(
        [jnp.sum(grad_hidden_one * normed_one, 0), jnp.sum(grad_hidden_two * normed_two, 0)]
    )
    stored = (
        grad_query,
        hidden_one,
        grad_key,
        grad_value,
        mixed,
        grad_branch,
        grad_gate,
        hidden_two,
        grad_up,
        inner,
        grad_rows,
    )
    return (grad_input, stored, gain_terms)


def slice_term(left_rows, right_rows, owner, width):
    piece = lax.dynamic_slice_in_dim(left_rows, owner * width, width, 1)
    return lax.dot_general(
        piece, right_rows, (((0,), (0,)), ((), ())), preferred_element_type=jnp.float32
    )


def on_device_general(
    block_input,
    out_grad,
    seq_lengths,
    attn_gain,
    w_query,
    w_key,
    w_value,
    w_output,
    mlp_gain,
    w_gate,
    w_up,
    w_down,
):
    block_outs = []
    grad_inputs = []
    collected = [[] for member in range(11)]
    gain_total = jnp.zeros((2, block_input.shape[2]), jnp.float32)
    for batch_index in range(block_input.shape[0]):
        forward_layer = (
            lax.all_gather(attn_gain, DEVICES, axis=0, tiled=True),
            lax.all_gather(w_query, DEVICES, axis=0, tiled=True),
            lax.all_gather(w_key, DEVICES, axis=0, tiled=True),
            lax.all_gather(w_value, DEVICES, axis=0, tiled=True),
            lax.all_gather(w_output, DEVICES, axis=0, tiled=True),
            lax.all_gather(mlp_gain, DEVICES, axis=0, tiled=True),
            lax.all_gather(w_gate, DEVICES, axis=0, tiled=True),
            lax.all_gather(w_up, DEVICES, axis=0, tiled=True),
            lax.all_gather(w_down, DEVICES, axis=0, tiled=True),
        )
        block_out, saved = forward_pass(
            block_input[batch_index], seq_lengths[batch_index, 0], forward_layer
        )
        backward_layer = (
            lax.all_gather(attn_gain, DEVICES, axis=0, tiled=True),
            lax.all_gather(w_query, DEVICES, axis=0, tiled=True),
            lax.all_gather(w_key, DEVICES, axis=0, tiled=True),
            lax.all_gather(w_value, DEVICES, axis=0, tiled=True),
            lax.all_gather(w_output, DEVICES, axis=0, tiled=True),
            lax.all_gather(mlp_gain, DEVICES, axis=0, tiled=True),
            lax.all_gather(w_gate, DEVICES, axis=0, tiled=True),
            lax.all_gather(w_up, DEVICES, axis=0, tiled=True),
            lax.all_gather(w_down, DEVICES, axis=0, tiled=True),
        )
        grad_input, stored, gain_terms = backward_pass(out_grad[batch_index], saved, backward_layer)
        block_outs.append(block_out)
        grad_inputs.append(grad_input)
        gain_total = gain_total + gain_terms
        for member in range(11):
            collected[member].append(stored[member])
    joined = [jnp.concatenate(member_list, 0) for member_list in collected]
    model_width = block_input.shape[2]
    query_width = w_query.shape[0]
    key_width = w_key.shape[0]
    hidden_width = w_gate.shape[0]
    gain_width = attn_gain.shape[0]
    own_rows = 2 * query_width + 2 * key_width + 3 * hidden_width + 1
    filler = jnp.zeros((model_width - 2 * gain_width,), jnp.float32)

    def owner_block(owner):
        gain_row = jnp.concatenate(
            [
                lax.dynamic_slice_in_dim(gain_total[0], owner * gain_width, gain_width, 0),
                lax.dynamic_slice_in_dim(gain_total[1], owner * gain_width, gain_width, 0),
                filler,
            ],
            0,
        )
        return jnp.concatenate(
            [
                slice_term(joined[0], joined[1], owner, query_width),
                slice_term(joined[2], joined[1], owner, key_width),
                slice_term(joined[3], joined[1], owner, key_width),
                slice_term(joined[4], joined[5], owner, query_width),
                slice_term(joined[6], joined[7], owner, hidden_width),
                slice_term(joined[8], joined[7], owner, hidden_width),
                slice_term(joined[9], joined[10], owner, hidden_width),
                gain_row[None, :],
            ],
            0,
        )

    owner_count = own_rows * lax.axis_size(DEVICES) // own_rows
    owners = jnp.arange(owner_count, dtype=jnp.int32)
    blocks = lax.map(owner_block, owners)
    owned = lax.psum_scatter(
        blocks.reshape(owner_count * own_rows, model_width),
        DEVICES,
        scatter_dimension=0,
        tiled=True,
    )
    cuts = [
        query_width,
        key_width,
        key_width,
        query_width,
        hidden_width,
        hidden_width,
        hidden_width,
    ]
    pieces = []
    offset = 0
    for width in cuts:
        pieces.append(owned[offset : offset + width])
        offset = offset + width
    gain_row = owned[offset]
    return (
        jnp.stack(block_outs),
        jnp.stack(grad_inputs),
        gain_row[:gain_width],
        pieces[0],
        pieces[1],
        pieces[2],
        pieces[3],
        gain_row[gain_width : 2 * gain_width],
        pieces[4],
        pieces[5],
        pieces[6],
    )


def solution(mesh):
    groups, sub = mesh.shape["dp"], mesh.shape["sub"]
    rows, weight, gain = P(None, DEVICES, None), P(DEVICES, None), P(DEVICES)
    body = on_device_general
    if groups == 16 and sub == 2:
        mesh = Mesh(mesh.devices.reshape(2, 2, groups // 8, 2, sub), AXES)
        rows, weight, gain = P(None, AXES, None), P(AXES, None), P(AXES)
        body = on_device_small
    return jax.shard_map(
        body,
        mesh=mesh,
        in_specs=(rows, rows, rows, gain) + (weight,) * 4 + (gain,) + (weight,) * 3,
        out_specs=(rows, rows, gain) + (weight,) * 4 + (gain,) + (weight,) * 3,
        check_vma=False,
    )
```

```python
import functools
import jax
import jax.numpy as jnp
from jax import lax
from jax.experimental import pallas as pl
from jax.experimental.pallas import tpu as pltpu
from jax.sharding import Mesh
from jax.sharding import PartitionSpec as P

ZH, ZL, MID, CORE, SUB = AXES = ("zh", "zl", "mid", "core", "sub")
DEVICES = ("dp", "sub")

HEAD_DIM = 64
EPS = 1e-05
ROPE_BASE = 10000.0
NEG_LARGE = -1e30
SUM_STEPS = 4
F32 = jnp.float32
BF16 = jnp.bfloat16
NT = (((1,), (1,)), ((), ()))
NN = (((1,), (0,)), ((), ()))
TN = (((0,), (0,)), ((), ()))


def dot(a, b, dims=NN):
    return lax.dot_general(a, b, dims, preferred_element_type=F32)


def call(kernel, name, grid, in_specs, out_specs, out_shape, scratch=()):
    return pl.pallas_call(
        kernel,
        grid=grid,
        in_specs=in_specs,
        out_specs=out_specs,
        out_shape=out_shape,
        scratch_shapes=scratch,
        name=name,
        cost_estimate=pl.CostEstimate(flops=1000, bytes_accessed=1000, transcendentals=0),
        compiler_params=pltpu.CompilerParams(
            dimension_semantics=("arbitrary",) * len(grid), vmem_limit_bytes=56 << 20
        ),
    )


def whole(shape):
    zeros = (0,) * len(shape)
    return pl.BlockSpec(shape, lambda *_: zeros, pipeline_mode=pl.Buffered(1))


def turn(values, cosine, sine):
    lane = lax.broadcasted_iota(jnp.int32, (values.shape[0], 128), 1)
    low = lane % HEAD_DIM < HEAD_DIM // 2
    blocks = []
    for at in range(0, values.shape[1], 128):
        block = values[:, at : at + 128]
        other = jnp.where(
            low,
            pltpu.roll(block, 128 - HEAD_DIM // 2, 1),
            pltpu.roll(block, HEAD_DIM // 2, 1),
        )
        blocks.append(block * cosine + other * sine)
    return jnp.concatenate(blocks, 1) if len(blocks) > 1 else blocks[0]


def two_heads(rows):
    low = lax.broadcasted_iota(jnp.int32, rows.shape, 1) < HEAD_DIM
    zero = jnp.zeros_like(rows)
    return jnp.concatenate([jnp.where(low, rows, zero), jnp.where(low, zero, rows)], 0)


def one_head(rows):
    half = rows.shape[0] // 2
    low = lax.broadcasted_iota(jnp.int32, (half, 128), 1) < HEAD_DIM
    return jnp.where(low, rows[:half], rows[half:])


def stack_lanes(values):
    return jnp.concatenate([values[:, at : at + 128] for at in range(0, values.shape[1], 128)], 0)


def unstack_lanes(values, rows):
    return jnp.concatenate([values[at : at + rows] for at in range(0, values.shape[0], rows)], 1)


def mask_of(segment):
    row = segment.shape[1]
    query = lax.broadcasted_iota(jnp.int32, (row, row), 0)
    key = lax.broadcasted_iota(jnp.int32, (row, row), 1)
    across = jnp.broadcast_to(segment, (row, row))
    return (across == across.T) & (key <= query)


def probabilities(stacked_q, keys2, allowed, row):
    scores = dot(stacked_q, keys2, NT)
    blocks = []
    for at in range(0, scores.shape[0], row):
        halves = []
        for side in range(2):
            part = scores[at : at + row, side * row : (side + 1) * row]
            part = jnp.where(allowed, part, NEG_LARGE)
            part = jnp.exp(part - jnp.max(part, -1, keepdims=True))
            halves.append(part * (1.0 / jnp.sum(part, -1, keepdims=True)))
        blocks.append(jnp.concatenate(halves, 1))
    return jnp.concatenate(blocks, 0)


def owner(mid, sub, zh):
    return 4 * mid + 2 * sub + zh


def assemble(parts, into, kind, rows, step=None, stride=None, offset=0):
    step = rows if step is None else step
    stride = rows if stride is None else stride
    for zh in range(2):
        for far in range(2):
            for inner in range(2):
                at = owner(far, inner, zh) if kind == "a" else owner(inner, far, zh)
                at = at * stride + offset
                into[at : at + rows] = parts[2 * zh + far][inner * step : inner * step + rows]


def assemble_down(parts, into, first):
    stride = into.shape[0] // 8
    assemble(parts[:4], into, "a", first, stride=stride)
    assemble(parts[4:], into, "b", stride - first, stride=stride, offset=first)


def tile_at(step):
    return (2 * step + 1) % 5


def pick(tile, refs, into):
    for at, ref in enumerate(refs):

        @pl.when(tile == at)
        def _(ref=ref):
            into[...] = ref[...]


def halves(part, send_ref, keep_ref, here=slice(None)):
    step = pl.program_id(0)

    @pl.when(step < 2)
    def _():
        send_ref[0, :, here] = part.astype(BF16)

    @pl.when(step >= 2)
    def _():
        keep_ref[0, :, here] = part.astype(BF16)


def halves_out(tile, width):
    specs = [
        pl.BlockSpec((1, tile, width), lambda s: (jnp.minimum(s, 1), 0, 0)),
        pl.BlockSpec((1, tile, width), lambda s: (jnp.maximum(s - 2, 0), 0, 0)),
    ]
    return specs, [jax.ShapeDtypeStruct((2, tile, width), BF16)] * 2


def quarters(part, send_refs, keep_ref, here=slice(None)):
    step = pl.program_id(0)
    near_ref, zero_ref, one_ref = send_refs
    rows = zero_ref.shape[0]

    @pl.when(step == 0)
    def _():
        near_ref[:, here] = part.astype(BF16)

    @pl.when(step == 1)
    def _():
        zero_ref[:, here] = part[:rows].astype(BF16)
        one_ref[:, here] = part[rows:].astype(BF16)

    @pl.when(step >= 2)
    def _():
        keep_ref[0, :, here] = part.astype(BF16)


def quarters_out(tile, width):
    specs, shapes = halves_out(tile, width)
    sizes = [(tile, width)] + [(tile // 2, width)] * 2
    return (
        [pl.BlockSpec(size, lambda s: (0, 0)) for size in sizes] + specs[1:],
        [jax.ShapeDtypeStruct(size, BF16) for size in sizes] + shapes[1:],
    )


def pick_two(tile, refs, into):
    rows = refs[0].shape[0]
    for at in range(4):

        @pl.when(tile == at)
        def _(at=at):
            into[:rows] = refs[2 * at][...]
            into[rows:] = refs[2 * at + 1][...]


def attn_forward_kernel(row, head_rows, *refs):
    x_refs, (gain_ref, cos_ref, sin_ref, seg_ref, moved_ref, kv_own_ref, kv_core_ref) = (
        refs[:4],
        refs[4:11],
    )
    a_refs, o_refs = refs[11:15], refs[15:19]
    hid_ref, qkv_ref, mixed_ref, send_ref, keep_ref, wqkv_ref, wo_ref, x_ref = refs[19:]
    step = pl.program_id(0)
    width = 8 * head_rows
    pick(tile_at(step), x_refs, x_ref)

    @pl.when(step == 0)
    def _():
        assemble(a_refs, wqkv_ref, "a", head_rows, step=head_rows + HEAD_DIM // 4)
        assemble(o_refs, wo_ref, "b", head_rows)
        kv_rows = HEAD_DIM // 8
        for side in range(2):
            both = [
                [ref[4 * side + at].astype(F32) for ref in (kv_own_ref, kv_core_ref)]
                for at in range(4)
            ]
            for which in range(2):
                here = slice(which * kv_rows, (which + 1) * kv_rows)
                parts = [
                    both[mid * 2 + sub][core][here]
                    for mid in range(2)
                    for core in range(2)
                    for sub in range(2)
                ]
                placed = dot(moved_ref[...], jnp.concatenate(parts, 0).astype(BF16)).astype(BF16)
                low = width + (2 * which + side) * HEAD_DIM
                wqkv_ref[low : low + HEAD_DIM] = placed

    x = x_ref[...].astype(F32)
    inverse = lax.rsqrt(jnp.mean(x * x, -1, keepdims=True) + EPS)
    hidden = (x * inverse * gain_ref[...]).astype(BF16)
    hid_ref[...] = hidden
    lin = dot(hidden, wqkv_ref[...], NT)
    cosine, sine = cos_ref[...], sin_ref[...]
    qk = turn(lin[:, : width + 128], cosine, sine).astype(BF16)
    v_rows = lin[:, width + 128 :].astype(BF16)
    qkv_ref[:, : width + 128] = qk
    qkv_ref[:, width + 128 :] = v_rows
    scale = HEAD_DIM ** (-0.5)
    for at in range(0, x.shape[0], row):
        allowed = mask_of(seg_ref[0, at // row : at // row + 1])
        keys2 = two_heads(qk[at : at + row, width:] * jnp.asarray(scale, BF16))
        values2 = two_heads(v_rows[at : at + row])
        probs = probabilities(stack_lanes(qk[at : at + row, :width]), keys2, allowed, row)
        mixed = dot(probs.astype(BF16), values2).astype(BF16)
        mixed_ref[at : at + row] = unstack_lanes(mixed, row)
    halves(dot(mixed_ref[...], wo_ref[...]), send_ref, keep_ref)


def attn_forward(x, gain, cosine, sine, segment, moved, kv_own, kv_core, a_parts, o_parts,
                 head_rows, row):
    tile, width = x[0].shape
    rows = lambda n: pl.BlockSpec((tile, n), lambda s: (tile_at(s), 0))
    full = lambda n: pl.BlockSpec((n, width), lambda s: (0, 0))
    q_width = 8 * head_rows
    shape = lambda *dims: jax.ShapeDtypeStruct(dims, BF16)
    half_specs, half_shapes = halves_out(tile, width)
    return call(
        functools.partial(attn_forward_kernel, row, head_rows),
        "attn_forward",
        (4,),
        [whole(one.shape) for one in x]
        + [
            whole((1, width)),
            rows(128),
            rows(128),
            pl.BlockSpec((1,) + segment.shape[1:], lambda s: (tile_at(s), 0, 0)),
        ]
        + [whole(one.shape) for one in (moved, kv_own, kv_core, *a_parts, *o_parts)],
        [rows(width), rows(q_width + 256), rows(q_width)]
        + half_specs
        + [full(q_width + 256), full(q_width)],
        [shape(4 * tile, width), shape(4 * tile, q_width + 256), shape(4 * tile, q_width)]
        + half_shapes
        + [shape(q_width + 256, width), shape(q_width, width)],
        [pltpu.VMEM((tile, width), BF16)],
    )(*x, gain, cosine, sine, segment, moved, kv_own, kv_core, *a_parts, *o_parts)


def attn_backward_kernel(row, *refs):
    g_refs, x_refs = refs[:8], refs[8:12]
    qkv_ref, cos_ref, sin_ref, seg_ref, wqkv_ref, wo_ref = refs[12:18]
    gqkv_ref, gain_ref, *send_refs, keep_ref, g_ref, x_ref = refs[18:]
    step = pl.program_id(0)
    pick_two(tile_at(step), g_refs, g_ref)
    pick(tile_at(step), x_refs, x_ref)
    grad_mixed = dot(g_ref[...], wo_ref[...], NT).astype(BF16)
    width = grad_mixed.shape[1]
    qkv = qkv_ref[...]
    cosine, sine = cos_ref[...], -sin_ref[...]
    scale = HEAD_DIM ** (-0.5)
    for at in range(0, grad_mixed.shape[0], row):
        here = slice(at, at + row)
        allowed = mask_of(seg_ref[0, at // row : at // row + 1])
        keys2 = two_heads(qkv[here, width : width + 128] * jnp.asarray(scale, BF16))
        values2 = two_heads(qkv[here, width + 128 :])
        stacked_q = stack_lanes(qkv[here, :width])
        stacked_g = stack_lanes(grad_mixed[here])
        probs = probabilities(stacked_q, keys2, allowed, row)
        grad_probs = dot(stacked_g, values2, NT)
        moved = grad_probs * probs
        left = probs[:, :row] * (
            grad_probs[:, :row] - jnp.sum(moved[:, :row], -1, keepdims=True)
        )
        right = probs[:, row:] * (
            grad_probs[:, row:] - jnp.sum(moved[:, row:], -1, keepdims=True)
        )
        grad_scores = jnp.concatenate([left, right], 1).astype(BF16)
        grad_value = one_head(dot(probs.astype(BF16), stacked_g, TN))
        grad_key = one_head(dot(grad_scores, stacked_q, TN)) * scale
        grad_query = unstack_lanes(dot(grad_scores, keys2), row)
        gqkv_ref[here, :width] = turn(grad_query, cosine[here], sine[here]).astype(BF16)
        gqkv_ref[here, width : width + 128] = turn(grad_key, cosine[here], sine[here]).astype(BF16)
        gqkv_ref[here, width + 128 :] = grad_value.astype(BF16)
    part = dot(gqkv_ref[...], wqkv_ref[...])
    x = x_ref[...].astype(F32)
    normed = x * lax.rsqrt(jnp.mean(x * x, -1, keepdims=True) + EPS)
    terms = jnp.sum(part * normed, 0, keepdims=True)

    @pl.when(step == 0)
    def _():
        gain_ref[...] = terms

    @pl.when(step > 0)
    def _():
        gain_ref[...] += terms

    quarters(part, send_refs, keep_ref)


def attn_backward(grads, x, qkv, cosine, sine, segment, wqkv, wo, row):
    tile, width = x[0].shape
    rows = lambda n: pl.BlockSpec((tile, n), lambda s: (tile_at(s), 0))
    half_specs, half_shapes = quarters_out(tile, width)
    return call(
        functools.partial(attn_backward_kernel, row),
        "attn_backward",
        (4,),
        [whole(one.shape) for one in (*grads, *x)]
        + [
            rows(qkv.shape[1]),
            rows(128),
            rows(128),
            pl.BlockSpec((1,) + segment.shape[1:], lambda s: (tile_at(s), 0, 0)),
            whole(wqkv.shape),
            whole(wo.shape),
        ],
        [rows(qkv.shape[1]), pl.BlockSpec((1, width), lambda s: (0, 0))] + half_specs,
        [jax.ShapeDtypeStruct(qkv.shape, BF16), jax.ShapeDtypeStruct((1, width), F32)]
        + half_shapes,
        [pltpu.VMEM((tile, width), BF16)] * 2,
    )(*grads, *x, qkv, cosine, sine, segment, wqkv, wo)


def units_kernel(*refs):
    inner_ref, dgate_ref, dup_ref, gate_ref, up_ref, h_ref = refs[12:]
    step = pl.program_id(0)
    pick(step, refs[:4], h_ref)

    @pl.when(step == 0)
    def _():
        assemble(refs[4:8], gate_ref, "a", gate_ref.shape[0] // 8)
        assemble(refs[8:12], up_ref, "b", up_ref.shape[0] // 8)

    gate = dot(h_ref[...], gate_ref[...], NT)
    up = dot(h_ref[...], up_ref[...], NT)
    sigmoid = 1.0 / (1.0 + jnp.exp(-gate))
    silu = gate * sigmoid
    inner_ref[...] = (silu * up).astype(BF16)
    dup_ref[...] = silu.astype(BF16)
    dgate_ref[...] = (up * (sigmoid * (1.0 + gate * (1.0 - sigmoid)))).astype(BF16)


def units(hidden, gate_parts, up_parts):
    tile, width = hidden[0].shape
    count = 4 * gate_parts[0].shape[0]
    rows = pl.BlockSpec((tile, count), lambda s: (s, 0))
    return call(
        units_kernel,
        "units",
        (4,),
        [whole(one.shape) for one in (*hidden, *gate_parts, *up_parts)],
        [rows] * 3,
        [jax.ShapeDtypeStruct((4 * tile, count), BF16)] * 3,
        [pltpu.VMEM((count, width), BF16)] * 2 + [pltpu.VMEM((tile, width), BF16)],
    )(*hidden, *gate_parts, *up_parts)


def unit_grads_kernel(first, *refs):
    dgate_ref, dup_ref = refs[4:6]
    gg_ref, gu_ref, down_ref, g_ref = refs[14:]
    step = pl.program_id(0)
    pick(step, refs[:4], g_ref)

    @pl.when(step == 0)
    def _():
        assemble_down(refs[6:14], down_ref, first)

    inner = dot(g_ref[...], down_ref[...], NT)
    gg_ref[...] = (inner * dgate_ref[...].astype(F32)).astype(BF16)
    gu_ref[...] = (inner * dup_ref[...].astype(F32)).astype(BF16)


def unit_grads(grads, down_parts, dgate, dup, first):
    tile, width = grads[0].shape
    count = dgate.shape[1]
    rows = pl.BlockSpec((tile, count), lambda s: (s, 0))
    return call(
        functools.partial(unit_grads_kernel, first),
        "unit_grads",
        (4,),
        [whole(one.shape) for one in grads]
        + [rows, rows]
        + [whole(one.shape) for one in down_parts],
        [rows] * 2,
        [jax.ShapeDtypeStruct((4 * tile, count), BF16)] * 2,
        [pltpu.VMEM((count, width), BF16), pltpu.VMEM((tile, width), BF16)],
    )(*grads, dgate, dup, *down_parts)


def sum_kernel(count, first, *refs):
    lefts, parts = refs[:count], refs[count : count + 8]
    *send_refs, keep_ref = refs[count + 8 : len(refs) - count]
    weights = refs[len(refs) - count :]
    rows = weights[0].shape[0] // 8
    if count == 1:
        assemble_down(parts, weights[0], first)
    else:
        assemble(parts[:4], weights[0], "a", rows)
        assemble(parts[4:], weights[1], "b", rows)
    total = dot(lefts[0][...], weights[0][...])
    for left, weight in zip(lefts[1:], weights[1:]):
        total = total + dot(left[...], weight[...])
    tile = keep_ref.shape[1]
    near, far = total[tile : 2 * tile].astype(BF16), total[3 * tile :].astype(BF16)
    keep_ref[0] = total[:tile].astype(BF16)
    keep_ref[1] = total[2 * tile : 3 * tile].astype(BF16)
    if len(send_refs) == 1:
        send_refs[0][0] = near
        send_refs[0][1] = far
    else:
        near_ref, zero_ref, one_ref = send_refs
        near_ref[...] = near
        zero_ref[...] = far[: tile // 2]
        one_ref[...] = far[tile // 2 :]


def sum_rows(lefts, parts, name, first=0):
    tokens, count = lefts[0].shape
    width = parts[0].shape[1]
    tile, columns = tokens // 4, width // SUM_STEPS
    both = (2, tile)
    sizes = [both, both] if len(lefts) == 1 else [(tile,), (tile // 2,), (tile // 2,), both]
    shape = jax.ShapeDtypeStruct

    def block(size):
        zeros = (0,) * len(size)
        return pl.BlockSpec((*size, columns), lambda s: (*zeros, s))

    return call(
        functools.partial(sum_kernel, len(lefts), first),
        name,
        (SUM_STEPS,),
        [whole(one.shape) for one in lefts]
        + [pl.BlockSpec((one.shape[0], columns), lambda s: (0, s)) for one in parts],
        [block(size) for size in sizes],
        [shape((*size, width), BF16) for size in sizes],
        [pltpu.VMEM((count, columns), BF16)] * len(lefts),
    )(*lefts, *parts)


def put_owners(place, a_keep, a_send, b_keep, b_send):
    step = pl.program_id(0)

    @pl.when(step < 2)
    def _():
        place(a_keep, (0, 1, 2, 3))
        place(a_send, (4, 5, 6, 7))

    @pl.when(step >= 2)
    def _():
        place(b_keep, (0, 1, 4, 5))
        place(b_send, (2, 3, 6, 7))


def owners_out(rows, width):
    half = lambda place: pl.BlockSpec((4, rows, width // 4), lambda s: (0, 0, place(s)))
    early, late = half(lambda s: jnp.minimum(s, 1)), half(lambda s: jnp.maximum(s - 2, 0))
    return [early, early, late, late], [jax.ShapeDtypeStruct((4, rows, width // 2), BF16)] * 4


def weight_grad_kernel(rows, l_ref, *refs):
    right = jnp.concatenate([ref[...] for ref in refs[:4]], 0)
    grads = dot(l_ref[...], right, TN).astype(BF16)

    def place(ref, owners):
        for at, one in enumerate(owners):
            ref[at] = grads[one * rows : (one + 1) * rows]

    put_owners(place, *refs[4:])


def weight_grad(left, right, name):
    tokens, count = left.shape
    tile, width = right[0].shape
    specs, shapes = owners_out(count // 8, width)
    return call(
        functools.partial(weight_grad_kernel, count // 8),
        name,
        (4,),
        [whole(left.shape)] + [pl.BlockSpec((tile, width // 4), lambda s: (0, s))] * 4,
        specs,
        shapes,
    )(left, *right)


def attn_grads_kernel(head_rows, kv_rows, gqkv_ref, hid_ref, mixed_ref, moved_ref, *refs):
    first = dot(gqkv_ref[...], hid_ref[...], TN).astype(BF16)
    right = jnp.concatenate([ref[...] for ref in refs[:8]], 0)
    second = dot(mixed_ref[...], right, TN).astype(BF16)
    width = 8 * head_rows
    placed = {}
    for which in range(2):
        for side in range(2):
            low = width + (2 * which + side) * HEAD_DIM
            placed[which, side] = dot(moved_ref[...], first[low : low + HEAD_DIM])

    def place(ref, owners):
        for at, one in enumerate(owners):
            mid, sub, side = one // 4, one // 2 % 2, one % 2
            lows = [(mid * 4 + core * 2 + sub) * kv_rows for core in range(2)]
            kv = [placed[which, side][low : low + kv_rows] for low in lows for which in range(2)]
            here = slice(one * head_rows, (one + 1) * head_rows)
            ref[at, :head_rows] = first[here]
            ref[at, head_rows : head_rows + 4 * kv_rows] = jnp.concatenate(kv, 0).astype(BF16)
            ref[at, head_rows + 4 * kv_rows :] = second[here]

    put_owners(place, *refs[8:])


def attn_grads(gqkv, hidden, mixed, right, moved, head_rows, kv_rows):
    tokens, width = hidden.shape
    columns = width // 4
    specs, shapes = owners_out(2 * head_rows + 4 * kv_rows, width)
    return call(
        functools.partial(attn_grads_kernel, head_rows, kv_rows),
        "attn_grads",
        (4,),
        [
            whole(gqkv.shape),
            pl.BlockSpec((tokens, columns), lambda s: (0, s)),
            whole(mixed.shape),
            whole(moved.shape),
        ]
        + [pl.BlockSpec((tokens // 8, columns), lambda s: (0, s))] * 8,
        specs,
        shapes,
    )(gqkv, hidden, mixed, moved, *right)


def total_kernel(ka_ref, ga_ref, kb_ref, gb_ref, ta_ref, tb_ref, *refs):
    *last_refs, out_ref = refs
    half = ka_ref.shape[2]
    last = jnp.concatenate([ref[...].astype(F32) for ref in last_refs], 1)
    a, b = (
        keep[0].astype(F32) + got[0].astype(F32) + two[0].astype(F32)
        for keep, got, two in ((ka_ref, ga_ref, ta_ref), (kb_ref, gb_ref, tb_ref))
    )
    out_ref[:, :half] = a + last[:, :half]
    out_ref[:, half:] = b + last[:, half:]


def total_sum(pairs):
    _, rows, half = pairs[0].shape
    block = pl.BlockSpec((1, rows, half), lambda s: (0, 0, 0))
    return call(
        total_kernel,
        "total",
        (1,),
        [block] * 6 + [whole(one.shape) for one in pairs[6:]],
        pl.BlockSpec((rows, 2 * half), lambda s: (0, 0)),
        jax.ShapeDtypeStruct((rows, 2 * half), F32),
    )(*pairs)


def finish_kernel(x_ref, gain_ref, mid0_ref, mid1_ref, keep_ref, near_ref, zero_ref, one_ref,
                  resid_ref, okeep_ref, ogot_ref, ozero_ref, oone_ref, grad_ref, out_ref):
    rows = zero_ref.shape[0]
    for at, far_ref, mid_ref, ofar_ref in (
        (0, zero_ref, mid0_ref, ozero_ref),
        (1, one_ref, mid1_ref, oone_ref),
    ):
        here = slice(at * rows, (at + 1) * rows)
        x = x_ref[here].astype(F32)
        inverse = lax.rsqrt(jnp.mean(x * x, -1, keepdims=True) + EPS)
        grad = keep_ref[0, here].astype(F32) + near_ref[here].astype(F32)
        grad = grad + far_ref[...].astype(F32)
        grad = mid_ref[...] + norm_backward(grad, x * inverse, inverse, gain_ref[...])
        grad_ref[here] = grad.astype(BF16)
        out = okeep_ref[0, here].astype(F32) + ogot_ref[0, here].astype(F32)
        out_ref[here] = (resid_ref[here] + (out + ofar_ref[...].astype(F32))).astype(BF16)


def finish(x, gain, mid0, mid1, keep, near, zero, one, resid, out_keep, out_got, out_far):
    tile, width = x.shape
    first = pl.BlockSpec((1, tile, width), lambda s: (0, 0, 0))
    full = lambda array: whole(array.shape)
    return call(
        finish_kernel,
        "finish",
        (1,),
        [full(x), full(gain), full(mid0), full(mid1), first, full(near), full(zero), full(one)]
        + [full(resid), first, first, *map(full, out_far)],
        [pl.BlockSpec((tile, width), lambda s: (0, 0))] * 2,
        [jax.ShapeDtypeStruct((tile, width), BF16)] * 2,
    )(x, gain, mid0, mid1, keep, near, zero, one, resid, out_keep, out_got, *out_far)


def norm_forward(values, gain):
    inverse = lax.rsqrt(jnp.mean(values * values, -1, keepdims=True) + EPS)
    normed = values * inverse
    return (normed, inverse, (normed * gain).astype(BF16))


def norm_backward(grad_hidden, normed, inverse, gain):
    grad_normed = grad_hidden * gain
    return inverse * (grad_normed - normed * jnp.mean(grad_normed * normed, -1, keepdims=True))


def swap(value, axis):
    return lax.ppermute(value, axis, [(0, 1), (1, 0)])


def up32(value):
    return value.astype(F32)


def join(*values):
    return jnp.concatenate(values, 0)


class Live:
    def cut(self):
        names = sorted(vars(self))
        values = lax.optimization_barrier(tuple(getattr(self, name) for name in names))
        for name, value in zip(names, values):
            setattr(self, name, value)

    @property
    def pop(self):
        return Pop(self)


class Pop:
    def __init__(self, live):
        self.live = live

    def __getattr__(self, name):
        value = getattr(self.live, name)
        delattr(self.live, name)
        return value


def tables(lengths_all, row_count):
    seq_ends = jnp.cumsum(lengths_all, 1)
    token = jnp.arange(row_count, dtype=jnp.int32)
    passed = (token[None, :, None] >= seq_ends[:, None, :]).astype(jnp.int32)
    segment = jnp.sum(passed, 2)
    offsets = token[None, :] - jnp.sum(passed * lengths_all[:, None, :], 2)
    half = HEAD_DIM // 2
    lane = jnp.arange(128, dtype=jnp.int32)
    frequency = ROPE_BASE ** (-(lane % half).astype(F32) * 2.0 / HEAD_DIM)
    angles = offsets.reshape(-1, 1).astype(F32) * frequency[None, :]
    sign = jnp.where(lane % HEAD_DIM < half, -1.0, 1.0)
    return (segment.astype(F32), jnp.cos(angles), jnp.sin(angles) * sign[None, :])


def on_device_small(
    block_input,
    out_grad,
    seq_lengths,
    attn_gain,
    w_query,
    w_key,
    w_value,
    w_output,
    mlp_gain,
    w_gate,
    w_up,
    w_down,
):
    width = block_input.shape[2]
    row_count = block_input.shape[1]
    micro = block_input.shape[0]
    tokens = micro * row_count
    head_rows = w_query.shape[0]
    kv_rows = w_key.shape[0]
    gain_width = attn_gain.shape[0]
    packed = seq_lengths.shape[2]
    units_own = w_gate.shape[0]
    first = -(-units_own // 2 // 32) * 32
    second = units_own - first
    qkv_rows = head_rows + 2 * kv_rows
    place = {name: lax.axis_index(name) for name in AXES}
    place8 = place[MID] * 4 + place[CORE] * 2 + place[SUB]
    place32 = place[ZH] * 16 + place[ZL] * 8 + place8
    index = jnp.arange(8 * kv_rows, dtype=jnp.int32)
    block, inside = index // kv_rows, index % kv_rows
    moved = (block[:, None] == (block[None, :] ^ place8)) & (inside[:, None] == inside[None, :])
    moved = moved.astype(BF16)
    index = jnp.arange(32, dtype=jnp.int32)
    ordered = (index[:, None] == (index[None, :] ^ place32)).astype(BF16)

    def pair_sum(keep, got, at):
        return up32(keep[at]) + up32(got[at])

    v = Live()
    own_x = block_input.reshape(tokens, width)
    v.own_g = out_grad.reshape(tokens, width)

    pack = join(attn_gain, mlp_gain, seq_lengths.reshape(micro * packed).astype(BF16))
    v.pack = jnp.pad(pack.reshape(1, -1), ((0, 0), (0, 256 - pack.shape[0])))
    v.pack_far = swap(v.pack, ZL)
    v.a0 = join(w_query, w_key, w_value)
    a_rows = v.a0.shape[0]
    v.w_gate, v.w_up, v.w_down, v.w_output = w_gate, w_up, w_down, w_output
    v.got_x = swap(join(v.a0, w_gate), SUB)
    v.got_y = swap(join(w_output, w_up), MID)
    v.ao = swap(join(v.a0, w_output), ZH)
    v.own_x = own_x
    v.x_far = swap(v.own_x, ZL)
    v.cut()

    v.g0x, v.u0y = v.got_x[a_rows:], v.got_y[head_rows:]
    v.a1, v.o1 = v.ao[:a_rows], v.ao[a_rows:]
    v.o0s = join(v.pop.w_output, v.got_y[:head_rows], v.a1)
    v.a0s = join(v.pop.a0, v.got_x[:a_rows], v.o1)
    v.o0t, v.a0t = swap(v.o0s, SUB), swap(v.a0s, MID)
    packs = jnp.concatenate([v.pop.pack, v.pop.pack_far], 1)
    packs = jnp.concatenate([packs, swap(packs, CORE)], 1)
    v.packs = jnp.pad(packs, ((0, 15), (0, width - packs.shape[1])))
    v.gate_low = swap(join(v.w_gate[:second], v.packs), ZH)
    v.x_core, v.x_far_core = swap(v.own_x, CORE), swap(v.x_far, CORE)
    del v.ao, v.got_x, v.got_y
    v.cut()

    packs = jnp.concatenate([v.packs[:, :1024], v.gate_low[second:, :1024]], 1)
    v.o1s = join(v.pop.o1, v.a0t[2 * a_rows :], packs)
    v.a1s = join(v.pop.a1, v.o0t[2 * head_rows :], packs)
    v.o1t, v.a1t = swap(v.o1s, SUB), swap(v.a1s, MID)
    v.gate_high = swap(v.w_gate[second:], ZH)
    v.packs_near = packs[:1]
    v.packs_across = lax.ppermute(packs[:1], (MID, SUB), [(at, 3 - at) for at in range(4)])
    lengths = v.pop.packs[0, :1024].reshape(2, 2, 256)
    lengths = lengths[:, :, 2 * gain_width : 2 * gain_width + micro * packed]
    lengths_all = lengths.transpose(1, 0, 2).reshape(4 * micro, packed).astype(jnp.int32)
    segment, v.cosine, v.sine = tables(lengths_all, row_count)
    v.segment = segment.reshape(4, micro, row_count)
    v.x = (v.own_x, v.pop.x_core, v.pop.x_far, v.pop.x_far_core)
    v.cut()

    v.u0s, v.g0s = join(v.w_up, v.pop.u0y), join(v.w_gate, v.pop.g0x)
    v.u0t, v.g0t = swap(v.u0s, SUB), swap(v.g0s, MID)
    v.u1 = swap(v.w_up, ZH)
    a_parts = (v.pop.a0s, v.pop.a0t, v.pop.a1s, v.pop.a1t)
    o_parts = (v.pop.o0s, v.pop.o0t, v.pop.o1s, v.pop.o1t)
    kv_own = join(
        *(one[: 2 * a_rows].reshape(2, a_rows, width)[:, head_rows:] for one in a_parts)
    )
    kv_core = swap(kv_own, CORE)
    packs = join(
        v.pop.packs_near, o_parts[3][-16:-15], a_parts[3][-16:-15], v.pop.packs_across
    )
    gains_rel = packs.reshape(2, 2, 2, 2, 2, 256)[..., : 2 * gain_width]
    gains_rel = gains_rel.transpose(2, 4, 0, 3, 1, 5)
    gains_all = dot(ordered, gains_rel.reshape(32, 2 * gain_width))
    v.gain_one = gains_all[:, :gain_width].reshape(1, width)
    v.gain_two = gains_all[:, gain_width:].reshape(1, width)
    attn = attn_forward(
        v.x,
        v.gain_one,
        v.cosine,
        v.sine,
        v.segment,
        moved,
        kv_own,
        kv_core,
        a_parts,
        o_parts,
        head_rows,
        row_count,
    )
    v.hidden_one, v.qkv, v.mixed, v.part_send, v.part_keep, v.wqkv, v.full_o = attn
    v.cut()

    v.g1 = join(v.gate_low[:second], v.pop.gate_high)
    del v.gate_low
    v.got_x = swap(join(v.g1, v.w_down[:first]), SUB)
    v.got_y = swap(join(v.u1, v.w_down[first:]), MID)
    v.da1 = swap(v.w_down[:first], ZH)
    v.part_got = swap(v.pop.part_send, CORE)
    mid_far = pair_sum(v.part_keep, v.part_got, 1).astype(BF16)
    v.mid_far = swap(mid_far, ZL)
    v.cut()

    v.dax, v.dby = v.got_x[units_own:], v.got_y[units_own:]
    v.g1s, v.u1s = join(v.pop.g1, v.got_x[:units_own]), join(v.pop.u1, v.got_y[:units_own])
    v.g1t, v.u1t = swap(v.g1s, MID), swap(v.u1s, SUB)
    v.resid_mid = up32(v.own_x) + (
        pair_sum(v.pop.part_keep, v.pop.part_got, 0) + up32(v.pop.mid_far)
    )
    v.db1 = swap(v.w_down[first:], ZH)
    h_own = norm_forward(v.resid_mid, v.gain_two)[2]
    v.h_far, v.h_core = swap(h_own, ZL), swap(h_own, CORE)
    v.h_own = h_own
    del v.got_x, v.got_y
    v.cut()

    v.db0s = join(v.w_down[first:], v.pop.dby, v.da1)
    v.da0s = join(v.w_down[:first], v.pop.dax, v.db1)
    v.db0t, v.da0t = swap(v.db0s, SUB), swap(v.da0s, MID)
    v.g_far, v.g_core = swap(v.own_g, ZL), swap(v.own_g, CORE)
    v.h = (v.pop.h_own, v.pop.h_core, v.h_far, swap(v.h_far, CORE))
    del v.w_gate, v.w_up, v.w_down, v.h_far
    v.gate_parts = (v.pop.g0s, v.pop.g0t, v.pop.g1s, v.pop.g1t)
    v.up_parts = (v.pop.u0s, v.pop.u0t, v.pop.u1s, v.pop.u1t)
    v.inner, v.dgate, v.dup = units(v.h, v.gate_parts, v.up_parts)
    v.cut()

    v.da1s = join(v.pop.da1, v.db0t[2 * second :])
    v.db1s = join(v.pop.db1, v.da0t[2 * first :])
    v.da1t, v.db1t = swap(v.da1s, MID), swap(v.db1s, SUB)
    v.g = (v.own_g, v.pop.g_core, v.g_far, swap(v.g_far, CORE))
    del v.g_far
    v.dg = weight_grad(v.inner, v.g, "down_grad")
    v.cut()

    def step_one(grads):
        keep_a, send_a, keep_b, send_b = grads
        return (keep_a, swap(send_a, MID), keep_b, swap(send_b, SUB))

    def sums_one(pairs):
        keep_a, got_a, keep_b, got_b = pairs
        far = slice(2, 4)
        return pairs + (
            pair_sum(keep_a, got_a, far).astype(BF16),
            pair_sum(keep_b, got_b, far).astype(BF16),
        )

    def step_two(pairs):
        return pairs[:4] + (swap(pairs[4], SUB), swap(pairs[5], MID))

    def part_sum(pairs, at, low, high):
        half = pairs[0].shape[2]
        sums = []
        for side in range(2):
            here = slice(max(low - side * half, 0), min(high - side * half, half))
            if here.start < here.stop:
                keep, got, two = pairs[2 * side], pairs[2 * side + 1], pairs[4 + side]
                sums.append(up32(keep[at, :, here]) + up32(got[at, :, here]) + up32(two[at, :, here]))
        return sums[0] if len(sums) == 1 else jnp.concatenate(sums, 1)

    def last_send(pairs, low, high):
        return part_sum(pairs, 1, low, high).astype(BF16)

    def step_three(pairs, send):
        return pairs + (swap(send, ZH),)

    def total(pairs):
        last = jnp.concatenate([up32(one) for one in pairs[6:]], 1)
        return part_sum(pairs, 0, 0, width) + last

    even, early, most = width // 2, width * 5 // 8, width * 3 // 4

    def gain_step(name):
        at = 1 + AXES.index(name)
        low, high = jnp.split(v.gain_grads, 2, at)
        mine = jnp.where(place[name] == 0, low, high)
        sent = jnp.where(place[name] == 0, high, low)
        v.gain_grads = mine + swap(sent, name)

    def far_of(keep, got, micro_at):
        here = slice(micro_at * row_count, (micro_at + 1) * row_count)
        return (up32(keep[1, here]) + up32(got)).astype(BF16)

    def mid_grads(micro_at, far):
        here = slice(micro_at * row_count, (micro_at + 1) * row_count)
        gh2 = up32(v.gh2_keep[0, here]) + up32(v.gh2_near[here]) + up32(far)
        resid = v.resid_mid[here]
        inverse = lax.rsqrt(jnp.mean(resid * resid, -1, keepdims=True) + EPS)
        normed = resid * inverse
        grad_mid = up32(v.own_g[here]) + norm_backward(gh2, normed, inverse, v.gain_two)
        return grad_mid, grad_mid.astype(BF16), jnp.sum(gh2 * normed, 0, keepdims=True)

    v.dg = step_one(v.dg)
    v.down_parts = (
        *(v.pop.da0s, v.pop.da0t, v.pop.da1s, v.pop.da1t),
        *(v.pop.db0s, v.pop.db0t, v.pop.db1s, v.pop.db1t),
    )
    v.gg, v.gu = unit_grads(v.pop.g, v.down_parts, v.pop.dgate, v.pop.dup, first)
    *send, v.gh2_keep = sum_rows(
        (v.gg, v.gu), (*v.pop.gate_parts, *v.pop.up_parts), "hidden_grads"
    )
    v.gh2_near = send[0]
    v.gh2_far = (swap(send[1], CORE), swap(send[2], CORE))
    v.cut()
    v.dg = sums_one(v.dg)
    v.cut()

    v.dg = step_two(v.dg)
    v.gh2_zero = swap(far_of(v.gh2_keep, v.gh2_far[0], 0), ZL)
    v.gh2_near = swap(v.gh2_near, CORE)
    v.gh2_one = far_of(v.gh2_keep, v.gh2_far[1], 1)
    v.gw = weight_grad(v.pop.gg, v.h, "gate_grad")
    v.cut()

    v.gw = step_one(v.gw)
    v.gh2_one = swap(v.gh2_one, ZL)
    v.grad_mid0, v.gb0, v.mlp_terms = mid_grads(0, v.pop.gh2_zero)
    v.gb0_far = swap(v.gb0, ZL)
    v.dg_send = last_send(v.dg, most, width)
    v.dg = step_three(v.dg, last_send(v.dg, 0, most))
    v.out_send, v.out_keep = sum_rows((v.pop.inner,), v.pop.down_parts, "block_out", first)
    v.cut()

    v.grad_mid1, v.gb1, terms = mid_grads(1, v.pop.gh2_one)
    v.mlp_terms = v.mlp_terms + terms
    v.gb1_far = swap(v.gb1, ZL)
    del v.gh2_keep, v.gh2_near, v.gh2_far
    v.gw = step_two(sums_one(v.gw))
    v.dg = step_three(v.dg, v.pop.dg_send)
    v.out_got = swap(v.pop.out_send, CORE)
    v.uw = weight_grad(v.pop.gu, v.pop.h, "up_grad")
    v.cut()

    v.uw = step_one(v.uw)
    v.gw_send = last_send(v.gw, most, width)
    v.gw = step_three(v.gw, last_send(v.gw, 0, most))
    v.out_zero = far_of(v.out_keep, v.out_got[1, :row_count], 0)
    v.out_zero = swap(v.out_zero, ZL)
    gb = (v.pop.gb0, v.pop.gb1), (v.pop.gb0_far, v.pop.gb1_far)
    v.gb = tuple(
        one for rows in gb for one in (*rows, *(swap(piece, CORE) for piece in rows))
    )
    v.gqkv, attn_terms, *send, v.gh1_keep = attn_backward(
        v.gb,
        v.pop.x,
        v.pop.qkv,
        v.pop.cosine,
        v.pop.sine,
        v.pop.segment,
        v.pop.wqkv,
        v.pop.full_o,
        row_count,
    )
    v.gh1_near = send[0]
    v.gh1_far = (swap(send[1], CORE), swap(send[2], CORE))
    gain_grads = join(attn_terms, v.pop.mlp_terms)
    v.gain_grads = gain_grads.reshape(2, 2, 2, 2, 2, 2, gain_width)
    v.cut()
    v.uw = sums_one(v.uw)
    v.cut()

    v.uw = step_two(v.uw)
    v.gh1_zero = swap(far_of(v.gh1_keep, v.gh1_far[0], 0), ZL)
    v.gh1_near = swap(v.gh1_near, CORE)
    v.gw = step_three(v.gw, v.pop.gw_send)
    v.aw = attn_grads(
        v.pop.gqkv, v.pop.hidden_one, v.pop.mixed, v.pop.gb, moved, head_rows, kv_rows
    )
    v.gh1_one = far_of(v.gh1_keep, v.gh1_far[1], 1)
    v.out_one = far_of(v.out_keep, v.out_got[1, row_count:], 1)
    v.cut()

    v.aw = step_one(v.aw)
    v.gh1_one = swap(v.gh1_one, ZL)
    v.uw_send = last_send(v.uw, early, width)
    v.uw = step_three(v.uw, last_send(v.uw, 0, early))
    v.cut()
    v.aw = sums_one(v.aw)
    v.cut()

    v.aw = step_two(v.aw)
    v.uw = step_three(v.uw, v.pop.uw_send)
    v.out_one = swap(v.out_one, ZL)
    gain_step(ZH)
    v.cut()

    aw = step_three(v.aw, last_send(v.aw, 0, even))
    aw = step_three(aw, last_send(v.aw, even, width))
    gain_step(MID)
    gain_step(SUB)
    gain_step(CORE)
    gain_step(ZL)
    input_grad, block_out = finish(
        v.own_x,
        v.gain_one,
        v.pop.grad_mid0,
        v.pop.grad_mid1,
        v.pop.gh1_keep,
        v.pop.gh1_near,
        v.pop.gh1_zero,
        v.pop.gh1_one,
        v.pop.resid_mid,
        v.pop.out_keep,
        v.pop.out_got,
        (v.pop.out_zero, v.pop.out_one),
    )
    down_grad, gate_grad, up_grad = (
        total_sum(v.pop.dg), total_sum(v.pop.gw), total_sum(v.pop.uw)
    )
    grads = total(aw)
    kv_grads = grads[head_rows:qkv_rows] + swap(grads[qkv_rows : qkv_rows + 2 * kv_rows], CORE)
    return (
        block_out.reshape(block_input.shape),
        input_grad.reshape(block_input.shape),
        v.gain_grads[0].reshape(gain_width),
        grads[:head_rows],
        kv_grads[:kv_rows],
        kv_grads[kv_rows:],
        grads[qkv_rows + 2 * kv_rows :],
        v.gain_grads[1].reshape(gain_width),
        gate_grad,
        up_grad,
        down_grad,
    )


def positions(lengths_row, row_count):
    seq_ends = jnp.cumsum(lengths_row)
    starts = seq_ends - lengths_row
    token_index = jnp.arange(row_count, dtype=jnp.int32)
    segment = jnp.sum((token_index[:, None] >= seq_ends[None, :]).astype(jnp.int32), 1)
    chosen = segment[:, None] == jnp.arange(lengths_row.shape[0], dtype=jnp.int32)[None, :]
    offsets = token_index - jnp.sum(jnp.where(chosen, starts[None, :], 0), 1)
    allowed = (segment[:, None] == segment[None, :]) & (
        token_index[None, :] <= token_index[:, None]
    )
    return (offsets, allowed)


def rotary_tables(offsets, width):
    half_width = width // 2
    frequency = ROPE_BASE ** (-jnp.arange(half_width, dtype=jnp.float32) * 2.0 / width)
    angles = offsets.astype(jnp.float32)[:, None] * frequency[None, :]
    return (jnp.cos(angles)[:, None, :], jnp.sin(angles)[:, None, :])


def rotate(values, cosine, sine_table):
    half_width = values.shape[-1] // 2
    first_half = values[..., :half_width]
    second_half = values[..., half_width:]
    return jnp.concatenate(
        [
            first_half * cosine - second_half * sine_table,
            second_half * cosine + first_half * sine_table,
        ],
        -1,
    )


def rotate_back(grads, cosine, sine_table):
    half_width = grads.shape[-1] // 2
    upper_half = grads[..., :half_width]
    lower_half = grads[..., half_width:]
    return jnp.concatenate(
        [
            upper_half * cosine + lower_half * sine_table,
            lower_half * cosine - upper_half * sine_table,
        ],
        -1,
    )


def project(activity, weight):
    return lax.dot_general(
        activity, weight, (((1,), (1,)), ((), ())), preferred_element_type=jnp.float32
    )


def apply_rows(activity, weight):
    return jnp.dot(activity, weight, preferred_element_type=jnp.float32)


def general_norm_forward(values, gain_row):
    inverse = lax.rsqrt(jnp.mean(values * values, -1, keepdims=True) + EPS)
    normed = values * inverse
    return (normed, inverse, (normed * gain_row.astype(jnp.float32)).astype(jnp.bfloat16))


def general_norm_backward(grad_hidden, normed, inverse, gain_row):
    grad_normed = grad_hidden * gain_row.astype(jnp.float32)
    return inverse * (grad_normed - normed * jnp.mean(grad_normed * normed, -1, keepdims=True))


def attention_scores(query_rot, key_rot, allowed):
    scores = jnp.einsum(
        "qhgd,khd->hgqk", query_rot, key_rot, preferred_element_type=jnp.float32
    ) * HEAD_DIM ** (-0.5)
    return jnp.where(allowed, scores, NEG_LARGE)


def forward_pass(block_rows, lengths_row, gathered):
    attn_gain, w_query, w_key, w_value, w_output, mlp_gain, w_gate, w_up, w_down = gathered
    row_count = block_rows.shape[0]
    query_heads = w_query.shape[0] // HEAD_DIM
    key_heads = w_key.shape[0] // HEAD_DIM
    group_size = query_heads // key_heads
    offsets, allowed = positions(lengths_row, row_count)
    cosine, sine_table = rotary_tables(offsets, HEAD_DIM)
    resid_in = block_rows.astype(jnp.float32)
    normed_one, inverse_one, hidden_one = general_norm_forward(resid_in, attn_gain)
    query_lin = project(hidden_one, w_query).reshape(row_count, query_heads, HEAD_DIM)
    key_lin = project(hidden_one, w_key).reshape(row_count, key_heads, HEAD_DIM)
    value_rows = (
        project(hidden_one, w_value).astype(jnp.bfloat16).reshape(row_count, key_heads, HEAD_DIM)
    )
    query_rot = (
        rotate(query_lin, cosine, sine_table)
        .astype(jnp.bfloat16)
        .reshape(row_count, key_heads, group_size, HEAD_DIM)
    )
    key_rot = rotate(key_lin, cosine, sine_table).astype(jnp.bfloat16)
    scores = attention_scores(query_rot, key_rot, allowed)
    top_score = jnp.max(scores, -1, keepdims=True)
    exp_scores = jnp.exp(scores - top_score)
    row_total = jnp.sum(exp_scores, -1, keepdims=True)
    prob_low = (exp_scores / row_total).astype(jnp.bfloat16)
    log_total = top_score + jnp.log(row_total)
    mixed = jnp.einsum("hgqk,khd->qhgd", prob_low, value_rows, preferred_element_type=jnp.float32)
    mixed = mixed.astype(jnp.bfloat16).reshape(row_count, query_heads * HEAD_DIM)
    resid_mid = resid_in + apply_rows(mixed, w_output)
    normed_two, inverse_two, hidden_two = general_norm_forward(resid_mid, mlp_gain)
    gate_rows = project(hidden_two, w_gate)
    up_rows = project(hidden_two, w_up)
    inner = (jax.nn.silu(gate_rows) * up_rows).astype(jnp.bfloat16)
    block_out = (resid_mid + apply_rows(inner, w_down)).astype(jnp.bfloat16)
    saved = (
        allowed,
        cosine,
        sine_table,
        normed_one,
        inverse_one,
        hidden_one,
        value_rows,
        query_rot,
        key_rot,
        log_total,
        mixed,
        normed_two,
        inverse_two,
        hidden_two,
        gate_rows,
        up_rows,
        inner,
    )
    return (block_out, saved)


def backward_pass(grad_rows, saved, gathered):
    attn_gain, w_query, w_key, w_value, w_output, mlp_gain, w_gate, w_up, w_down = gathered
    (
        allowed,
        cosine,
        sine_table,
        normed_one,
        inverse_one,
        hidden_one,
        value_rows,
        query_rot,
        key_rot,
        log_total,
        mixed,
        normed_two,
        inverse_two,
        hidden_two,
        gate_rows,
        up_rows,
        inner,
    ) = saved
    row_count = grad_rows.shape[0]
    grad_out = grad_rows.astype(jnp.float32)
    grad_inner = project(grad_rows, w_down)
    sigmoid_gate = jax.nn.sigmoid(gate_rows)
    silu_gate = gate_rows * sigmoid_gate
    grad_gate = (
        grad_inner * up_rows * sigmoid_gate * (1.0 + gate_rows * (1.0 - sigmoid_gate))
    ).astype(jnp.bfloat16)
    grad_up = (grad_inner * silu_gate).astype(jnp.bfloat16)
    grad_hidden_two = apply_rows(grad_gate, w_gate) + apply_rows(grad_up, w_up)
    grad_mid = grad_out + general_norm_backward(grad_hidden_two, normed_two, inverse_two, mlp_gain)
    grad_branch = grad_mid.astype(jnp.bfloat16)
    grad_mixed = project(grad_branch, w_output).astype(jnp.bfloat16).reshape(query_rot.shape)
    scores = attention_scores(query_rot, key_rot, allowed)
    attn_probs = jnp.exp(scores - log_total)
    prob_low = attn_probs.astype(jnp.bfloat16)
    grad_probs = jnp.einsum(
        "qhgd,khd->hgqk", grad_mixed, value_rows, preferred_element_type=jnp.float32
    )
    grad_scores = attn_probs * (grad_probs - jnp.sum(grad_probs * attn_probs, -1, keepdims=True))
    grad_scores = grad_scores.astype(jnp.bfloat16)
    grad_value = jnp.einsum(
        "hgqk,qhgd->khd", prob_low, grad_mixed, preferred_element_type=jnp.float32
    )
    grad_value = grad_value.astype(jnp.bfloat16).reshape(row_count, -1)
    score_scale = HEAD_DIM ** (-0.5)
    grad_qrot = (
        jnp.einsum("hgqk,khd->qhgd", grad_scores, key_rot, preferred_element_type=jnp.float32)
        * score_scale
    )
    grad_krot = (
        jnp.einsum("hgqk,qhgd->khd", grad_scores, query_rot, preferred_element_type=jnp.float32)
        * score_scale
    )
    grad_query = rotate_back(grad_qrot.reshape(row_count, -1, HEAD_DIM), cosine, sine_table)
    grad_query = grad_query.astype(jnp.bfloat16).reshape(row_count, -1)
    grad_key = (
        rotate_back(grad_krot, cosine, sine_table).astype(jnp.bfloat16).reshape(row_count, -1)
    )
    grad_hidden_one = (
        apply_rows(grad_query, w_query)
        + apply_rows(grad_key, w_key)
        + apply_rows(grad_value, w_value)
    )
    grad_input = (
        grad_mid + general_norm_backward(grad_hidden_one, normed_one, inverse_one, attn_gain)
    ).astype(jnp.bfloat16)
    gain_terms = jnp.stack(
        [jnp.sum(grad_hidden_one * normed_one, 0), jnp.sum(grad_hidden_two * normed_two, 0)]
    )
    stored = (
        grad_query,
        hidden_one,
        grad_key,
        grad_value,
        mixed,
        grad_branch,
        grad_gate,
        hidden_two,
        grad_up,
        inner,
        grad_rows,
    )
    return (grad_input, stored, gain_terms)


def slice_term(left_rows, right_rows, owner, width):
    piece = lax.dynamic_slice_in_dim(left_rows, owner * width, width, 1)
    return lax.dot_general(
        piece, right_rows, (((0,), (0,)), ((), ())), preferred_element_type=jnp.float32
    )


def on_device_general(
    block_input,
    out_grad,
    seq_lengths,
    attn_gain,
    w_query,
    w_key,
    w_value,
    w_output,
    mlp_gain,
    w_gate,
    w_up,
    w_down,
):
    block_outs = []
    grad_inputs = []
    collected = [[] for member in range(11)]
    gain_total = jnp.zeros((2, block_input.shape[2]), jnp.float32)
    for batch_index in range(block_input.shape[0]):
        forward_layer = (
            lax.all_gather(attn_gain, DEVICES, axis=0, tiled=True),
            lax.all_gather(w_query, DEVICES, axis=0, tiled=True),
            lax.all_gather(w_key, DEVICES, axis=0, tiled=True),
            lax.all_gather(w_value, DEVICES, axis=0, tiled=True),
            lax.all_gather(w_output, DEVICES, axis=0, tiled=True),
            lax.all_gather(mlp_gain, DEVICES, axis=0, tiled=True),
            lax.all_gather(w_gate, DEVICES, axis=0, tiled=True),
            lax.all_gather(w_up, DEVICES, axis=0, tiled=True),
            lax.all_gather(w_down, DEVICES, axis=0, tiled=True),
        )
        block_out, saved = forward_pass(
            block_input[batch_index], seq_lengths[batch_index, 0], forward_layer
        )
        backward_layer = (
            lax.all_gather(attn_gain, DEVICES, axis=0, tiled=True),
            lax.all_gather(w_query, DEVICES, axis=0, tiled=True),
            lax.all_gather(w_key, DEVICES, axis=0, tiled=True),
            lax.all_gather(w_value, DEVICES, axis=0, tiled=True),
            lax.all_gather(w_output, DEVICES, axis=0, tiled=True),
            lax.all_gather(mlp_gain, DEVICES, axis=0, tiled=True),
            lax.all_gather(w_gate, DEVICES, axis=0, tiled=True),
            lax.all_gather(w_up, DEVICES, axis=0, tiled=True),
            lax.all_gather(w_down, DEVICES, axis=0, tiled=True),
        )
        grad_input, stored, gain_terms = backward_pass(out_grad[batch_index], saved, backward_layer)
        block_outs.append(block_out)
        grad_inputs.append(grad_input)
        gain_total = gain_total + gain_terms
        for member in range(11):
            collected[member].append(stored[member])
    joined = [jnp.concatenate(member_list, 0) for member_list in collected]
    model_width = block_input.shape[2]
    query_width = w_query.shape[0]
    key_width = w_key.shape[0]
    hidden_width = w_gate.shape[0]
    gain_width = attn_gain.shape[0]
    own_rows = 2 * query_width + 2 * key_width + 3 * hidden_width + 1
    filler = jnp.zeros((model_width - 2 * gain_width,), jnp.float32)

    def owner_block(owner):
        gain_row = jnp.concatenate(
            [
                lax.dynamic_slice_in_dim(gain_total[0], owner * gain_width, gain_width, 0),
                lax.dynamic_slice_in_dim(gain_total[1], owner * gain_width, gain_width, 0),
                filler,
            ],
            0,
        )
        return jnp.concatenate(
            [
                slice_term(joined[0], joined[1], owner, query_width),
                slice_term(joined[2], joined[1], owner, key_width),
                slice_term(joined[3], joined[1], owner, key_width),
                slice_term(joined[4], joined[5], owner, query_width),
                slice_term(joined[6], joined[7], owner, hidden_width),
                slice_term(joined[8], joined[7], owner, hidden_width),
                slice_term(joined[9], joined[10], owner, hidden_width),
                gain_row[None, :],
            ],
            0,
        )

    owner_count = own_rows * lax.axis_size(DEVICES) // own_rows
    owners = jnp.arange(owner_count, dtype=jnp.int32)
    blocks = lax.map(owner_block, owners)
    owned = lax.psum_scatter(
        blocks.reshape(owner_count * own_rows, model_width),
        DEVICES,
        scatter_dimension=0,
        tiled=True,
    )
    cuts = [
        query_width,
        key_width,
        key_width,
        query_width,
        hidden_width,
        hidden_width,
        hidden_width,
    ]
    pieces = []
    offset = 0
    for width in cuts:
        pieces.append(owned[offset : offset + width])
        offset = offset + width
    gain_row = owned[offset]
    return (
        jnp.stack(block_outs),
        jnp.stack(grad_inputs),
        gain_row[:gain_width],
        pieces[0],
        pieces[1],
        pieces[2],
        pieces[3],
        gain_row[gain_width : 2 * gain_width],
        pieces[4],
        pieces[5],
        pieces[6],
    )


def solution(mesh):
    groups, sub = mesh.shape["dp"], mesh.shape["sub"]
    rows, weight, gain = P(None, DEVICES, None), P(DEVICES, None), P(DEVICES)
    body = on_device_general
    if groups == 16 and sub == 2:
        mesh = Mesh(mesh.devices.reshape(2, 2, groups // 8, 2, sub), AXES)
        rows, weight, gain = P(None, AXES, None), P(AXES, None), P(AXES)
        body = on_device_small
    return jax.shard_map(
        body,
        mesh=mesh,
        in_specs=(rows, rows, rows, gain) + (weight,) * 4 + (gain,) + (weight,) * 3,
        out_specs=(rows, rows, gain) + (weight,) * 4 + (gain,) + (weight,) * 3,
        check_vma=False,
    )
```
